32 devices in a mesh: dp: 8 (over z, x), seq: 4 (over y, core).
Axes of the slice: x: 2, y: 2, z: 4, core: 2. Of those that a mesh axis runs over, the one named last changes fastest.
Arguments:
- tokens: bfloat16 [16, 1024, 512], P('dp', 'seq'), may hold values from -6 to 6
- memory: bfloat16 [16, 1024, 512], P('dp', 'seq'), may hold values from -6 to 6
- segment_ids: int32 [16, 1024], P('dp', 'seq'), may hold values from 0 to 7, never falling along the last dimension, each value on 1 to 768 neighbouring positions
- source_ids: int32 [16, 1024], P('dp', 'seq'), may hold values from 0 to 7, as said below
- source_lengths: int32 [16], P('dp'), may hold values from 512 to 1024, as said below
- cotangent: bfloat16 [16, 1024, 512], P('dp', 'seq'), may hold values from -6 to 6
- self_qkv: bfloat16 [512, 1536], replicated, may hold values from -0.25 to 0.25
- self_out: bfloat16 [512, 512], replicated, may hold values from -0.75 to 0.75
- cross_q: bfloat16 [512, 512], replicated, may hold values from -0.25 to 0.25
- cross_kv: bfloat16 [512, 1024], replicated, may hold values from -0.25 to 0.25
- cross_out: bfloat16 [512, 512], replicated, may hold values from -0.75 to 0.75
- ffn_in: bfloat16 [512, 2048], replicated, may hold values from -0.25 to 0.25
- ffn_out: bfloat16 [2048, 512], replicated, may hold values from -0.125 to 0.125
- norm_gains: float32 [3, 512], replicated, may hold values from 0.5 to 1.5
- bias_rows: float32 [10, 512], replicated, may hold values from -1.5 to 1.5
- hidden_bias: float32 [2048], replicated, may hold values from -1.5 to 1.5
Outputs:
- output: bfloat16 [16, 1024, 512], P('dp', 'seq')
- grad_tokens: bfloat16 [16, 1024, 512], P('dp', 'seq')
- grad_memory: bfloat16 [16, 1024, 512], P('dp', 'seq')
- grad_self_qkv: float32 [512, 1536], replicated
- grad_self_out: float32 [512, 512], replicated
- grad_cross_q: float32 [512, 512], replicated
- grad_cross_kv: float32 [512, 1024], replicated
- grad_cross_out: float32 [512, 512], replicated
- grad_ffn_in: float32 [512, 2048], replicated
- grad_ffn_out: float32 [2048, 512], replicated
- grad_norm_gains: float32 [3, 512], replicated
- grad_bias_rows: float32 [10, 512], replicated
- grad_hidden_bias: float32 [2048], replicated
The draws below stay inside these ranges and needn't reach their ends.
Inputs may be any that keep to these rules, and one draw needn't show every extreme that they name: `segment_ids`: Non-decreasing along each row; every number 0 to 7 occurs in every row. `source_ids`: in each row, positions below the row's source length hold every number 0 to 7 in non-decreasing order, each on at least two positions; later positions hold 7. `source_lengths`: at least one row has length 1024.
All inputs are finite; a program needn't handle non-finite values.
Results may differ from the reference program's by a relative error of at most 0.02.
Values may be sent and summed in bfloat16 or wider, within the bound.
A program may use at most 192 MiB of HBM per device.

```python
import math
import jax
import jax.numpy as jnp
import numpy as np
from jax import lax

D = 512
HEADS = 8
FF = 2048
LEN = 1024
SRC = 1024
SEGS = 8
ROWS_DEV = 2
ROWS = 16


def source_layout(key):
    length_key = jax.random.fold_in(key, 101)
    full_key = jax.random.fold_in(key, 102)
    border_key = jax.random.fold_in(key, 103)
    lengths = jax.random.randint(length_key, (ROWS,), SRC // 2, SRC + 1)
    full_row = jax.random.randint(full_key, (), 0, ROWS)
    lengths = jnp.where(jnp.arange(ROWS) == full_row, SRC, lengths).astype(jnp.int32)
    spacing = lengths // SEGS
    spread_cells = spacing // 4
    offsets = jax.random.randint(border_key, (ROWS, SEGS - 1), 0, 1 << 20) % (2 * spread_cells[:, None] + 1) - spread_cells[:, None]
    borders = jnp.arange(1, SEGS)[None, :] * lengths[:, None] // SEGS + offsets
    places = jnp.arange(SRC)
    segment_of = jnp.sum((places[None, :, None] >= borders[:, None, :]).astype(jnp.int32), axis=-1)
    return (segment_of.astype(jnp.int32), lengths)


def draw_source_ids(key, part):
    return source_layout(key)[0]


def draw_source_lengths(key, part):
    return source_layout(key)[1]


def raised(array, own_key, source, target, blocks, factor):
    def block_of(dim):
        return (jnp.arange(array.shape[dim]) // (array.shape[dim] // blocks)).reshape((-1,) + (1,) * (array.ndim - 1 - dim))

    one_side = jax.random.permutation(own_key, blocks)[block_of(target)]
    far = (block_of(target) + blocks // 2) % blocks
    return jnp.where((block_of(source) == one_side) | (block_of(source) == far), factor * array, array)


def shard_levels(own_key, dims, pieces, low, top_value):
    def one(axis_at, shards_of):
        heights = jax.random.uniform(jax.random.fold_in(jax.random.fold_in(own_key, 6), axis_at), (shards_of,), jnp.float32, low / len(pieces), top_value / len(pieces))
        return jnp.repeat(jnp.exp(heights), dims[axis_at] // shards_of).reshape((-1,) + (1,) * (len(dims) - axis_at - 1))

    level = one(*pieces[0])
    for cut in pieces[1:]:
        level = level * one(*cut)
    return level


def split_up(number_of, total, bound, lean):
    weights = [(1 << 20) // math.isqrt(grade ** lean) + 1 for grade in range(2, number_of + 1)]
    spare, given = total - bound - (number_of - 1), [1] * (number_of - 1)
    while spare > 0:
        movable = [i for i in range(number_of - 1) if given[i] < bound]
        pool, remaining = sum([weights[i] for i in movable]), spare
        for i in movable:
            addition = min(bound - given[i], max(1, remaining * weights[i] // pool), spare)
            given[i] = given[i] + addition
            spare = spare - addition
    return np.array([bound] + given)


def uneven(rng, amount, total, most, lean):
    if amount == 2:
        one = jax.random.randint(rng, (), max(1, total - most), min(most, total - 1) + 1)
        return jnp.stack([one, total - one])
    tallies = jnp.asarray(split_up(amount, total, most, lean), jnp.int32)
    pairs = (amount - 1) // 2
    giver, taker = tallies[1:1 + 2 * pairs:2], tallies[2:2 + 2 * pairs:2]
    margin = jnp.minimum(giver - 1, most - taker)
    moved = jax.random.randint(jax.random.fold_in(rng, 1), (pairs,), 0, 1 << 20) % (margin + 1)
    tallies = tallies.at[1:1 + 2 * pairs:2].set(giver - moved).at[2:2 + 2 * pairs:2].set(taker + moved)
    return tallies[jax.random.permutation(jax.random.fold_in(rng, 2), amount)]


def noise(stream_key, extent, spread, most, split=(), kind=jnp.bfloat16):
    level = shard_levels(stream_key, extent, split, -0.22, 0.18) if split else 1.0
    values = jax.random.normal(stream_key, extent, jnp.float32) * spread * level
    return jnp.minimum(jnp.maximum(values, -most), most).astype(kind)


def bell_draw_with(own_key, dims, width, most, shards, heavy, kind=jnp.bfloat16):
    values = width * jax.random.normal(own_key, dims, jnp.float32)
    if shards:
        values = values * shard_levels(own_key, dims, shards, -0.22, 0.18)
    return jnp.clip(raised(values, jax.random.fold_in(own_key, 3), *heavy), -most, most).astype(kind)


def setup_inputs(seed: int = 0) -> dict:
    arg_keys = jax.random.split(jax.random.key(seed), 17)
    return {
        "tokens": noise(arg_keys[0], (ROWS, LEN, D), 1.0, 6.0, ((0, 8), (1, 4))),
        "memory": noise(arg_keys[1], (ROWS, SRC, D), 1.0, 6.0, ((0, 8), (1, 4))),
        "segment_ids": jax.vmap(lambda own: jnp.searchsorted(jnp.cumsum(uneven(own, SEGS, LEN, LEN * 3 // 4, 1)), jnp.arange(LEN), side="right"))(jax.random.split(arg_keys[2], ROWS)).reshape((ROWS, LEN)).astype(jnp.int32),
        "source_ids": draw_source_ids(jax.random.fold_in(arg_keys[16], 71), 0),
        "source_lengths": draw_source_lengths(jax.random.fold_in(arg_keys[16], 71), 0),
        "cotangent": bell_draw_with(arg_keys[5], (ROWS, LEN, D), 1.0, 6.0, ((0, 8), (1, 4)), (0, 2, 8, 2.0)),
        "self_qkv": noise(arg_keys[6], (D, 3 * D), D ** -0.5, 0.25),
        "self_out": noise(arg_keys[7], (D, D), (D // 8) ** -0.5, 0.75),
        "cross_q": noise(arg_keys[8], (D, D), D ** -0.5, 0.25),
        "cross_kv": noise(arg_keys[9], (D, 2 * D), D ** -0.5, 0.25),
        "cross_out": noise(arg_keys[10], (D, D), (D // 8) ** -0.5, 0.75),
        "ffn_in": noise(arg_keys[11], (D, FF), D ** -0.5, 0.25),
        "ffn_out": noise(arg_keys[12], (FF, D), FF ** -0.5, 0.125),
        "norm_gains": jnp.clip(1.0 + 0.1 * jax.random.normal(arg_keys[13], (3, D), jnp.float32), 0.5, 1.5),
        "bias_rows": noise(arg_keys[14], (10, D), 0.3, 1.5, (), jnp.float32),
        "hidden_bias": noise(arg_keys[15], (FF,), 0.3, 1.5, (), jnp.float32),
    }


HIGHEST_PRECISION = lax.Precision.HIGHEST
SCORE_SCALE = 0.125
EPSILON = 1e-05
MASKED = -1000000000.0

@jax.custom_vjp
def low(v):
    return lax.optimization_barrier(v.astype(jnp.bfloat16)).astype(jnp.float32)

@jax.custom_vjp
def low_back(v):
    return v

def low_keep(v):
    return (low(v), None)

def low_pass(kept, grad):
    return (grad,)

def back_keep(v):
    return (v, None)

def back_low(kept, grad):
    return (low(grad),)
low.defvjp(low_keep, low_pass)
low_back.defvjp(back_keep, back_low)

def rounded(values):
    return low_back(low(values))

def linear(values, weight):
    return jnp.einsum('rtd,de->rte', values, weight, precision=HIGHEST_PRECISION)

def split_heads(values):
    return values.reshape(values.shape[0], values.shape[1], HEADS, values.shape[2] // HEADS)

def attention(queries, key_rows, value_rows, allowed):
    raw_scores = jnp.einsum('rqhd,rkhd->rhqk', split_heads(queries), split_heads(key_rows), precision=HIGHEST_PRECISION) * SCORE_SCALE
    scores = jnp.where(allowed, low_back(raw_scores), MASKED)
    row_peak = lax.optimization_barrier(jnp.max(scores, axis=-1, keepdims=True))
    exponent = jnp.exp(scores - row_peak)
    weights = low(exponent / lax.optimization_barrier(jnp.sum(exponent, axis=-1, keepdims=True)))
    mixed = jnp.einsum('rhqk,rkhd->rqhd', weights, split_heads(value_rows), precision=HIGHEST_PRECISION)
    return mixed.reshape(queries.shape)

def normalize(residual, gain, shift):
    centred = residual - lax.optimization_barrier(jnp.mean(residual, axis=-1, keepdims=True))
    inverse_root = lax.rsqrt(lax.optimization_barrier(jnp.mean(centred * centred, axis=-1, keepdims=True)) + EPSILON)
    return centred * inverse_root * gain + shift

def decoder_layer(weights, row_group):
    self_qkv, self_out, cross_q, cross_kv, cross_out, ffn_in, ffn_out, norm_gains, bias_rows, hidden_bias = weights
    tokens, memory, row_segments, row_sources, row_lengths = row_group
    model_width = tokens.shape[2]
    positions = jnp.arange(tokens.shape[1], dtype=jnp.int32)
    source_pos = jnp.arange(memory.shape[1], dtype=jnp.int32)
    self_allowed = ((row_segments[:, :, None] == row_segments[:, None, :]) & (positions[:, None] >= positions[None, :])[None])[:, None]
    cross_allowed = ((row_segments[:, :, None] == row_sources[:, None, :]) & (source_pos[None, None, :] < row_lengths[:, None, None]))[:, None]
    projected = linear(tokens, self_qkv)
    queries = rounded(projected[:, :, :model_width] + bias_rows[3])
    key_rows = rounded(projected[:, :, model_width:2 * model_width])
    value_rows = rounded(projected[:, :, 2 * model_width:] + bias_rows[4])
    attended = rounded(attention(queries, key_rows, value_rows, self_allowed))
    residual = tokens + low_back(linear(attended, self_out) + bias_rows[5])
    after_self = normalize(residual, norm_gains[0], bias_rows[0])
    cross_query = rounded(linear(low(after_self), cross_q) + bias_rows[6])
    key_value = linear(memory, cross_kv)
    cross_key = low(key_value[:, :, :model_width])
    cross_value = low(key_value[:, :, model_width:] + bias_rows[7])
    crossed = rounded(attention(cross_query, cross_key, cross_value, cross_allowed))
    after_cross = normalize(after_self + low_back(linear(crossed, cross_out) + bias_rows[8]), norm_gains[1], bias_rows[1])
    before = low_back(linear(low(after_cross), ffn_in) + hidden_bias)
    hidden = low(jax.nn.gelu(before, approximate=False))
    return normalize(after_cross + low_back(linear(hidden, ffn_out) + bias_rows[9]), norm_gains[2], bias_rows[2])

def reference(tokens, memory, segment_ids, source_ids, source_lengths, cotangent, self_qkv, self_out, cross_q, cross_kv, cross_out, ffn_in, ffn_out, norm_gains, bias_rows, hidden_bias):
    floats = tuple((a.astype(jnp.float32) for a in (self_qkv, self_out, cross_q, cross_kv, cross_out, ffn_in, ffn_out, norm_gains, bias_rows, hidden_bias)))
    groups = tokens.shape[0] // ROWS_DEV

    def grouped(values):
        return values.reshape((groups, ROWS_DEV) + values.shape[1:])
    checkpointed = jax.checkpoint(decoder_layer)

    def forward(weights, tokens_float, memory_float):

        def scan_body(carried, row_group):
            return (carried, checkpointed(weights, row_group))
        _, results = lax.scan(scan_body, jnp.zeros((), jnp.float32), (grouped(tokens_float), grouped(memory_float), grouped(segment_ids), grouped(source_ids), grouped(source_lengths)))
        return results.reshape(tokens_float.shape)
    output, pullback = jax.vjp(forward, floats, tokens.astype(jnp.float32), memory.astype(jnp.float32))
    grad_weights, grad_tokens, grad_memory = pullback(cotangent.astype(jnp.float32))
    return (output.astype(jnp.bfloat16), grad_tokens.astype(jnp.bfloat16), grad_memory.astype(jnp.bfloat16), grad_weights[0], grad_weights[1], grad_weights[2], grad_weights[3], grad_weights[4], grad_weights[5], grad_weights[6], grad_weights[7], grad_weights[8], grad_weights[9])
```

```python
import functools

import jax
import jax.numpy as jnp
from jax import lax
from jax.experimental import pallas as pl
from jax.experimental.pallas import tpu as pltpu
from jax.sharding import PartitionSpec as P

HEADS = 8
SCORE_SCALE = 0.125
EPSILON = 1e-05
ROOT_HALF = 0.7071067811865476
NORMAL_DENSITY = 0.3989422804014327

BIG=float(2.0**30)
HALF=64
LSE=8; DELTA=32
NT=(((1,),(1,)),((),()))
F32=jnp.float32; BF=jnp.bfloat16
def lanes(shape): return lax.broadcasted_iota(jnp.int32,shape,len(shape)-1)
def pick(even, mine, aux):
    low=lanes(mine.shape)<HALF
    return jnp.where(low,mine,aux) if even else jnp.where(low,aux,mine)
def dot_nt(a,b): return lax.dot_general(a,b,NT,preferred_element_type=F32)
def dot_nn(a,b): return jnp.dot(a,b,preferred_element_type=F32)
def put_parts(aux,x,at):
    lane=lanes(aux.shape)%HALF
    hi=x.astype(BF).astype(F32); r=x-hi; mid=r.astype(BF).astype(F32)
    return jnp.where(lane==at,hi,jnp.where(lane==at+1,mid,jnp.where(lane==at+2,r-mid,aux)))
def row_const(shape,at,n,val):
    lane=lanes(shape)%HALF
    return (lane>=at)&(lane<at+n)
def schedule(n,ahead,first,rest):
    kept={}
    for h in range(min(ahead,n)): kept[h]=first(h)
    for h in range(n):
        if h+ahead<n: kept[h+ahead]=first(h+ahead)
        rest(h,kept.pop(h))

def fwd_kernel(tq,width,causal,ahead,start_ref,count_ref,base_ref,q_ref,aq_ref,k_ref,v_ref,ak_ref,o_ref,l_ref):
    rows=q_ref.shape[0]; subs=q_ref.shape[1]//tq; keys=k_ref.shape[1]; heads=q_ref.shape[2]//HALF
    def step(i,_):
        r=i//subs; s=i%subs
        n=count_ref[r,s]; st=pl.multiple_of(start_ref[r,s],128)
        qs=pl.ds(pl.multiple_of(s*tq,tq),tq)
        for blocks in range(1,keys//width+1):
            @pl.when(n==blocks)
            def _(blocks=blocks):
                span=blocks*width
                ks=pl.ds(st,span)
                ak=ak_ref[r,ks]; aq=aq_ref[r,qs]
                state={"stats":aq.astype(F32)}
                if causal:
                    qp=base_ref[0]+s*tq+lax.broadcasted_iota(jnp.int32,(tq,width),0)
                    kp=st+span-width+lax.broadcasted_iota(jnp.int32,(tq,width),1)
                    seen=kp<=qp
                def first(h):
                    cs=slice(h//2*128,h//2*128+128)
                    q=q_ref[r,qs,cs]*jnp.asarray(0.125,BF); k=k_ref[r,ks,cs]
                    return dot_nt(pick(h%2==0,q,aq),pick(h%2==0,k,ak))
                def rest(h,S):
                    cs=slice(h//2*128,h//2*128+128)
                    v=v_ref[r,ks,cs]
                    if causal:
                        tail=jnp.where(seen,S[:,span-width:],-BIG)
                        S=tail if blocks==1 else jnp.concatenate([S[:,:span-width],tail],axis=1)
                    m=jnp.max(S,axis=1,keepdims=True)
                    W=jnp.exp(S-m).astype(BF)
                    R=dot_nn(W,pick(h%2==0,v,jnp.ones_like(v)))
                    at=64 if h%2==0 else 0
                    state["stats"]=put_parts(state["stats"],m+jnp.log(R[:,at:at+1]),LSE+3*h)
                    if h%2==0: state["even"]=R
                    else:
                        low=lanes((tq,128))<HALF
                        total=pltpu.roll(jnp.where(low,R,state["even"]),HALF,1)
                        o_ref[r,qs,cs]=(jnp.where(low,state["even"],R)/total).astype(o_ref.dtype)
                schedule(heads,ahead,first,rest)
                l_ref[r,qs]=state["stats"].astype(BF)
        return 0
    lax.fori_loop(0,rows*subs,step,0)

def bwd_kernel(dkv,tq,width,causal,ahead,start_ref,count_ref,base_ref,a_ref,b_ref,aq_ref,ak_ref,k_ref,v_ref,*outs):
    loc=k_ref if dkv else a_ref
    win=a_ref if dkv else k_ref
    rows=loc.shape[0]; subs=loc.shape[1]//tq; keys=win.shape[1]; heads=loc.shape[2]//HALF
    def step(i,_):
        r=i//subs; s=i%subs
        n=count_ref[r,s]; st=pl.multiple_of(start_ref[r,s],128)
        ls=pl.ds(pl.multiple_of(s*tq,tq),tq)
        if dkv:
            @pl.when(n==0)
            def _():
                for out in outs: out[r,ls]=jnp.zeros((tq,out.shape[2]),out.dtype)
        for blocks in range(1,keys//width+1):
            @pl.when(n==blocks)
            def _(blocks=blocks):
                span=blocks*width
                ws=pl.ds(st,span)
                qs,ks=(ws,ls) if dkv else (ls,ws)
                ak=ak_ref[r,ks]; aq=aq_ref[r,qs]
                state={}
                if causal:
                    at=base_ref[0]+s*tq
                    if dkv:
                        seen=at+lax.broadcasted_iota(jnp.int32,(tq,width),0)<=st+lax.broadcasted_iota(jnp.int32,(tq,width),1)
                    else:
                        seen=st+span-width+lax.broadcasted_iota(jnp.int32,(tq,width),1)<=at+lax.broadcasted_iota(jnp.int32,(tq,width),0)
                minus=jnp.asarray(-1.0,BF)
                def first(h):
                    e=h%2==0
                    cs=slice(h//2*128,h//2*128+128)
                    q=a_ref[r,qs,cs]*jnp.asarray(0.125,BF); g=b_ref[r,qs,cs]; k=k_ref[r,ks,cs]; v=v_ref[r,ks,cs]
                    ka=pick(e,k,jnp.where(row_const(ak.shape,LSE+3*h,3,-1),minus,ak))
                    va=pick(e,v,jnp.where(row_const(v.shape,DELTA+3*h,3,-1),minus,jnp.zeros_like(v)))
                    qa=pick(e,q,aq); ga=pick(e,g,aq)
                    if dkv: return dot_nt(ka,qa),dot_nt(va,ga)
                    return dot_nt(qa,ka),dot_nt(ga,va)
                def rest(h,XG):
                    X,G=XG
                    cs=slice(h//2*128,h//2*128+128)
                    if causal:
                        if dkv:
                            X1=jnp.where(seen,X[:,:width],-BIG)
                            X=X1 if blocks==1 else jnp.concatenate([X1,X[:,width:]],axis=1)
                        else:
                            X1=jnp.where(seen,X[:,span-width:],-BIG)
                            X=X1 if blocks==1 else jnp.concatenate([X[:,:span-width],X1],axis=1)
                    W=jnp.exp(X); D=(W*G).astype(BF)
                    low=lanes((tq,128))<HALF
                    if not dkv:
                        R=dot_nn(D,k_ref[r,ks,cs])
                        if h%2==0: state["a"]=R
                        else: outs[0][r,ls,cs]=(0.125*jnp.where(low,state["a"],R)).astype(outs[0].dtype)
                    else:
                        R2=dot_nn(W.astype(BF),b_ref[r,qs,cs])
                        R=dot_nn(D,a_ref[r,qs,cs])
                        if h%2==0: state["a"]=R; state["b"]=R2
                        else:
                            outs[0][r,ls,cs]=(0.125*jnp.where(low,state["a"],R)).astype(outs[0].dtype)
                            outs[1][r,ls,cs]=jnp.where(low,state["b"],R2).astype(outs[1].dtype)
                schedule(heads,ahead,first,rest)
        return 0
    lax.fori_loop(0,rows*subs,step,0)
SM=pl.BlockSpec(memory_space=pltpu.SMEM); VM=pl.BlockSpec(memory_space=pltpu.VMEM)
def fwd(tq,width,causal,ahead,start,count,base,q,aq,k,v,ak):
    R,T,D=q.shape
    return pl.pallas_call(functools.partial(fwd_kernel,tq,width,causal,ahead),
        out_shape=(jax.ShapeDtypeStruct(q.shape,BF),jax.ShapeDtypeStruct((R,T,128),BF)),
        in_specs=[SM]*3+[VM]*5,out_specs=(VM,VM),name="attend_rows",
        compiler_params=pltpu.CompilerParams(vmem_limit_bytes=48<<20))(start,count,base,q,aq,k,v,ak)
def bwd_dq(tq,width,causal,ahead,start,count,base,q,g,aq,ak,k,v):
    return pl.pallas_call(functools.partial(bwd_kernel,False,tq,width,causal,ahead),
        out_shape=(jax.ShapeDtypeStruct(q.shape,BF),),
        in_specs=[SM]*3+[VM]*6,out_specs=(VM,),name="query_grad",
        compiler_params=pltpu.CompilerParams(vmem_limit_bytes=48<<20))(start,count,base,q,g,aq,ak,k,v)[0]
def bwd_dkv(tq,width,causal,ahead,start,count,base,q,g,aq,ak,k,v):
    return pl.pallas_call(functools.partial(bwd_kernel,True,tq,width,causal,ahead),
        out_shape=(jax.ShapeDtypeStruct(k.shape,BF),)*2,
        in_specs=[SM]*3+[VM]*6,out_specs=(VM,VM),name="key_grad",
        compiler_params=pltpu.CompilerParams(vmem_limit_bytes=48<<20))(start,count,base,q,g,aq,ak,k,v)
def aux_q(seg):
    lane=jnp.arange(128)%HALF
    return jnp.where((lane<8)&(seg[...,None]==lane),1.0,0.0).astype(BF)
def aux_k(seg,valid=None):
    lane=jnp.arange(128)%HALF
    ok=seg[...,None]==lane
    if valid is not None: ok=ok&valid[...,None]
    return jnp.where((lane<8)&~ok,-BIG,0.0).astype(BF)

def gather_row(block, axis=1):
    size = lax.axis_size("seq")
    place = lax.axis_index("seq")
    held = {0: block}
    bit = size // 2
    while bit:
        swap = [(i, i ^ bit) for i in range(size)]
        for key in list(held):
            held[key | bit] = lax.ppermute(held[key], "seq", swap)
        bit //= 2
    shape = list(block.shape)
    extent = shape[axis]
    shape[axis] = extent * size
    full = jnp.zeros(shape, block.dtype)
    for key, value in held.items():
        at = [0] * len(shape)
        at[axis] = (place ^ key) * extent
        full = lax.dynamic_update_slice(full, value, at)
    return full


def count_below(ids, bound):
    return jnp.sum((ids[:, None, :] < bound[:, :, None]).astype(jnp.int32), axis=-1)


def window(low, high, width, extent):
    floor = low // 128 * 128
    blocks = jnp.where(high > low, (high - floor + width - 1) // width, 0)
    start = jnp.minimum(floor, extent - blocks * width)
    return start.astype(jnp.int32), blocks.astype(jnp.int32)


def with_inner(aux, grad_mixed, mixed):
    width = mixed.shape[-1]
    lane = jnp.arange(128) % HALF
    head = (lane - DELTA) // 3
    chosen = (
        (jnp.arange(width)[:, None] // HALF == head[None]) & (lane >= DELTA) & (lane < DELTA + 3 * HEADS)
    ).astype(F32)
    inner = jnp.einsum(
        "rtd,dl->rtl",
        grad_mixed.astype(F32) * mixed.astype(F32),
        chosen,
        precision=lax.Precision.HIGHEST,
        preferred_element_type=F32,
    )
    high = lax.reduce_precision(inner, 8, 7)
    rest = inner - high
    middle = lax.reduce_precision(rest, 8, 7)
    part = (lane - DELTA) % 3
    return (
        aux.astype(F32) + jnp.where(part == 0, high, jnp.where(part == 1, middle, rest - middle))
    ).astype(BF)

def project(values, weight):
    return jnp.einsum("rtd,de->rte", values, weight, preferred_element_type=jnp.float32)


def weight_grad(left, right):
    return jnp.einsum("rtd,rte->de", left, right, preferred_element_type=jnp.float32)


def input_grad(grad, weight):
    return jnp.einsum("rte,de->rtd", grad, weight, preferred_element_type=jnp.float32)


def token_sum(values):
    return jnp.sum(values.astype(jnp.float32), axis=(0, 1))


def gelu_slope(values):
    return 0.5 * (1.0 + lax.erf(values * ROOT_HALF)) + values * NORMAL_DENSITY * jnp.exp(
        -0.5 * values * values
    )


def normalize(residual, gain, shift):
    centred = residual - jnp.mean(residual, axis=-1, keepdims=True)
    inverse_root = lax.rsqrt(jnp.mean(centred * centred, axis=-1, keepdims=True) + EPSILON)
    unit_rows = centred * inverse_root
    return (unit_rows * gain + shift, unit_rows, inverse_root)


def normalize_back(grad, unit_rows, inverse_root, gain):
    scaled = grad * gain
    grad_residual = inverse_root * (
        scaled
        - jnp.mean(scaled, axis=-1, keepdims=True)
        - unit_rows * jnp.mean(scaled * unit_rows, axis=-1, keepdims=True)
    )
    return (grad_residual, jnp.sum(grad * unit_rows, axis=(0, 1)), jnp.sum(grad, axis=(0, 1)))


def shards(
    tokens,
    memory,
    segment_ids,
    source_ids,
    source_lengths,
    cotangent,
    self_qkv,
    self_out,
    cross_q,
    cross_kv,
    cross_out,
    ffn_in,
    ffn_out,
    norm_gains,
    bias_rows,
    hidden_bias,
):
    model_width = tokens.shape[2]
    local_len = tokens.shape[1]
    seq_place = lax.axis_index("seq")
    base = (seq_place * local_len).astype(jnp.int32)
    rows = tokens.shape[0]
    base_ref = base.reshape((1,))
    tokens_full = gather_row(tokens)
    row_ids = gather_row(jnp.stack([segment_ids, source_ids]), axis=2)
    memory_full = gather_row(memory)
    row_segments, row_sources = row_ids[0], row_ids[1]
    row_len, source_len = row_segments.shape[1], row_sources.shape[1]
    source_pos = jnp.arange(source_len, dtype=jnp.int32)
    usable = source_pos[None] < source_lengths[:, None]
    masked_sources = jnp.where(usable, row_sources, 1 << 20)
    local_pos = base + jnp.arange(local_len, dtype=jnp.int32)
    local_usable = local_pos[None] < source_lengths[:, None]
    aux_query = aux_q(segment_ids)
    aux_key = aux_k(row_segments)
    aux_key_local = aux_k(segment_ids)
    aux_source = aux_k(row_sources, usable)
    aux_source_local = aux_k(source_ids, local_usable)

    wide = 256
    first_seg, last_seg = segment_ids[:, ::wide], segment_ids[:, wide - 1 :: wide]
    tops = base + jnp.arange(0, local_len, wide, dtype=jnp.int32)[None] + jnp.zeros((rows, 1), jnp.int32)
    low = count_below(row_segments, first_seg) // wide * wide
    self_start, self_count = window(low, tops + wide, wide, row_len)
    back_start, back_count = window(tops, count_below(row_segments, last_seg + 1), wide, row_len)
    fine = 128
    cross_start, cross_count = window(
        count_below(masked_sources, segment_ids[:, ::fine]),
        count_below(masked_sources, segment_ids[:, fine - 1 :: fine] + 1),
        wide,
        source_len,
    )
    source_tops = base + jnp.arange(0, local_len, fine, dtype=jnp.int32)[None]
    source_last = jnp.clip(source_lengths[:, None] - 1 - base, 0, local_len - 1)
    last_index = jnp.minimum(source_tops - base + fine - 1, source_last)
    source_high = jnp.take_along_axis(source_ids, last_index, axis=1)
    source_high = jnp.where(source_tops < source_lengths[:, None], source_high, -1)
    feed_start, feed_count = window(
        count_below(row_segments, source_ids[:, ::fine]),
        count_below(row_segments, source_high + 1),
        wide,
        row_len,
    )

    projected = project(tokens_full, self_qkv)
    queries_full = (projected[:, :, :model_width] + bias_rows[3]).astype(BF)
    key_full = projected[:, :, model_width : 2 * model_width].astype(BF)
    value_full = (projected[:, :, 2 * model_width :] + bias_rows[4]).astype(BF)
    local = lambda array: lax.dynamic_slice_in_dim(array, base, local_len, 1)
    queries = local(queries_full)
    attended, self_aux = fwd(
        wide, wide, True, 1, self_start, self_count, base_ref, queries, aux_query, key_full, value_full, aux_key
    )
    after_self, unit_first, root_first = normalize(
        tokens.astype(jnp.float32) + project(attended, self_out) + bias_rows[5],
        norm_gains[0],
        bias_rows[0],
    )
    self_low = after_self.astype(jnp.bfloat16)
    cross_query = (project(self_low, cross_q) + bias_rows[6]).astype(jnp.bfloat16)
    cross_query_full = gather_row(cross_query)
    key_value = project(memory_full, cross_kv)
    cross_key = key_value[:, :, :model_width].astype(BF)
    cross_value = (key_value[:, :, model_width:] + bias_rows[7]).astype(BF)
    crossed, cross_aux = fwd(
        fine, wide, False, 2, cross_start, cross_count, base_ref, cross_query, aux_query, cross_key, cross_value, aux_source
    )
    after_cross, unit_second, root_second = normalize(
        after_self + project(crossed, cross_out) + bias_rows[8], norm_gains[1], bias_rows[1]
    )
    cross_low = after_cross.astype(jnp.bfloat16)
    before = project(cross_low, ffn_in) + hidden_bias
    hidden = jax.nn.gelu(before, approximate=False).astype(jnp.bfloat16)
    output, unit_third, root_third = normalize(
        after_cross + project(hidden, ffn_out) + bias_rows[9], norm_gains[2], bias_rows[2]
    )
    grad_third, gain_third, shift_third = normalize_back(
        cotangent.astype(jnp.float32), unit_third, root_third, norm_gains[2]
    )
    ffn_branch = grad_third.astype(jnp.bfloat16)
    bias_ffn_out = token_sum(ffn_branch)
    grad_ffn_out = weight_grad(hidden, ffn_branch)
    grad_hidden = (input_grad(ffn_branch, ffn_out) * gelu_slope(before)).astype(jnp.bfloat16)
    grad_hbias = token_sum(grad_hidden)
    grad_ffn_in = weight_grad(cross_low, grad_hidden)
    grad_second = grad_third + input_grad(grad_hidden, ffn_in)
    grad_mid, gain_second, shift_second = normalize_back(
        grad_second, unit_second, root_second, norm_gains[1]
    )
    cross_branch = grad_mid.astype(jnp.bfloat16)
    bias_cross_out = token_sum(cross_branch)
    grad_cross_out = weight_grad(crossed, cross_branch)
    grad_crossed = input_grad(cross_branch, cross_out).astype(jnp.bfloat16)
    grad_crossed_full = gather_row(grad_crossed)
    cross_aux = with_inner(cross_aux, grad_crossed, crossed)
    cross_aux_full = gather_row(cross_aux)
    grad_cquery = bwd_dq(
        fine, wide, False, 2, cross_start, cross_count, base_ref, cross_query, grad_crossed, cross_aux, aux_source, cross_key, cross_value
    )
    bias_cross_query = token_sum(grad_cquery)
    grad_cross_q = weight_grad(self_low, grad_cquery)
    grad_first = grad_mid + input_grad(grad_cquery, cross_q)
    grad_start, gain_first, shift_first = normalize_back(
        grad_first, unit_first, root_first, norm_gains[0]
    )
    self_branch = grad_start.astype(jnp.bfloat16)
    bias_self_out = token_sum(self_branch)
    grad_self_out = weight_grad(attended, self_branch)
    grad_attended = input_grad(self_branch, self_out).astype(jnp.bfloat16)
    grad_attended_full = gather_row(grad_attended)
    self_aux = with_inner(self_aux, grad_attended, attended)
    self_aux_full = gather_row(self_aux)
    grad_ckey, grad_cvalue = bwd_dkv(
        fine, wide, False, 2, feed_start, feed_count, base_ref, cross_query_full, grad_crossed_full, cross_aux_full, aux_source_local,
        local(cross_key), local(cross_value)
    )
    grad_pair = jnp.concatenate([grad_ckey, grad_cvalue], axis=2)
    bias_cross_value = token_sum(grad_cvalue)
    grad_cross_kv = weight_grad(memory, grad_pair)
    grad_memory = input_grad(grad_pair, cross_kv).astype(jnp.bfloat16)
    grad_query = bwd_dq(
        wide, wide, True, 1, self_start, self_count, base_ref, queries, grad_attended, self_aux, aux_key, key_full, value_full
    )
    grad_key, grad_value = bwd_dkv(
        wide, wide, True, 1, back_start, back_count, base_ref, queries_full, grad_attended_full, self_aux_full, aux_key_local,
        local(key_full), local(value_full)
    )
    joined = jnp.concatenate([grad_query, grad_key, grad_value], axis=2)
    bias_query = token_sum(grad_query)
    bias_value = token_sum(grad_value)
    grad_self_qkv = weight_grad(tokens, joined)
    grad_tokens = (grad_start + input_grad(joined, self_qkv)).astype(jnp.bfloat16)
    reduced = lax.psum(
        (
            grad_self_qkv,
            grad_self_out,
            grad_cross_q,
            grad_cross_kv,
            grad_cross_out,
            grad_ffn_in,
            grad_ffn_out,
            jnp.stack([gain_first, gain_second, gain_third]),
            jnp.stack(
                [
                    shift_first,
                    shift_second,
                    shift_third,
                    bias_query,
                    bias_value,
                    bias_self_out,
                    bias_cross_query,
                    bias_cross_value,
                    bias_cross_out,
                    bias_ffn_out,
                ]
            ),
            grad_hbias,
        ),
        ("dp", "seq"),
    )
    return (
        output.astype(jnp.bfloat16),
        grad_tokens,
        grad_memory,
        reduced[0],
        reduced[1],
        reduced[2],
        reduced[3],
        reduced[4],
        reduced[5],
        reduced[6],
        reduced[7],
        reduced[8],
        reduced[9],
    )


def solution(mesh):
    placed = (
        P("dp", "seq", None),
        P("dp", "seq", None),
        P("dp", "seq"),
        P("dp", "seq"),
        P("dp"),
        P("dp", "seq", None),
        P(),
        P(),
        P(),
        P(),
        P(),
        P(),
        P(),
        P(),
        P(),
        P(),
    )
    return jax.shard_map(
        shards,
        mesh=mesh,
        in_specs=placed,
        out_specs=(
            P("dp", "seq", None),
            P("dp", "seq", None),
            P("dp", "seq", None),
            P(),
            P(),
            P(),
            P(),
            P(),
            P(),
            P(),
            P(),
            P(),
            P(),
        ),
        check_vma=False,
    )
```

```python
import functools

import jax
import jax.numpy as jnp
from jax import lax
from jax.experimental import pallas as pl
from jax.experimental.pallas import tpu as pltpu
from jax.sharding import PartitionSpec as P

HEADS = 8
SCORE_SCALE = 0.125
EPSILON = 1e-05
ROOT_HALF = 0.7071067811865476
NORMAL_DENSITY = 0.3989422804014327

BIG=float(2.0**30)
HALF=64
LSE=8; DELTA=32
NT=(((1,),(1,)),((),()))
F32=jnp.float32; BF=jnp.bfloat16
def lanes(shape): return lax.broadcasted_iota(jnp.int32,shape,len(shape)-1)
def pick(even, mine, aux):
    low=lanes(mine.shape)<HALF
    return jnp.where(low,mine,aux) if even else jnp.where(low,aux,mine)
def dot_nt(a,b): return lax.dot_general(a,b,NT,preferred_element_type=F32)
def dot_nn(a,b): return jnp.dot(a,b,preferred_element_type=F32)
def put_parts(aux,x,at):
    lane=lanes(aux.shape)%HALF
    hi=x.astype(BF).astype(F32); r=x-hi; mid=r.astype(BF).astype(F32)
    return jnp.where(lane==at,hi,jnp.where(lane==at+1,mid,jnp.where(lane==at+2,r-mid,aux)))
def row_const(shape,at,n,val):
    lane=lanes(shape)%HALF
    return (lane>=at)&(lane<at+n)
def schedule(n,ahead,first,rest):
    kept={}
    for h in range(min(ahead,n)): kept[h]=first(h)
    for h in range(n):
        if h+ahead<n: kept[h+ahead]=first(h+ahead)
        rest(h,kept.pop(h))

def fwd_kernel(tq,width,causal,ahead,start_ref,count_ref,base_ref,q_ref,aq_ref,k_ref,v_ref,ak_ref,o_ref,l_ref):
    rows=q_ref.shape[0]; subs=q_ref.shape[1]//tq; keys=k_ref.shape[1]; heads=q_ref.shape[2]//HALF
    def step(i,_):
        r=i//subs; s=i%subs
        n=count_ref[r,s]; st=pl.multiple_of(start_ref[r,s],128)
        qs=pl.ds(pl.multiple_of(s*tq,tq),tq)
        for blocks in range(1,keys//width+1):
            @pl.when(n==blocks)
            def _(blocks=blocks):
                span=blocks*width
                ks=pl.ds(st,span)
                ak=ak_ref[r,ks]; aq=aq_ref[r,qs]
                state={"stats":aq.astype(F32)}
                if causal:
                    qp=base_ref[0]+s*tq+lax.broadcasted_iota(jnp.int32,(tq,width),0)
                    kp=st+span-width+lax.broadcasted_iota(jnp.int32,(tq,width),1)
                    seen=kp<=qp
                def first(h):
                    cs=slice(h//2*128,h//2*128+128)
                    q=q_ref[r,qs,cs]*jnp.asarray(0.125,BF); k=k_ref[r,ks,cs]
                    return dot_nt(pick(h%2==0,q,aq),pick(h%2==0,k,ak))
                def rest(h,S):
                    cs=slice(h//2*128,h//2*128+128)
                    v=v_ref[r,ks,cs]
                    if causal:
                        tail=jnp.where(seen,S[:,span-width:],-BIG)
                        S=tail if blocks==1 else jnp.concatenate([S[:,:span-width],tail],axis=1)
                    m=jnp.max(S,axis=1,keepdims=True)
                    W=jnp.exp(S-m).astype(BF)
                    R=dot_nn(W,pick(h%2==0,v,jnp.ones_like(v)))
                    at=64 if h%2==0 else 0
                    state["stats"]=put_parts(state["stats"],m+jnp.log(R[:,at:at+1]),LSE+3*h)
                    if h%2==0: state["even"]=R
                    else:
                        low=lanes((tq,128))<HALF
                        total=pltpu.roll(jnp.where(low,R,state["even"]),HALF,1)
                        o_ref[r,qs,cs]=(jnp.where(low,state["even"],R)/total).astype(o_ref.dtype)
                schedule(heads,ahead,first,rest)
                l_ref[r,qs]=state["stats"].astype(BF)
        return 0
    lax.fori_loop(0,rows*subs,step,0)

def bwd_kernel(dkv,tq,width,causal,ahead,start_ref,count_ref,base_ref,a_ref,b_ref,aq_ref,ak_ref,k_ref,v_ref,*outs):
    loc=k_ref if dkv else a_ref
    win=a_ref if dkv else k_ref
    rows=loc.shape[0]; subs=loc.shape[1]//tq; keys=win.shape[1]; heads=loc.shape[2]//HALF
    def step(i,_):
        r=i//subs; s=i%subs
        n=count_ref[r,s]; st=pl.multiple_of(start_ref[r,s],128)
        ls=pl.ds(pl.multiple_of(s*tq,tq),tq)
        if dkv:
            @pl.when(n==0)
            def _():
                for out in outs: out[r,ls]=jnp.zeros((tq,out.shape[2]),out.dtype)
        for blocks in range(1,keys//width+1):
            @pl.when(n==blocks)
            def _(blocks=blocks):
                span=blocks*width
                ws=pl.ds(st,span)
                qs,ks=(ws,ls) if dkv else (ls,ws)
                ak=ak_ref[r,ks]; aq=aq_ref[r,qs]
                state={}
                if causal:
                    at=base_ref[0]+s*tq
                    if dkv:
                        seen=at+lax.broadcasted_iota(jnp.int32,(tq,width),0)<=st+lax.broadcasted_iota(jnp.int32,(tq,width),1)
                    else:
                        seen=st+span-width+lax.broadcasted_iota(jnp.int32,(tq,width),1)<=at+lax.broadcasted_iota(jnp.int32,(tq,width),0)
                minus=jnp.asarray(-1.0,BF)
                def first(h):
                    e=h%2==0
                    cs=slice(h//2*128,h//2*128+128)
                    q=a_ref[r,qs,cs]*jnp.asarray(0.125,BF); g=b_ref[r,qs,cs]; k=k_ref[r,ks,cs]; v=v_ref[r,ks,cs]
                    ka=pick(e,k,jnp.where(row_const(ak.shape,LSE+3*h,3,-1),minus,ak))
                    va=pick(e,v,jnp.where(row_const(v.shape,DELTA+3*h,3,-1),minus,jnp.zeros_like(v)))
                    qa=pick(e,q,aq); ga=pick(e,g,aq)
                    if dkv: return dot_nt(ka,qa),dot_nt(va,ga)
                    return dot_nt(qa,ka),dot_nt(ga,va)
                def rest(h,XG):
                    X,G=XG
                    cs=slice(h//2*128,h//2*128+128)
                    if causal:
                        if dkv:
                            X1=jnp.where(seen,X[:,:width],-BIG)
                            X=X1 if blocks==1 else jnp.concatenate([X1,X[:,width:]],axis=1)
                        else:
                            X1=jnp.where(seen,X[:,span-width:],-BIG)
                            X=X1 if blocks==1 else jnp.concatenate([X[:,:span-width],X1],axis=1)
                    W=jnp.exp(X); D=(W*G).astype(BF)
                    low=lanes((tq,128))<HALF
                    if not dkv:
                        R=dot_nn(D,k_ref[r,ks,cs])
                        if h%2==0: state["a"]=R
                        else: outs[0][r,ls,cs]=(0.125*jnp.where(low,state["a"],R)).astype(outs[0].dtype)
                    else:
                        R2=dot_nn(W.astype(BF),b_ref[r,qs,cs])
                        R=dot_nn(D,a_ref[r,qs,cs])
                        if h%2==0: state["a"]=R; state["b"]=R2
                        else:
                            outs[0][r,ls,cs]=(0.125*jnp.where(low,state["a"],R)).astype(outs[0].dtype)
                            outs[1][r,ls,cs]=jnp.where(low,state["b"],R2).astype(outs[1].dtype)
                schedule(heads,ahead,first,rest)
        return 0
    lax.fori_loop(0,rows*subs,step,0)
SM=pl.BlockSpec(memory_space=pltpu.SMEM); VM=pl.BlockSpec(memory_space=pltpu.VMEM)
def fwd(tq,width,causal,ahead,start,count,base,q,aq,k,v,ak):
    R,T,D=q.shape
    return pl.pallas_call(functools.partial(fwd_kernel,tq,width,causal,ahead),
        out_shape=(jax.ShapeDtypeStruct(q.shape,BF),jax.ShapeDtypeStruct((R,T,128),BF)),
        in_specs=[SM]*3+[VM]*5,out_specs=(VM,VM),name="attend_rows",
        compiler_params=pltpu.CompilerParams(vmem_limit_bytes=48<<20))(start,count,base,q,aq,k,v,ak)
def bwd_dq(tq,width,causal,ahead,start,count,base,q,g,aq,ak,k,v):
    return pl.pallas_call(functools.partial(bwd_kernel,False,tq,width,causal,ahead),
        out_shape=(jax.ShapeDtypeStruct(q.shape,BF),),
        in_specs=[SM]*3+[VM]*6,out_specs=(VM,),name="query_grad",
        compiler_params=pltpu.CompilerParams(vmem_limit_bytes=48<<20))(start,count,base,q,g,aq,ak,k,v)[0]
def bwd_dkv(tq,width,causal,ahead,start,count,base,q,g,aq,ak,k,v):
    return pl.pallas_call(functools.partial(bwd_kernel,True,tq,width,causal,ahead),
        out_shape=(jax.ShapeDtypeStruct(k.shape,BF),)*2,
        in_specs=[SM]*3+[VM]*6,out_specs=(VM,VM),name="key_grad",
        compiler_params=pltpu.CompilerParams(vmem_limit_bytes=48<<20))(start,count,base,q,g,aq,ak,k,v)
def aux_q(seg):
    lane=jnp.arange(128)%HALF
    return jnp.where((lane<8)&(seg[...,None]==lane),1.0,0.0).astype(BF)
def aux_k(seg,valid=None):
    lane=jnp.arange(128)%HALF
    ok=seg[...,None]==lane
    if valid is not None: ok=ok&valid[...,None]
    return jnp.where((lane<8)&~ok,-BIG,0.0).astype(BF)

def gather_row(block, axis=1):
    size = lax.axis_size("seq")
    place = lax.axis_index("seq")
    held = {0: block}
    bit = size // 2
    while bit:
        swap = [(i, i ^ bit) for i in range(size)]
        for key in list(held):
            held[key | bit] = lax.ppermute(held[key], "seq", swap)
        bit //= 2
    shape = list(block.shape)
    extent = shape[axis]
    shape[axis] = extent * size
    full = jnp.zeros(shape, block.dtype)
    for key, value in held.items():
        at = [0] * len(shape)
        at[axis] = (place ^ key) * extent
        full = lax.dynamic_update_slice(full, value, at)
    return full


def count_below(ids, bound):
    return jnp.sum((ids[:, None, :] < bound[:, :, None]).astype(jnp.int32), axis=-1)


def window(low, high, width, extent):
    floor = low // 128 * 128
    blocks = jnp.where(high > low, (high - floor + width - 1) // width, 0)
    start = jnp.minimum(floor, extent - blocks * width)
    return start.astype(jnp.int32), blocks.astype(jnp.int32)


def with_inner(aux, grad_mixed, mixed):
    width = mixed.shape[-1]
    lane = jnp.arange(128) % HALF
    head = (lane - DELTA) // 3
    chosen = (
        (jnp.arange(width)[:, None] // HALF == head[None]) & (lane >= DELTA) & (lane < DELTA + 3 * HEADS)
    ).astype(F32)
    inner = jnp.einsum(
        "rtd,dl->rtl",
        grad_mixed.astype(F32) * mixed.astype(F32),
        chosen,
        precision=lax.Precision.HIGHEST,
        preferred_element_type=F32,
    )
    high = lax.reduce_precision(inner, 8, 7)
    rest = inner - high
    middle = lax.reduce_precision(rest, 8, 7)
    part = (lane - DELTA) % 3
    return (
        aux.astype(F32) + jnp.where(part == 0, high, jnp.where(part == 1, middle, rest - middle))
    ).astype(BF)

def project(values, weight):
    return jnp.einsum("rtd,de->rte", values, weight, preferred_element_type=jnp.float32)


def weight_grad(left, right):
    return jnp.einsum("rtd,rte->de", left, right, preferred_element_type=jnp.float32)


def input_grad(grad, weight):
    return jnp.einsum("rte,de->rtd", grad, weight, preferred_element_type=jnp.float32)


def token_sum(values):
    return jnp.sum(values.astype(jnp.float32), axis=(0, 1))


def gelu_slope(values):
    return 0.5 * (1.0 + lax.erf(values * ROOT_HALF)) + values * NORMAL_DENSITY * jnp.exp(
        -0.5 * values * values
    )


MESH = pl.DeviceIdType.MESH


def dimensions(dp_size, seq_size):
    dp, seq = lax.axis_index("dp"), lax.axis_index("seq")
    return {
        "core": (2, seq % 2, lambda i: (dp, seq - seq % 2 + i)),
        "y": (seq_size // 2, seq // 2, lambda i: (dp, i * 2 + seq % 2)),
        "x": (2, dp % 2, lambda i: (dp - dp % 2 + i, seq)),
        "z": (dp_size // 2, dp // 2, lambda i: (i * 2 + dp % 2, seq)),
    }


ORDERS = (("core", "x", "y", "z"), ("core", "y", "x", "z"))


def exchange_sizes(dp_size, seq_size):
    return {"core": 2, "y": seq_size // 2, "x": 2, "z": dp_size // 2}


def sum_kernel(dp_size, seq_size, chunks, src, small, out, small_out, *scratch):
    dims = dimensions(dp_size, seq_size)
    stages = 4
    held = scratch[: chunks * stages]
    (gathered, small_slots, small_sum, send, recv, small_send, small_recv, save) = scratch[chunks * stages :]
    total_rows = src.shape[0]
    rows = total_rows // chunks

    peers = [(name, step) for name in dims for step in range(1, dims[name][0])]
    barrier = pltpu.get_barrier_semaphore()
    for name, step in peers:
        size, me, device = dims[name]
        pl.semaphore_signal(barrier, inc=1, device_id=device((me + step) % size), device_id_type=MESH)
    pl.semaphore_wait(barrier, len(peers))

    def reduce_copies(c, s):
        size, me, device = dims[ORDERS[c % len(ORDERS)][s]]
        current = src.at[pl.ds(c * rows, rows)] if s == 0 else held[c * stages + s - 1].at[0]
        piece = current.shape[0] // size
        copies = []
        for step in range(1, size):
            other = (me + step) % size
            copies.append(
                pltpu.make_async_remote_copy(
                    src_ref=current.at[pl.ds(pl.multiple_of(other * piece, piece), piece)],
                    dst_ref=held[c * stages + s].at[size - step - 1],
                    send_sem=send.at[c, s, step - 1],
                    recv_sem=recv.at[c, s, size - step - 1],
                    device_id=device(other),
                    device_id_type=MESH,
                )
            )
        return copies

    def offset(c, s):
        at, extent = c * rows, rows
        for name in ORDERS[c % len(ORDERS)][:s]:
            size, me, _ = dims[name]
            extent //= size
            at = at + me * extent
        return pl.multiple_of(at, extent), extent

    def spread_copies(c, s):
        size, me, device = dims[ORDERS[c % len(ORDERS)][s - 1]]
        at, extent = offset(c, s)
        copies = []
        for step in range(1, size):
            other = (me + step) % size
            copies.append(
                pltpu.make_async_remote_copy(
                    src_ref=gathered.at[pl.ds(at, extent)],
                    dst_ref=gathered.at[pl.ds(at, extent)],
                    send_sem=send.at[c, 2 * stages - s, step - 1],
                    recv_sem=recv.at[c, 2 * stages - s, size - step - 1],
                    device_id=device(other),
                    device_id_type=MESH,
                )
            )
        return copies

    def add_arrived(c, s):
        size, me, _ = dims[ORDERS[c % len(ORDERS)][s]]
        current = src.at[pl.ds(c * rows, rows)] if s == 0 else held[c * stages + s - 1].at[0]
        piece = current.shape[0] // size
        mine = current.at[pl.ds(pl.multiple_of(me * piece, piece), piece)]
        block = min(piece, 128)
        last = s == stages - 1
        at = offset(c, stages)[0] if last else 0

        def add(i, carry):
            part = pl.ds(pl.multiple_of(i * block, block), block)
            value = mine[part].astype(F32)
            for slot in range(size - 1):
                value = value + held[c * stages + s][slot, part].astype(F32)
            if last:
                gathered[pl.ds(pl.multiple_of(at + i * block, 16), block)] = value.astype(BF)
            else:
                held[c * stages + s][0, part] = value.astype(BF)
            return carry

        lax.fori_loop(0, piece // block, add, 0)

    small_names = ("core", "x", "y", "z")

    def small_copies(s):
        size, me, device = dims[small_names[s]]
        copies = []
        for step in range(1, size):
            copies.append(
                pltpu.make_async_remote_copy(
                    src_ref=small_sum.at[s],
                    dst_ref=small_slots.at[s, me],
                    send_sem=small_send.at[s, step - 1],
                    recv_sem=small_recv.at[s, size - step - 1],
                    device_id=device((me + step) % size),
                    device_id_type=MESH,
                )
            )
        return copies

    started = {}

    def begin(key, copies):
        for copy in copies:
            copy.start()
        started[key] = copies

    def finish(key):
        for copy in started[key]:
            copy.wait()

    small_sum[0] = small[...]
    saves = []
    for wave in range((chunks - 1) // len(ORDERS) + 2 * stages + 1):
        for c in range(chunks):
            s = wave - c // len(ORDERS)
            if s == 0:
                begin((c, 0), reduce_copies(c, 0))
            elif 1 <= s <= stages:
                finish((c, s - 1))
                add_arrived(c, s - 1)
                if s < stages:
                    begin((c, s), reduce_copies(c, s))
                else:
                    begin((c, s), spread_copies(c, stages))
            elif stages < s <= 2 * stages:
                finish((c, s - 1))
                if s < 2 * stages:
                    begin((c, s), spread_copies(c, 2 * stages - s))
                else:
                    part = pl.ds(c * rows, rows)
                    copy = pltpu.make_async_copy(gathered.at[part], out.at[part], save.at[c])
                    copy.start()
                    saves.append(copy)
        if wave <= stages:
            if wave > 0:
                finish(("small", wave - 1))
                size, me, _ = dims[small_names[wave - 1]]
                small_slots[wave - 1, me] = small_sum[wave - 1]
                value = small_slots[wave - 1, 0]
                for i in range(1, size):
                    value = value + small_slots[wave - 1, i]
                small_sum[wave] = value
            if wave < stages:
                begin(("small", wave), small_copies(wave))
    small_out[...] = small_sum[stages]
    for copy in saves:
        copy.wait()


def sum_over_devices(mesh_shape, values, small):
    dp_size, seq_size = mesh_shape["dp"], mesh_shape["seq"]
    sizes = exchange_sizes(dp_size, seq_size)
    total_rows, columns = values.shape
    per_device = 1
    for size in sizes.values():
        per_device *= size
    chunks = min(16, total_rows // (16 * per_device))
    most = max(sizes.values())
    scratch = []
    for c in range(chunks):
        extent = total_rows // chunks
        for name in ORDERS[c % len(ORDERS)]:
            extent //= sizes[name]
            scratch.append(pltpu.VMEM((sizes[name] - 1, extent, columns), BF))
    scratch += [
        pltpu.VMEM((total_rows, columns), BF),
        pltpu.VMEM((4, most) + small.shape, F32),
        pltpu.VMEM((5,) + small.shape, F32),
        pltpu.SemaphoreType.DMA((chunks, 8, most - 1)),
        pltpu.SemaphoreType.DMA((chunks, 8, most - 1)),
        pltpu.SemaphoreType.DMA((4, most - 1)),
        pltpu.SemaphoreType.DMA((4, most - 1)),
        pltpu.SemaphoreType.DMA((chunks,)),
    ]
    return pl.pallas_call(
        functools.partial(sum_kernel, dp_size, seq_size, chunks),
        out_shape=(jax.ShapeDtypeStruct(values.shape, BF), jax.ShapeDtypeStruct(small.shape, F32)),
        in_specs=[VM, VM],
        out_specs=(pl.BlockSpec(memory_space=pl.ANY), VM),
        scratch_shapes=scratch,
        name="sum_grads",
        compiler_params=pltpu.CompilerParams(collective_id=0, has_side_effects=True, vmem_limit_bytes=52 << 20),
    )(values, small)


def normalize(residual, gain, shift):
    centred = residual - jnp.mean(residual, axis=-1, keepdims=True)
    inverse_root = lax.rsqrt(jnp.mean(centred * centred, axis=-1, keepdims=True) + EPSILON)
    unit_rows = centred * inverse_root
    return (unit_rows * gain + shift, unit_rows, inverse_root)


def normalize_back(grad, unit_rows, inverse_root, gain):
    scaled = grad * gain
    grad_residual = inverse_root * (
        scaled
        - jnp.mean(scaled, axis=-1, keepdims=True)
        - unit_rows * jnp.mean(scaled * unit_rows, axis=-1, keepdims=True)
    )
    return (grad_residual, jnp.sum(grad * unit_rows, axis=(0, 1)), jnp.sum(grad, axis=(0, 1)))


def shards(
    mesh_shape,
    tokens,
    memory,
    segment_ids,
    source_ids,
    source_lengths,
    cotangent,
    self_qkv,
    self_out,
    cross_q,
    cross_kv,
    cross_out,
    ffn_in,
    ffn_out,
    norm_gains,
    bias_rows,
    hidden_bias,
):
    model_width = tokens.shape[2]
    local_len = tokens.shape[1]
    seq_place = lax.axis_index("seq")
    base = (seq_place * local_len).astype(jnp.int32)
    rows = tokens.shape[0]
    base_ref = base.reshape((1,))
    tokens_full = gather_row(tokens)
    row_ids = gather_row(jnp.stack([segment_ids, source_ids]), axis=2)
    memory_full = gather_row(memory)
    row_segments, row_sources = row_ids[0], row_ids[1]
    row_len, source_len = row_segments.shape[1], row_sources.shape[1]
    source_pos = jnp.arange(source_len, dtype=jnp.int32)
    usable = source_pos[None] < source_lengths[:, None]
    masked_sources = jnp.where(usable, row_sources, 1 << 20)
    local_pos = base + jnp.arange(local_len, dtype=jnp.int32)
    local_usable = local_pos[None] < source_lengths[:, None]
    aux_query = aux_q(segment_ids)
    aux_key = aux_k(row_segments)
    aux_key_local = aux_k(segment_ids)
    aux_source = aux_k(row_sources, usable)
    aux_source_local = aux_k(source_ids, local_usable)

    wide = 256
    first_seg, last_seg = segment_ids[:, ::wide], segment_ids[:, wide - 1 :: wide]
    tops = base + jnp.arange(0, local_len, wide, dtype=jnp.int32)[None] + jnp.zeros((rows, 1), jnp.int32)
    low = count_below(row_segments, first_seg) // wide * wide
    self_start, self_count = window(low, tops + wide, wide, row_len)
    back_start, back_count = window(tops, count_below(row_segments, last_seg + 1), wide, row_len)
    fine = 128
    cross_start, cross_count = window(
        count_below(masked_sources, segment_ids[:, ::fine]),
        count_below(masked_sources, segment_ids[:, fine - 1 :: fine] + 1),
        wide,
        source_len,
    )
    source_tops = base + jnp.arange(0, local_len, fine, dtype=jnp.int32)[None]
    source_last = jnp.clip(source_lengths[:, None] - 1 - base, 0, local_len - 1)
    last_index = jnp.minimum(source_tops - base + fine - 1, source_last)
    source_high = jnp.take_along_axis(source_ids, last_index, axis=1)
    source_high = jnp.where(source_tops < source_lengths[:, None], source_high, -1)
    feed_start, feed_count = window(
        count_below(row_segments, source_ids[:, ::fine]),
        count_below(row_segments, source_high + 1),
        wide,
        row_len,
    )

    projected = project(tokens_full, self_qkv)
    queries_full = (projected[:, :, :model_width] + bias_rows[3]).astype(BF)
    key_full = projected[:, :, model_width : 2 * model_width].astype(BF)
    value_full = (projected[:, :, 2 * model_width :] + bias_rows[4]).astype(BF)
    local = lambda array: lax.dynamic_slice_in_dim(array, base, local_len, 1)
    queries = local(queries_full)
    attended, self_aux = fwd(
        wide, wide, True, 1, self_start, self_count, base_ref, queries, aux_query, key_full, value_full, aux_key
    )
    after_self, unit_first, root_first = normalize(
        tokens.astype(jnp.float32) + project(attended, self_out) + bias_rows[5],
        norm_gains[0],
        bias_rows[0],
    )
    self_low = after_self.astype(jnp.bfloat16)
    cross_query = (project(self_low, cross_q) + bias_rows[6]).astype(jnp.bfloat16)
    cross_query_full = gather_row(cross_query)
    key_value = project(memory_full, cross_kv)
    cross_key = key_value[:, :, :model_width].astype(BF)
    cross_value = (key_value[:, :, model_width:] + bias_rows[7]).astype(BF)
    crossed, cross_aux = fwd(
        fine, wide, False, 2, cross_start, cross_count, base_ref, cross_query, aux_query, cross_key, cross_value, aux_source
    )
    after_cross, unit_second, root_second = normalize(
        after_self + project(crossed, cross_out) + bias_rows[8], norm_gains[1], bias_rows[1]
    )
    cross_low = after_cross.astype(jnp.bfloat16)
    before = project(cross_low, ffn_in) + hidden_bias
    hidden = jax.nn.gelu(before, approximate=False).astype(jnp.bfloat16)
    output, unit_third, root_third = normalize(
        after_cross + project(hidden, ffn_out) + bias_rows[9], norm_gains[2], bias_rows[2]
    )
    grad_third, gain_third, shift_third = normalize_back(
        cotangent.astype(jnp.float32), unit_third, root_third, norm_gains[2]
    )
    ffn_branch = grad_third.astype(jnp.bfloat16)
    bias_ffn_out = token_sum(ffn_branch)
    grad_ffn_out = weight_grad(hidden, ffn_branch)
    grad_hidden = (input_grad(ffn_branch, ffn_out) * gelu_slope(before)).astype(jnp.bfloat16)
    grad_hbias = token_sum(grad_hidden)
    grad_ffn_in = weight_grad(cross_low, grad_hidden)
    grad_second = grad_third + input_grad(grad_hidden, ffn_in)
    grad_mid, gain_second, shift_second = normalize_back(
        grad_second, unit_second, root_second, norm_gains[1]
    )
    cross_branch = grad_mid.astype(jnp.bfloat16)
    bias_cross_out = token_sum(cross_branch)
    grad_cross_out = weight_grad(crossed, cross_branch)
    grad_crossed = input_grad(cross_branch, cross_out).astype(jnp.bfloat16)
    grad_crossed_full = gather_row(grad_crossed)
    cross_aux = with_inner(cross_aux, grad_crossed, crossed)
    cross_aux_full = gather_row(cross_aux)
    grad_cquery = bwd_dq(
        fine, wide, False, 2, cross_start, cross_count, base_ref, cross_query, grad_crossed, cross_aux, aux_source, cross_key, cross_value
    )
    bias_cross_query = token_sum(grad_cquery)
    grad_cross_q = weight_grad(self_low, grad_cquery)
    grad_first = grad_mid + input_grad(grad_cquery, cross_q)
    grad_start, gain_first, shift_first = normalize_back(
        grad_first, unit_first, root_first, norm_gains[0]
    )
    self_branch = grad_start.astype(jnp.bfloat16)
    bias_self_out = token_sum(self_branch)
    grad_self_out = weight_grad(attended, self_branch)
    grad_attended = input_grad(self_branch, self_out).astype(jnp.bfloat16)
    grad_attended_full = gather_row(grad_attended)
    self_aux = with_inner(self_aux, grad_attended, attended)
    self_aux_full = gather_row(self_aux)
    grad_ckey, grad_cvalue = bwd_dkv(
        fine, wide, False, 2, feed_start, feed_count, base_ref, cross_query_full, grad_crossed_full, cross_aux_full, aux_source_local,
        local(cross_key), local(cross_value)
    )
    grad_pair = jnp.concatenate([grad_ckey, grad_cvalue], axis=2)
    bias_cross_value = token_sum(grad_cvalue)
    grad_cross_kv = weight_grad(memory, grad_pair)
    grad_memory = input_grad(grad_pair, cross_kv).astype(jnp.bfloat16)
    grad_query = bwd_dq(
        wide, wide, True, 1, self_start, self_count, base_ref, queries, grad_attended, self_aux, aux_key, key_full, value_full
    )
    grad_key, grad_value = bwd_dkv(
        wide, wide, True, 1, back_start, back_count, base_ref, queries_full, grad_attended_full, self_aux_full, aux_key_local,
        local(key_full), local(value_full)
    )
    joined = jnp.concatenate([grad_query, grad_key, grad_value], axis=2)
    bias_query = token_sum(grad_query)
    bias_value = token_sum(grad_value)
    grad_self_qkv = weight_grad(tokens, joined)
    grad_tokens = (grad_start + input_grad(joined, self_qkv)).astype(jnp.bfloat16)
    def columns(value):
        return [value[:, i * 512 : i * 512 + 512] for i in range(value.shape[1] // 512)]

    low = lambda value: value.astype(BF)
    values = jnp.concatenate(
        columns(low(grad_self_qkv)) + [low(grad_self_out), low(grad_cross_q)] + columns(low(grad_cross_kv))
        + [low(grad_cross_out)] + columns(low(grad_ffn_in)) + [low(grad_ffn_out)],
        axis=0,
    )
    small = jnp.concatenate(
        [
            jnp.stack([gain_first, gain_second, gain_third, shift_first, shift_second, shift_third, bias_query, bias_value,
                       bias_self_out, bias_cross_query, bias_cross_value, bias_cross_out, bias_ffn_out]),
            grad_hbias.reshape(4, 512),
            jnp.zeros((7, 512), F32),
        ],
        axis=0,
    )
    values, small = sum_over_devices(mesh_shape, values, small)

    def block(first, count):
        return jnp.concatenate([values[512 * (first + i) : 512 * (first + i) + 512] for i in range(count)], axis=1).astype(F32)

    return (
        output.astype(BF), grad_tokens, grad_memory, block(0, 3), block(3, 1), block(4, 1), block(5, 2), block(7, 1), block(8, 4),
        values[6144:].astype(F32), small[:3], small[3:13], small[13:17].reshape(2048),
    )


def solution(mesh):
    placed = (
        P("dp", "seq", None),
        P("dp", "seq", None),
        P("dp", "seq"),
        P("dp", "seq"),
        P("dp"),
        P("dp", "seq", None),
        P(),
        P(),
        P(),
        P(),
        P(),
        P(),
        P(),
        P(),
        P(),
        P(),
    )
    return jax.shard_map(
        functools.partial(shards, dict(mesh.shape)),
        mesh=mesh,
        in_specs=placed,
        out_specs=(
            P("dp", "seq", None),
            P("dp", "seq", None),
            P("dp", "seq", None),
            P(),
            P(),
            P(),
            P(),
            P(),
            P(),
            P(),
            P(),
            P(),
            P(),
        ),
        check_vma=False,
    )
```

```python
import functools

import jax
import jax.numpy as jnp
from jax import lax
from jax.experimental import pallas as pl
from jax.experimental.pallas import tpu as pltpu
from jax.sharding import PartitionSpec as P

HEADS = 8
SCORE_SCALE = 0.125
EPSILON = 1e-05
ROOT_HALF = 0.7071067811865476
NORMAL_DENSITY = 0.3989422804014327

BIG=float(2.0**30)
HALF=64
LSE=8; DELTA=32
NT=(((1,),(1,)),((),()))
F32=jnp.float32; BF=jnp.bfloat16
def lanes(shape): return lax.broadcasted_iota(jnp.int32,shape,len(shape)-1)
def pick(even, mine, aux):
    low=lanes(mine.shape)<HALF
    return jnp.where(low,mine,aux) if even else jnp.where(low,aux,mine)
def dot_nt(a,b): return lax.dot_general(a,b,NT,preferred_element_type=F32)
def dot_nn(a,b): return jnp.dot(a,b,preferred_element_type=F32)
def put_parts(aux,x,at):
    lane=lanes(aux.shape)%HALF
    hi=x.astype(BF).astype(F32); r=x-hi; mid=r.astype(BF).astype(F32)
    return jnp.where(lane==at,hi,jnp.where(lane==at+1,mid,jnp.where(lane==at+2,r-mid,aux)))
def row_const(shape,at,n):
    lane=lanes(shape)%HALF
    return (lane>=at)&(lane<at+n)
def schedule(heads,ahead,first,rest):
    heads=list(heads) if not isinstance(heads,int) else list(range(heads))
    kept={}
    for h in heads[:ahead]: kept[h]=first(h)
    for i,h in enumerate(heads):
        if i+ahead<len(heads): kept[heads[i+ahead]]=first(heads[i+ahead])
        rest(h,kept.pop(h))


VM = pl.BlockSpec(memory_space=pltpu.VMEM)

MESH = pl.DeviceIdType.MESH


def dimensions(dp_size, seq_size):
    dp, seq = lax.axis_index("dp"), lax.axis_index("seq")
    return {
        "core": (2, seq % 2, lambda i: (dp, seq - seq % 2 + i)),
        "y": (seq_size // 2, seq // 2, lambda i: (dp, i * 2 + seq % 2)),
        "x": (2, dp % 2, lambda i: (dp - dp % 2 + i, seq)),
        "z": (dp_size // 2, dp // 2, lambda i: (i * 2 + dp % 2, seq)),
        "near": (2, dp // 2 % 2, lambda i: (dp + (i - dp // 2 % 2) * 2, seq)),
        "far": (dp_size // 4, dp // 4, lambda i: (i * 4 + dp % 4, seq)),
    }


def plan(chunks):
    if chunks != 16:
        orders = [("core", "x", "y", "z"), ("core", "y", "x", "z")] * (chunks // 2)
        waiting = [0] * (chunks // 2) + [20] * (chunks - chunks // 2)
        sequence = []
        for slot in range(21):
            sequence += [c for c in range(chunks) if waiting[c] <= slot < waiting[c] + 9]
            sequence.append(-1)
        sequence += [c for _ in range(8) for c in range(chunks) if waiting[c] == 20]
        return orders, sequence + [chunks] * 5
    kinds = (
        ('core', 'near', 'far', 'x', 'y'),
        ('core', 'x', 'near', 'far', 'y'),
        ('core', 'near', 'far', 'y', 'x'),
        ('core', 'near', 'x', 'far', 'y'),
        ('core', 'y', 'x', 'near', 'far'),
        ('core', 'x', 'y', 'z'),
        ('core', 'x', 'y', 'near', 'far'),
        ('core', 'x', 'near', 'y', 'far'),
        ('core', 'y', 'x', 'z'),
    )
    orders = [kinds[i] for i in (0, 1, 2, 3, 4, 1, 4, 1, 0, 5, 6, 7, 6, 8, 8, 5)]
    sequence = [4, 7, 6, 3, 0, 2, 8, 1, 5, -1, -1, -1, 4, 7, 6, 3, 0, 2, 8, 1, 5, -1, -1, 4, 7, 6, 3, 0, 2, 8, 1, 9, 10, 5, -1, 9, 10, -1, 4, 6, 7, 3, -1, -1, 4, 6, 7, 3, 0, 2, 8, 1, 9, 10, 5, -1, 4, 7, 6, 3, 0, 2, 8, 1, 11, 9, 10, 5, 12, -1, 4, 7, 6, 3, 0, 2, 8, 1, 11, 10, 5, 12, 9, -1, 0, 2, 8, 1, 5, -1, 4, 6, 2, 10, -1, 7, 3, 0, 8, -1, 9, 13, -1, 11, 10, 1, 13, 9, 5, -1, 4, 7, 6, 3, 12, -1, 9, 10, 13, -1, 0, 2, 7, 8, 1, 11, 9, 5, -1, 7, 3, 13, 12, 14, 15, 16, -1, 10, 11, 3, 4, 6, 14, 15, 1, 4, 6, 16, 11, 12, 5, 13, 1, 14, 5, 11, 12, 10, 16, 0, 11, 2, 8, 15, 12, 13, 14, 10, 0, 16, 2, 8, 15, 13, 12, 11, 14, 15, 14, 12, 16, 11, 15, 13, 11, 14, 13, 15, 12, 12, 14, 15, 14, 15]
    return orders, sequence


def exchange_sizes(dp_size, seq_size):
    return {"core": 2, "y": seq_size // 2, "x": 2, "z": dp_size // 2, "near": 2, "far": dp_size // 4}


def row_grads(dkv, heads, tq, blocks, width, seen, a, b, aq, ak, k, v, put):
    state = {}
    minus = jnp.asarray(-1.0, BF)
    edge = (slice(None), slice(0, width)) if dkv else (slice(None), slice((blocks - 1) * width, blocks * width))

    def columns(h):
        return slice(h // 2 * 128, h // 2 * 128 + 128)

    def first(h):
        e, cs = h % 2 == 0, columns(h)
        keys, values = k(cs), v(cs)
        ka = pick(e, keys, jnp.where(row_const(keys.shape, LSE + 3 * h, 3), minus, ak))
        va = pick(e, values, jnp.where(row_const(values.shape, DELTA + 3 * h, 3), minus, jnp.zeros_like(values)))
        qa, ga = pick(e, a(cs) * jnp.asarray(SCORE_SCALE, BF), aq), pick(e, b(cs), aq)
        return (dot_nt(ka, qa), dot_nt(va, ga)) if dkv else (dot_nt(qa, ka), dot_nt(ga, va))

    def rest(h, pair):
        scores, grads = pair
        cs = columns(h)
        if seen is not None:
            masked = jnp.where(seen, scores[edge], -BIG)
            if blocks == 1:
                scores = masked
            elif dkv:
                scores = jnp.concatenate([masked, scores[:, width:]], axis=1)
            else:
                scores = jnp.concatenate([scores[:, : (blocks - 1) * width], masked], axis=1)
        weights = jnp.exp(scores)
        grad_scores = (weights * grads).astype(BF)
        low = lanes((tq, 128)) < HALF
        if dkv:
            values_grad = dot_nn(weights.astype(BF), b(cs))
            keys_grad = dot_nn(grad_scores, a(cs))
            if h % 2 == 0:
                state["k"], state["v"] = keys_grad, values_grad
            else:
                put(cs, SCORE_SCALE * jnp.where(low, state["k"], keys_grad), jnp.where(low, state["v"], values_grad))
        else:
            query_grad = dot_nn(grad_scores, k(cs))
            if h % 2 == 0:
                state["q"] = query_grad
            else:
                put(cs, SCORE_SCALE * jnp.where(low, state["q"], query_grad))

    schedule(heads, 1, first, rest)


TN = (((0,), (0,)), ((), ()))


def dot_tn(a, b):
    return lax.dot_general(a, b, TN, preferred_element_type=F32)


def head_inner(grad_mixed, mixed):
    product = grad_mixed.astype(F32) * mixed.astype(F32)
    lane = lax.broadcasted_iota(jnp.int32, (product.shape[1], 128), 1) % HALF
    head = lax.broadcasted_iota(jnp.int32, (product.shape[1], 128), 0) // HALF
    first = DELTA + 3 * head
    chosen = jnp.where((lane >= first) & (lane < first + 3), 1.0, 0.0).astype(BF)
    high = product.astype(BF)
    rest = product - high.astype(F32)
    middle = rest.astype(BF)
    inner = dot_nn(high, chosen) + dot_nn(middle, chosen) + dot_nn((rest - middle.astype(F32)).astype(BF), chosen)
    high = inner.astype(BF).astype(F32)
    rest = inner - high
    middle = rest.astype(BF).astype(F32)
    part = (lanes(inner.shape) % HALF - DELTA + 3) % 3
    return jnp.where(part == 0, high, jnp.where(part == 1, middle, rest - middle))


GROUP = 2


def back_kernel(dp_size, seq_size, chunks, orders, sequence,
                cross_out_grad, small, grad_crossed, cross_aux, self_aux, root, gain, away_refs,
                out, small_out, grad_tokens, grad_memory, *scratch):
    dims = dimensions(dp_size, seq_size)
    held = [[None] * len(order) for order in orders]
    taken = 0
    for c, order in enumerate(orders):
        for s in range(len(order)):
            held[c][s] = scratch[taken]
            taken += 1
    (own, gathered, small_slots, small_sum, gc_full, caux_full, ga_full, saux_full, dcq, pair, joined,
     send, recv, small_send, small_recv, save, row_send, row_recv, local_sem, load_sem, *here_refs) = scratch[taken:]
    half_rows = own.shape[0]
    total_rows = 2 * half_rows
    rows = total_rows // chunks
    place = lax.axis_index("seq")
    batch, length, width = grad_crossed.shape
    heads = width // HALF
    base = pl.multiple_of(place * length, length)
    mine = pl.ds(base, length)
    flat = batch * length

    peers = [(name, step) for name in ("core", "x", "y", "z") for step in range(1, dims[name][0])]
    barrier = pltpu.get_barrier_semaphore()
    for name, step in peers:
        size, me, device = dims[name]
        pl.semaphore_signal(barrier, inc=1, device_id=device((me + step) % size), device_id_type=MESH)

    locals_ = []
    for i, (block, full) in enumerate(((grad_crossed, gc_full), (cross_aux, caux_full))):
        locals_.append(pltpu.make_async_copy(block, full.at[:, mine], local_sem.at[i]))
    locals_.append(pltpu.make_async_copy(cross_out_grad, own.at[pl.ds(0, width)], local_sem.at[2]))
    for copy in locals_:
        copy.start()
    loads = {}
    here_refs = list(here_refs)
    here_refs[13:13] = here_refs[1:3]
    for i, (away, here) in enumerate(zip(away_refs, here_refs)):
        loads[i] = pltpu.make_async_copy(away, here, load_sem.at[i])
        if i not in (13, 14):
            loads[i].start()

    def load_later():
        loads[13].start()
        loads[14].start()

    def loaded(*which):
        def run():
            for i in which:
                loads.pop(i).wait()

        return run

    (ffn_grads, cross_key, cross_value, mask, self_low, unit, grad_mid, cross_q, self_out, attended, memory, cross_kv,
     cq_full, queries, keys, values, tokens, self_qkv) = here_refs
    small_value = [small[...]]
    pl.semaphore_wait(barrier, len(peers))
    for copy in locals_:
        copy.wait()

    def source(c):
        at = c * rows
        return ffn_grads.at[pl.ds(at, rows)] if at < half_rows else own.at[pl.ds(at - half_rows, rows)]

    def current(c, s):
        return source(c) if s == 0 else held[c][s - 1].at[0]

    def reduce_copies(c, s):
        size, me, device = dims[orders[c][s]]
        now = current(c, s)
        piece = now.shape[0] // size
        copies = []
        for step in range(1, size):
            other = (me + step) % size
            copies.append(
                pltpu.make_async_remote_copy(
                    src_ref=now.at[pl.ds(pl.multiple_of(other * piece, piece), piece)],
                    dst_ref=held[c][s].at[size - step - 1],
                    send_sem=send.at[c, s, step - 1],
                    recv_sem=recv.at[c, s, size - step - 1],
                    device_id=device(other),
                    device_id_type=MESH,
                )
            )
        return copies

    def offset(c, s):
        at, extent = c * rows, rows
        for name in orders[c][:s]:
            size, me, _ = dims[name]
            extent //= size
            at = at + me * extent
        return pl.multiple_of(at, extent), extent

    def spread_copies(c, s):
        size, me, device = dims[orders[c][s - 1]]
        at, extent = offset(c, s)
        copies = []
        for step in range(1, size):
            copies.append(
                pltpu.make_async_remote_copy(
                    src_ref=gathered.at[pl.ds(at, extent)],
                    dst_ref=gathered.at[pl.ds(at, extent)],
                    send_sem=send.at[c, 2 * len(orders[c]) - s, step - 1],
                    recv_sem=recv.at[c, 2 * len(orders[c]) - s, size - step - 1],
                    device_id=device((me + step) % size),
                    device_id_type=MESH,
                )
            )
        return copies

    def add_arrived(c, s):
        size, me, _ = dims[orders[c][s]]
        now = current(c, s)
        piece = now.shape[0] // size
        kept = now.at[pl.ds(pl.multiple_of(me * piece, piece), piece)]
        block = min(piece, 128)
        last = s == len(orders[c]) - 1
        at = offset(c, len(orders[c]))[0] if last else 0

        def add(i, carry):
            part = pl.ds(pl.multiple_of(i * block, block), block)
            value = kept[part].astype(F32)
            for slot in range(size - 1):
                value = value + held[c][s][slot, part].astype(F32)
            if last:
                gathered[pl.ds(pl.multiple_of(at + i * block, 16), block)] = value.astype(BF)
            else:
                held[c][s][0, part] = value.astype(BF)
            return carry

        lax.fori_loop(0, piece // block, add, 0)

    small_names = ("core", "x", "y", "z")

    def small_copies(s):
        size, me, device = dims[small_names[s]]
        return [
            pltpu.make_async_remote_copy(
                src_ref=small_sum.at[s],
                dst_ref=small_slots.at[s, me],
                send_sem=small_send.at[s, step - 1],
                recv_sem=small_recv.at[s, size - step - 1],
                device_id=device((me + step) % size),
                device_id_type=MESH,
            )
            for step in range(1, size)
        ]

    started = {}

    def begin(key, copies):
        for copy in copies:
            copy.start()
        started[key] = copies

    def finish(key):
        for copy in started.pop(key):
            copy.wait()

    saves = []
    reached = [0] * (chunks + 1)

    def advance(c):
        s = reached[c]
        reached[c] += 1
        if c == chunks:
            if s == 0:
                small_sum[0] = small_value[0]
            else:
                finish(("small", s - 1))
                size, me, _ = dims[small_names[s - 1]]
                small_slots[s - 1, me] = small_sum[s - 1]
                value = small_slots[s - 1, 0]
                for i in range(1, size):
                    value = value + small_slots[s - 1, i]
                small_sum[s] = value
            if s < len(small_names):
                begin(("small", s), small_copies(s))
            return
        stages = len(orders[c])
        if s > 0:
            finish((c, s - 1))
        if 1 <= s <= stages:
            add_arrived(c, s - 1)
        if s < stages:
            begin((c, s), reduce_copies(c, s))
        elif s < 2 * stages:
            begin((c, s), spread_copies(c, 2 * stages - s))
        else:
            part = pl.ds(c * rows, rows)
            copy = pltpu.make_async_copy(gathered.at[part], out.at[part], save.at[c])
            copy.start()
            saves.append(copy)

    def row_block(full, device):
        return full.at[:, pl.ds(pl.multiple_of(device * length, length), length)]

    def row_copies(which, fulls, far):
        copies = []
        y_size, y_me, y_device = dims["y"]
        _, core_me, core_device = dims["core"]
        for a, full in enumerate(fulls):
            if not far:
                for step in range(1, y_size):
                    copies.append((full, place, y_device((y_me + step) % y_size), which, a, step - 1, y_size - step - 1))
                copies.append((full, place, core_device(1 - core_me), which, a, y_size - 1, y_size - 1))
            else:
                for step in range(1, y_size):
                    copies.append((full, (y_me - step + y_size) % y_size * 2 + core_me, core_device(1 - core_me), which, a,
                                   y_size - 1 + step, y_size - 1 + step))
        return [
            pltpu.make_async_remote_copy(
                src_ref=row_block(full, block), dst_ref=row_block(full, block), send_sem=row_send.at[w, a, i],
                recv_sem=row_recv.at[w, a, j], device_id=device, device_id_type=MESH)
            for full, block, device, w, a, i, j in copies
        ]

    def put_row(row, value):
        small_value[0] = jnp.where(lax.broadcasted_iota(jnp.int32, small.shape, 0) == row, value, small_value[0])

    def total(value):
        return jnp.sum(value.astype(F32), axis=0, keepdims=True)

    def rowwise(ref):
        return ref[...].reshape(flat, ref.shape[2])

    def cross_query_grads(group):
        def step(r, carry):
            def put(cs, value):
                dcq[r, :, cs] = value.astype(BF)

            attn_step(False, r, group, mask.shape[1] // length, None, cq_full, gc_full, caux_full, mask, cross_key,
                      cross_value, mine, slice(None), put)
            return carry

        lax.fori_loop(0, batch, step, 0)

    def attn_step(dkv, r, group, blocks, seen, a, b, aq, ak, k, v, query_at, key_at, put):
        def loader(ref, at):
            return lambda cs: ref[r, at, cs]

        row_grads(dkv, range(group * GROUP, group * GROUP + GROUP), length, blocks, length, seen, loader(a, query_at),
                  loader(b, query_at), aq[r, query_at], ak[r, key_at], loader(k, key_at), loader(v, key_at), put)

    def cross_key_grads(group):
        def step(r, carry):
            def put(cs, keys_grad, values_grad):
                at = cs.start
                pair[r, :, at : at + 128] = keys_grad.astype(BF)
                pair[r, :, width + at : width + at + 128] = values_grad.astype(BF)

            attn_step(True, r, group, queries.shape[1] // length, None, cq_full, gc_full, caux_full, mask, cross_key,
                      cross_value, slice(None), mine, put)
            return carry

        lax.fori_loop(0, batch, step, 0)

    def causal(dkv):
        down = lax.broadcasted_iota(jnp.int32, (length, length), 0)
        along = lax.broadcasted_iota(jnp.int32, (length, length), 1)
        return down <= along if dkv else along <= down

    def self_query_grads(group):
        def step(r, carry):
            def put(cs, value):
                at = cs.start
                joined[r, :, at : at + 128] = value.astype(BF)

            for blocks in range(1, seq_size + 1):

                @pl.when(place == blocks - 1)
                def _(blocks=blocks):
                    attn_step(False, r, group, blocks, causal(False), queries, ga_full, saux_full, mask, keys, values,
                              pl.ds((blocks - 1) * length, length), pl.ds(0, blocks * length), put)

            return carry

        lax.fori_loop(0, batch, step, 0)

    def self_key_grads(group):
        def step(r, carry):
            def put(cs, keys_grad, values_grad):
                at = cs.start
                joined[r, :, width + at : width + at + 128] = keys_grad.astype(BF)
                joined[r, :, 2 * width + at : 2 * width + at + 128] = values_grad.astype(BF)

            for blocks in range(1, seq_size + 1):

                @pl.when(place == seq_size - blocks)
                def _(blocks=blocks):
                    first = (seq_size - blocks) * length
                    attn_step(True, r, group, blocks, causal(True), queries, ga_full, saux_full, mask, keys, values,
                              pl.ds(first, blocks * length), pl.ds(first, length), put)

            return carry

        lax.fori_loop(0, batch, step, 0)

    def put_block(block, value):
        own[pl.ds((block - half_rows // width) * width, width)] = value.astype(BF)

    def middle():
        query_grad = rowwise(dcq)
        put_block(9, dot_tn(rowwise(self_low), query_grad))
        put_row(9, total(query_grad))
        grad = rowwise(grad_mid) + dot_nt(query_grad, cross_q[...])
        u, v = rowwise(unit), rowwise(root)
        put_row(0, total(grad * u))
        put_row(3, total(grad))
        scaled = grad * gain[...]
        start = v * (scaled - jnp.mean(scaled, axis=-1, keepdims=True) - u * jnp.mean(scaled * u, axis=-1, keepdims=True))
        grad_mid[...] = start.reshape(batch, length, width)
        branch = start.astype(BF)
        put_row(8, total(branch))
        mixed = rowwise(attended)
        grad_mixed = dot_nt(branch, self_out[...]).astype(BF)
        ga_full[:, mine] = grad_mixed.reshape(batch, length, width)
        saux = rowwise(self_aux).astype(F32) + head_inner(grad_mixed, mixed)
        saux_full[:, mine] = saux.astype(BF).reshape(batch, length, 128)
        begin("self", row_copies(1, (ga_full, saux_full), False))
        put_block(10, dot_tn(mixed, branch))

    def cross_weights():
        both = rowwise(pair)
        grad = dot_tn(rowwise(memory), both)
        put_block(11, grad[:, :width])
        put_block(12, grad[:, width:])
        put_row(10, total(both[:, width:]))
        grad_memory[...] = dot_nt(both, cross_kv[...]).astype(BF).reshape(batch, length, width)

    def query_weights():
        grads = joined[:, :, :width].reshape(flat, width)
        put_block(13, dot_tn(rowwise(tokens), grads))
        put_row(6, total(grads))

    def self_weights():
        grads = joined[:, :, width:].reshape(flat, 2 * width)
        grad = dot_tn(rowwise(tokens), grads)
        put_block(14, grad[:, :width])
        put_block(15, grad[:, width:])
        put_row(7, total(grads[:, width:]))

    def last():
        grads = rowwise(joined)
        grad_tokens[...] = (rowwise(grad_mid) + dot_nt(grads, self_qkv[...])).astype(BF).reshape(batch, length, width)

    def relay(key, which, fulls):
        def run():
            finish(key)
            begin(key, row_copies(which, fulls, True))

        return run

    groups = range(heads // GROUP)
    begin("cross", row_copies(0, (gc_full, caux_full), False))
    loaded(0)()
    steps = [functools.partial(cross_query_grads, g) for g in groups]
    steps += [middle]
    steps += [functools.partial(cross_key_grads, g) for g in groups]
    steps += [cross_weights]
    steps += [functools.partial(self_query_grads, g) for g in groups]
    steps += [query_weights]
    steps += [functools.partial(self_key_grads, g) for g in groups]
    steps += [self_weights, last]
    n = len(groups)
    before = {0: [loaded(1, 2, 3, 12)], n: [loaded(4, 5, 6, 7, 8, 9), relay("cross", 0, (gc_full, caux_full))], n + 1: [functools.partial(finish, "cross")],
              2 * n + 1: [load_later, loaded(10, 11), relay("self", 1, (ga_full, saux_full))], 2 * n + 2: [loaded(13, 14, 15)],
              3 * n + 2: [loaded(16, 17)], 3 * n + 3: [functools.partial(finish, "self")]}
    todo = list(enumerate(steps))
    for action in sequence:
        if action < 0:
            i, step = todo.pop(0)
            for extra in before.get(i, ()):
                extra()
            step()
        else:
            advance(action)
    small_out[...] = small_sum[len(small_names)]
    for copy in saves:
        copy.wait()


def back_and_sum(mesh_shape, heads, operands):
    dp_size, seq_size = mesh_shape["dp"], mesh_shape["seq"]
    sizes = exchange_sizes(dp_size, seq_size)
    (cross_out_grad, small, nearby, away) = operands
    ffn_grads = away[0]
    columns = ffn_grads.shape[1]
    total_rows = 2 * ffn_grads.shape[0]
    batch, length, width = nearby[0].shape
    per_device = 1
    for name in ("core", "y", "x", "z"):
        per_device *= sizes[name]
    chunks = min(16, total_rows // (16 * per_device))
    orders, sequence = plan(chunks)
    most = max(sizes.values())
    scratch = []
    for order in orders:
        extent = total_rows // chunks
        for name in order:
            extent //= sizes[name]
            scratch.append(pltpu.VMEM((sizes[name] - 1, extent, columns), BF))
    full = seq_size * length
    scratch += [
        pltpu.VMEM((total_rows // 2, columns), BF),
        pltpu.VMEM((total_rows, columns), BF),
        pltpu.VMEM((4, most) + small.shape, F32),
        pltpu.VMEM((5,) + small.shape, F32),
        pltpu.VMEM((batch, full, width), BF),
        pltpu.VMEM((batch, full, 128), BF),
        pltpu.VMEM((batch, full, width), BF),
        pltpu.VMEM((batch, full, 128), BF),
        pltpu.VMEM((batch, length, width), BF),
        pltpu.VMEM((batch, length, 2 * width), BF),
        pltpu.VMEM((batch, length, 3 * width), BF),
        pltpu.SemaphoreType.DMA((chunks, 10, most - 1)),
        pltpu.SemaphoreType.DMA((chunks, 10, most - 1)),
        pltpu.SemaphoreType.DMA((4, most - 1)),
        pltpu.SemaphoreType.DMA((4, most - 1)),
        pltpu.SemaphoreType.DMA((chunks,)),
        pltpu.SemaphoreType.DMA((2, 2, seq_size)),
        pltpu.SemaphoreType.DMA((2, 2, seq_size)),
        pltpu.SemaphoreType.DMA((3,)),
        pltpu.SemaphoreType.DMA((len(away),)),
    ] + [pltpu.VMEM(value.shape, value.dtype) for i, value in enumerate(away) if i not in (13, 14)]
    anywhere = pl.BlockSpec(memory_space=pl.ANY)

    def kernel(*refs):
        ends = 2 + len(nearby)
        back_kernel(dp_size, seq_size, chunks, orders, sequence, *refs[:ends],
                    refs[ends : ends + len(away)], *refs[ends + len(away) :])

    return pl.pallas_call(
        kernel,
        out_shape=(
            jax.ShapeDtypeStruct((total_rows, columns), BF),
            jax.ShapeDtypeStruct(small.shape, F32),
            jax.ShapeDtypeStruct((batch, length, width), BF),
            jax.ShapeDtypeStruct((batch, length, width), BF),
        ),
        in_specs=[anywhere, VM] + [anywhere] * 2 + [VM] * (len(nearby) - 2) + [anywhere] * len(away),
        out_specs=(anywhere, VM, VM, VM),
        scratch_shapes=scratch,
        name="backward_and_sums",
        compiler_params=pltpu.CompilerParams(collective_id=0, has_side_effects=True, vmem_limit_bytes=62 << 20),
    )(cross_out_grad, small, *nearby, *away)

SOURCE = 56


def row_mix(heads, tq, blocks, width, seen, q, aq, k, v, ak, put):
    state = {"aux": aq.astype(F32)}
    low = lanes((tq, 128)) < HALF

    def columns(h):
        return slice(h // 2 * 128, h // 2 * 128 + 128)

    def first(h):
        even = h % 2 == 0
        return dot_nt(pick(even, q(columns(h)) * jnp.asarray(SCORE_SCALE, BF), aq), pick(even, k(columns(h)), ak))

    def rest(h, scores):
        values = v(columns(h))
        if seen is not None:
            tail = jnp.where(seen, scores[:, (blocks - 1) * width :], -BIG)
            scores = tail if blocks == 1 else jnp.concatenate([scores[:, : (blocks - 1) * width], tail], axis=1)
        peak = jnp.max(scores, axis=1, keepdims=True)
        weights = jnp.exp(scores - peak).astype(BF)
        mixed = dot_nn(weights, pick(h % 2 == 0, values, jnp.ones_like(values)))
        at = HALF if h % 2 == 0 else 0
        state["aux"] = put_parts(state["aux"], peak + jnp.log(mixed[:, at : at + 1]), LSE + 3 * h)
        if h % 2 == 0:
            state["even"] = mixed
        else:
            total = pltpu.roll(jnp.where(low, mixed, state["even"]), HALF, 1)
            put(columns(h), jnp.where(low, state["even"], mixed) / total)

    schedule(heads, 1, first, rest)
    return state["aux"].astype(BF)


def norm_rows(residual, gain, shift):
    centred = residual - jnp.mean(residual, axis=-1, keepdims=True)
    inverse = lax.rsqrt(jnp.mean(centred * centred, axis=-1, keepdims=True) + EPSILON)
    unit = centred * inverse
    return unit * gain + shift, unit, inverse


def norm_rows_back(grad, unit, inverse, gain):
    scaled = grad * gain
    return inverse * (scaled - jnp.mean(scaled, axis=-1, keepdims=True) - unit * jnp.mean(scaled * unit, axis=-1, keepdims=True))


def front_kernel(dp_size, seq_size, self_mask, cross_mask, mask_local, gains, biases, hidden_bias, tokens, memory, cotangent, *refs):
    weights_away, refs = refs[:7], refs[7:]
    (output, small, *away_outs, root_out), refs = refs[:19], refs[19:]
    kept, refs = refs[:16], refs[16:]
    (ffn_grads, cross_out_grad, mask, queries, keys, values, cross_key, cross_value, cq_full, attended, self_aux, self_low, unit,
     grad_mid, grad_crossed, cross_aux) = kept
    (tokens_full, memory_full, self_qkv, self_out, cross_q, cross_kv, cross_out, ffn_in, ffn_out, cot, after_self, crossed, hidden,
     slope, row_send, row_recv, load_sem, save_sem) = refs
    here_weights = (self_qkv, self_out, cross_q, cross_kv, cross_out, ffn_in, ffn_out)
    dims = dimensions(dp_size, seq_size)
    place = lax.axis_index("seq")
    batch, length, width = attended.shape
    heads = width // HALF
    flat = batch * length
    base = pl.multiple_of(place * length, length)
    mine = pl.ds(base, length)

    y_size, y_me, y_device = dims["y"]
    _, core_me, core_device = dims["core"]
    barrier = pltpu.get_barrier_semaphore()
    targets = [y_device((y_me + step) % y_size) for step in range(1, y_size)] + [core_device(1 - core_me)]
    for device in targets:
        pl.semaphore_signal(barrier, inc=1, device_id=device, device_id_type=MESH)

    loads = []

    def load(away, here):
        copy = pltpu.make_async_copy(away, here, load_sem.at[len(loads)])
        copy.start()
        loads.append(copy)
        return len(loads) - 1

    load(tokens, tokens_full.at[:, mine])
    load(memory, memory_full.at[:, mine])
    for away, here in zip(weights_away, here_weights):
        load(away, here)
    load(cotangent, cot)
    mask[:, mine] = mask_local[...]
    pl.semaphore_wait(barrier, len(targets))

    def row_block(full, block):
        return full.at[:, pl.ds(pl.multiple_of(block * length, length), length)]

    started = {}

    def send(key, which, fulls, kind):
        copies = []
        for a, full in enumerate(fulls):
            if kind == "y":
                todo = [(place, y_device((y_me + step) % y_size), step - 1, y_size - step - 1) for step in range(1, y_size)]
            elif kind == "core":
                todo = [(place, core_device(1 - core_me), y_size - 1, y_size - 1)]
            else:
                todo = [((y_me - step + y_size) % y_size * 2 + core_me, core_device(1 - core_me), y_size - 1 + step, y_size - 1 + step)
                        for step in range(1, y_size)]
            for block, device, i, j in todo:
                copies.append(pltpu.make_async_remote_copy(
                    src_ref=row_block(full, block), dst_ref=row_block(full, block), send_sem=row_send.at[which, a, i],
                    recv_sem=row_recv.at[which, a, j], device_id=device, device_id_type=MESH))
        for copy in copies:
            copy.start()
        started[key] = copies

    def finish(key):
        for copy in started.pop(key):
            copy.wait()

    saves = []

    def save(*which):
        for i in which:
            copy = pltpu.make_async_copy(kept[i], away_outs[i], save_sem.at[i])
            copy.start()
            saves.append(copy)

    def total(value):
        return jnp.sum(value.astype(F32), axis=0, keepdims=True)

    def rowwise(ref):
        return ref[...].reshape(flat, ref.shape[2])

    small_rows = {}
    gain, shift = [gains[i : i + 1] for i in range(3)], [biases[i : i + 1] for i in range(3)]
    bias = lambda i: biases[i : i + 1]

    loads[0].wait()
    send("tokens y", 0, (tokens_full, mask), "y")
    send("tokens core", 0, (tokens_full, mask), "core")
    loads[1].wait()
    send("memory y", 1, (memory_full,), "y")
    send("memory core", 1, (memory_full,), "core")

    def project_block(block):
        at = pl.ds(pl.multiple_of(block * length, length), length)
        rows = tokens_full[:, at].reshape(flat, width)
        for i, (ref, extra) in enumerate(((queries, bias(3)), (keys, None), (values, bias(4)))):
            value = dot_nn(rows, self_qkv[:, i * width : (i + 1) * width])
            if extra is not None:
                value = value + extra
            ref[:, at] = value.astype(BF).reshape(batch, length, width)

    loads[2].wait()
    project_block(place)
    finish("tokens core")
    project_block(place + 1 - 2 * core_me)
    finish("tokens y")
    send("tokens relay", 0, (tokens_full, mask), "relay")
    for step in range(1, y_size):
        project_block((y_me - step + y_size) % y_size * 2 + core_me)
    finish("tokens relay")
    for step in range(1, y_size):
        project_block((y_me - step + y_size) % y_size * 2 + 1 - core_me)
    save(2, 3, 4, 5)

    down = lax.broadcasted_iota(jnp.int32, (length, length), 0)
    along = lax.broadcasted_iota(jnp.int32, (length, length), 1)
    for blocks in range(1, seq_size + 1):

        @pl.when(place == blocks - 1)
        def _(blocks=blocks):
            def row(r, carry):
                at, span = pl.ds((blocks - 1) * length, length), pl.ds(0, blocks * length)

                def put(cs, value):
                    attended[r, :, cs] = value.astype(BF)

                self_aux[r] = row_mix(heads, length, blocks, length, along <= down, lambda cs: queries[r, at, cs], self_mask[r],
                                      lambda cs: keys[r, span, cs], lambda cs: values[r, span, cs], mask[r, span], put)
                return carry

            lax.fori_loop(0, batch, row, 0)

    for i in (3, 4):
        loads[i].wait()
    state, unit_first, root_first = norm_rows(
        tokens_full[:, mine].reshape(flat, width).astype(F32) + dot_nn(rowwise(attended), self_out[...]) + bias(5), gain[0], shift[0]
    )
    after_self[...] = state
    unit[...] = unit_first.reshape(batch, length, width)
    root_out[...] = root_first.reshape(batch, length, 1)
    self_low[...] = state.astype(BF).reshape(batch, length, width)
    query = (dot_nn(state.astype(BF), cross_q[...]) + bias(6)).astype(BF)
    cq_full[:, mine] = query.reshape(batch, length, width)
    finish("memory core")
    finish("memory y")
    send("memory relay", 1, (memory_full,), "relay")
    send("query y", 2, (cq_full,), "y")
    send("query core", 2, (cq_full,), "core")
    save(9, 10, 11, 12)
    loads[5].wait()

    def project_memory(block):
        at = pl.ds(pl.multiple_of(block * length, length), length)
        rows = memory_full[:, at].reshape(flat, width)
        cross_key[:, at] = dot_nn(rows, cross_kv[:, :width]).astype(BF).reshape(batch, length, width)
        cross_value[:, at] = (dot_nn(rows, cross_kv[:, width:]) + bias(7)).astype(BF).reshape(batch, length, width)

    project_memory(place)
    project_memory(place + 1 - 2 * core_me)
    for step in range(1, y_size):
        project_memory((y_me - step + y_size) % y_size * 2 + core_me)
    finish("memory relay")
    for step in range(1, y_size):
        project_memory((y_me - step + y_size) % y_size * 2 + 1 - core_me)
    save(6, 7)

    def cross_row(r, carry):
        def put(cs, value):
            crossed[r, :, cs] = value.astype(BF)

        cross_aux[r] = row_mix(heads, length, seq_size, length, None, lambda cs: cq_full[r, mine, cs], cross_mask[r],
                               lambda cs: cross_key[r, :, cs], lambda cs: cross_value[r, :, cs], mask[r], put)
        return carry

    lax.fori_loop(0, batch, cross_row, 0)
    for i in range(6, 10):
        loads[i].wait()
    after_cross, unit_second, root_second = norm_rows(after_self[...] + dot_nn(rowwise(crossed), cross_out[...]) + bias(8), gain[1],
                                                      shift[1])
    finish("query core")
    finish("query y")
    send("query relay", 2, (cq_full,), "relay")
    cross_low = after_cross.astype(BF)
    parts = ffn_in.shape[1] // width
    summed = after_cross + bias(9)
    for j in range(parts):
        cs = slice(j * width, (j + 1) * width)
        before = dot_nn(cross_low, ffn_in[:, cs]) + hidden_bias[:, cs]
        share = 0.5 * (1.0 + lax.erf(before * ROOT_HALF))
        slope[:, cs] = share + before * NORMAL_DENSITY * jnp.exp(-0.5 * before * before)
        value = (before * share).astype(BF)
        hidden[:, cs] = value
        summed = summed + dot_nn(value, ffn_out[cs])
    result, unit_third, root_third = norm_rows(summed, gain[2], shift[2])
    output[...] = result.astype(BF).reshape(batch, length, width)
    grad = rowwise(cot).astype(F32)
    small_rows[2], small_rows[5] = total(grad * unit_third), total(grad)
    grad_third = norm_rows_back(grad, unit_third, root_third, gain[2])
    branch = grad_third.astype(BF)
    small_rows[12] = total(branch)
    grad_second = grad_third
    for j in range(parts):
        cs = slice(j * width, (j + 1) * width)
        ffn_grads[pl.ds((parts + j) * width, width)] = dot_tn(hidden[:, cs], branch).astype(BF)
        grad_hidden = (dot_nt(branch, ffn_out[cs]) * slope[:, cs]).astype(BF)
        small_rows[13 + j] = total(grad_hidden)
        ffn_grads[pl.ds(j * width, width)] = dot_tn(cross_low, grad_hidden).astype(BF)
        grad_second = grad_second + dot_nt(grad_hidden, ffn_in[:, cs])
    save(0)
    finish("query relay")
    save(8)
    small_rows[1], small_rows[4] = total(grad_second * unit_second), total(grad_second)
    middle = norm_rows_back(grad_second, unit_second, root_second, gain[1])
    grad_mid[...] = middle.reshape(batch, length, width)
    branch = middle.astype(BF)
    small_rows[11] = total(branch)
    mixed = rowwise(crossed)
    grad_mixed = dot_nt(branch, cross_out[...]).astype(BF)
    grad_crossed[...] = grad_mixed.reshape(batch, length, width)
    aux = rowwise(cross_aux).astype(F32) + head_inner(grad_mixed, mixed)
    cross_aux[...] = aux.astype(BF).reshape(batch, length, 128)
    cross_out_grad[...] = dot_tn(mixed, branch).astype(BF)
    save(1, 13, 14, 15)
    small[...] = jnp.zeros(small.shape, F32)
    for row, value in small_rows.items():
        small[row : row + 1] = value
    for copy in saves:
        copy.wait()


def front(mesh_shape, self_mask, cross_mask, mask_local, gains, biases, hidden_bias, tokens, memory, cotangent, weights):
    dp_size, seq_size = mesh_shape["dp"], mesh_shape["seq"]
    batch, length, width = tokens.shape
    hidden = weights[5].shape[1]
    flat, full = batch * length, seq_size * length
    anywhere = pl.BlockSpec(memory_space=pl.ANY)
    whole, part, narrow = (batch, full, width), (batch, length, width), (batch, length, 128)
    saved = [((2 * hidden, width), BF), ((width, width), BF), ((batch, full, 128), BF)] + [(whole, BF)] * 6
    saved += [(part, BF), (narrow, BF), (part, BF), (part, F32), (part, F32), (part, BF), (narrow, BF)]
    out_shape = [(part, BF), ((24, width), F32)] + saved + [((batch, length, 1), F32)]
    scratch = [pltpu.VMEM(shape, kind) for shape, kind in saved]
    scratch += [pltpu.VMEM(whole, BF)] * 2 + [pltpu.VMEM(value.shape, BF) for value in weights]
    scratch += [
        pltpu.VMEM(part, BF),
        pltpu.VMEM((flat, width), F32),
        pltpu.VMEM(part, BF),
        pltpu.VMEM((flat, hidden), BF),
        pltpu.VMEM((flat, hidden), F32),
        pltpu.SemaphoreType.DMA((3, 2, seq_size)),
        pltpu.SemaphoreType.DMA((3, 2, seq_size)),
        pltpu.SemaphoreType.DMA((10,)),
        pltpu.SemaphoreType.DMA((len(saved),)),
    ]
    return pl.pallas_call(
        functools.partial(front_kernel, dp_size, seq_size),
        out_shape=tuple(jax.ShapeDtypeStruct(shape, kind) for shape, kind in out_shape),
        in_specs=[VM] * 6 + [anywhere] * 10,
        out_specs=(VM, VM) + (anywhere,) * len(saved) + (VM,),
        scratch_shapes=scratch,
        name="forward_and_feed_forward",
        compiler_params=pltpu.CompilerParams(collective_id=1, has_side_effects=True, vmem_limit_bytes=62 << 20),
    )(self_mask, cross_mask, mask_local, gains, biases, hidden_bias, tokens, memory, cotangent, *weights)


def shards(mesh_shape, tokens, memory, segment_ids, source_ids, source_lengths, cotangent, self_qkv, self_out, cross_q, cross_kv,
           cross_out, ffn_in, ffn_out, norm_gains, bias_rows, hidden_bias):
    length = tokens.shape[1]
    place = lax.axis_index("seq") * length + jnp.arange(length, dtype=jnp.int32)
    lane = jnp.arange(128) % HALF
    usable = (place[None] < source_lengths[:, None])[..., None]
    segments, sources = segment_ids[..., None], source_ids[..., None]
    self_mask = jnp.where(segments == lane, 1.0, 0.0).astype(BF)
    cross_mask = jnp.where(segments == lane - SOURCE, 1.0, 0.0).astype(BF)
    other = jnp.where(lane < 8, segments != lane, (lane >= SOURCE) & ~((sources == lane - SOURCE) & usable))
    mask = jnp.where(other, -BIG, 0.0).astype(BF)
    (output, small, ffn_grads, cross_out_grad, mask_full, queries, keys, values, cross_key, cross_value, cross_query, attended, self_aux,
     self_low, unit, grad_mid, grad_crossed, cross_aux, root) = front(
        mesh_shape, self_mask, cross_mask, mask, norm_gains, bias_rows, hidden_bias.reshape(1, -1), tokens, memory, cotangent,
        (self_qkv, self_out, cross_q, cross_kv, cross_out, ffn_in, ffn_out),
    )
    summed, small, grad_tokens, grad_memory = back_and_sum(
        mesh_shape, HEADS,
        (
            cross_out_grad, small,
            (grad_crossed, cross_aux, self_aux, root, norm_gains[:1]),
            (ffn_grads, cross_key, cross_value, mask_full, self_low, unit, grad_mid, cross_q, self_out, attended, memory,
             cross_kv, cross_query, queries, keys, values, tokens, self_qkv),
        ),
    )

    def block(first, count):
        return jnp.concatenate([summed[512 * (first + i) : 512 * (first + i) + 512] for i in range(count)], axis=1).astype(F32)

    return (
        output, grad_tokens, grad_memory, block(13, 3), block(10, 1), block(9, 1), block(11, 2), block(8, 1), block(0, 4),
        summed[2048:4096].astype(F32), small[:3], small[3:13], small[13:17].reshape(2048),
    )


def solution(mesh):
    placed = (
        P("dp", "seq", None),
        P("dp", "seq", None),
        P("dp", "seq"),
        P("dp", "seq"),
        P("dp"),
        P("dp", "seq", None),
        P(),
        P(),
        P(),
        P(),
        P(),
        P(),
        P(),
        P(),
        P(),
        P(),
    )
    return jax.shard_map(
        functools.partial(shards, dict(mesh.shape)),
        mesh=mesh,
        in_specs=placed,
        out_specs=(
            P("dp", "seq", None),
            P("dp", "seq", None),
            P("dp", "seq", None),
            P(),
            P(),
            P(),
            P(),
            P(),
            P(),
            P(),
            P(),
            P(),
            P(),
        ),
        check_vma=False,
    )
```

```python
import functools

import jax
import jax.numpy as jnp
from jax import lax
from jax.experimental import pallas as pl
from jax.experimental.pallas import tpu as pltpu
from jax.sharding import PartitionSpec as P

HEADS = 8
SCORE_SCALE = 0.125
EPSILON = 1e-05
ROOT_HALF = 0.7071067811865476
NORMAL_DENSITY = 0.3989422804014327

BIG=float(2.0**30)
HALF=64
LSE=8; DELTA=32
NT=(((1,),(1,)),((),()))
F32=jnp.float32; BF=jnp.bfloat16
def lanes(shape): return lax.broadcasted_iota(jnp.int32,shape,len(shape)-1)
def pick(even, mine, aux):
    low=lanes(mine.shape)<HALF
    return jnp.where(low,mine,aux) if even else jnp.where(low,aux,mine)
def dot_nt(a,b): return lax.dot_general(a,b,NT,preferred_element_type=F32)
def dot_nn(a,b): return jnp.dot(a,b,preferred_element_type=F32)
def put_parts(aux,x,at):
    lane=lanes(aux.shape)%HALF
    hi=x.astype(BF).astype(F32); r=x-hi; mid=r.astype(BF).astype(F32)
    return jnp.where(lane==at,hi,jnp.where(lane==at+1,mid,jnp.where(lane==at+2,r-mid,aux)))
def row_const(shape,at,n):
    lane=lanes(shape)%HALF
    return (lane>=at)&(lane<at+n)
def schedule(heads,ahead,first,rest):
    heads=list(heads) if not isinstance(heads,int) else list(range(heads))
    kept={}
    for h in heads[:ahead]: kept[h]=first(h)
    for i,h in enumerate(heads):
        if i+ahead<len(heads): kept[heads[i+ahead]]=first(heads[i+ahead])
        rest(h,kept.pop(h))


VM = pl.BlockSpec(memory_space=pltpu.VMEM)

MESH = pl.DeviceIdType.MESH


def dimensions(dp_size, seq_size):
    dp, seq = lax.axis_index("dp"), lax.axis_index("seq")
    return {
        "core": (2, seq % 2, lambda i: (dp, seq - seq % 2 + i)),
        "y": (seq_size // 2, seq // 2, lambda i: (dp, i * 2 + seq % 2)),
        "x": (2, dp % 2, lambda i: (dp - dp % 2 + i, seq)),
        "z": (dp_size // 2, dp // 2, lambda i: (i * 2 + dp % 2, seq)),
        "near": (2, dp // 2 % 2, lambda i: (dp + (i - dp // 2 % 2) * 2, seq)),
        "far": (dp_size // 4, dp // 4, lambda i: (i * 4 + dp % 4, seq)),
    }


def plan(chunks, rows, columns):
    if chunks != 16:
        pieces = [(c * (rows // chunks), rows // chunks, 0, columns) for c in range(chunks)]
        orders = [("core", "x", "y", "z"), ("core", "y", "x", "z")] * (chunks // 2)
        waiting = [0] * (chunks // 2) + [20] * (chunks - chunks // 2)
        sequence = []
        for slot in range(21):
            sequence += [c for c in range(chunks) if waiting[c] <= slot < waiting[c] + 9]
            sequence.append(-1)
        sequence += [c for _ in range(8) for c in range(chunks) if waiting[c] == 20]
        return pieces, orders, sequence + [chunks] * 5
    half = columns // 2
    pieces = [(columns * block, columns, first * half, taken * half) for block, first, taken in [(0, 0, 2), (1, 0, 2), (2, 0, 2), (3, 0, 2), (4, 0, 2), (5, 0, 2), (6, 0, 2), (7, 0, 2), (8, 0, 2), (9, 0, 2), (10, 0, 2), (11, 0, 2), (12, 0, 2), (14, 0, 2), (15, 0, 2), (13, 0, 1), (13, 1, 1)]]
    kinds = (
        ('core', 'near', 'x', 'far', 'y'),
        ('core', 'x', 'near', 'y', 'far'),
        ('core', 'x', 'near', 'far', 'y'),
        ('core', 'y', 'x', 'z'),
        ('core', 'near', 'far', 'x', 'y'),
        ('core', 'near', 'x', 'y', 'far'),
        ('core', 'x', 'y', 'z'),
    )
    orders = [kinds[i] for i in (0, 0, 1, 2, 3, 2, 4, 5, 0, 2, 6, 0, 6, 6, 3, 3, 6)]
    sequence = [0, 1, 7, 4, 2, 3, 8, 5, 6, -1, -1, -1, 0, 1, 7, 4, 2, 3, 8, 5, 6, -1, -1, 4, 2, 0, 3, 10, 9, 5, -1, 1, 7, 10, 8, 9, 4, 6, 0, -1, 2, 3, 5, -1, 4, -1, 0, 1, 7, 2, 8, -1, 0, 1, 7, 4, 11, 2, 3, 12, 10, 8, 9, 5, 6, -1, 0, 1, 7, 11, 2, 3, 12, 4, 8, 9, 5, 6, -1, 1, 10, -1, 0, 7, 2, 3, 12, 8, 9, 5, 6, -1, 1, 4, 0, 10, -1, 7, 4, 11, 12, 9, 6, 1, -1, 2, 3, 8, 9, 10, 5, -1, 14, 7, 13, 6, -1, 11, 12, 10, -1, 14, 13, 2, 8, 9, -1, 16, 15, 17, -1, 2, 10, 0, 16, 15, 14, 3, 13, 5, 11, 10, 0, 17, 15, 12, 11, 6, 16, 1, 13, 9, 11, 1, 14, 15, 17, 16, 12, 7, 7, 13, 3, 11, 15, 16, 5, 8, 14, 17, 3, 5, 8, 9, 15, 16, 6, 13, 12, 11, 14, 9, 17, 15, 16, 6, 12, 13, 14, 11, 15, 16, 15, 11, 16, 13, 14, 13, 14]
    return pieces, orders, sequence


def exchange_sizes(dp_size, seq_size):
    return {"core": 2, "y": seq_size // 2, "x": 2, "z": dp_size // 2, "near": 2, "far": dp_size // 4}


def row_grads(dkv, heads, tq, blocks, width, seen, a, b, aq, ak, k, v, put):
    state = {}
    minus = jnp.asarray(-1.0, BF)
    edge = (slice(None), slice(0, width)) if dkv else (slice(None), slice((blocks - 1) * width, blocks * width))

    def columns(h):
        return slice(h // 2 * 128, h // 2 * 128 + 128)

    def first(h):
        e, cs = h % 2 == 0, columns(h)
        keys, values = k(cs), v(cs)
        ka = pick(e, keys, jnp.where(row_const(keys.shape, LSE + 3 * h, 3), minus, ak))
        va = pick(e, values, jnp.where(row_const(values.shape, DELTA + 3 * h, 3), minus, jnp.zeros_like(values)))
        qa, ga = pick(e, a(cs) * jnp.asarray(SCORE_SCALE, BF), aq), pick(e, b(cs), aq)
        return (dot_nt(ka, qa), dot_nt(va, ga)) if dkv else (dot_nt(qa, ka), dot_nt(ga, va))

    def rest(h, pair):
        scores, grads = pair
        cs = columns(h)
        if seen is not None:
            masked = jnp.where(seen, scores[edge], -BIG)
            if blocks == 1:
                scores = masked
            elif dkv:
                scores = jnp.concatenate([masked, scores[:, width:]], axis=1)
            else:
                scores = jnp.concatenate([scores[:, : (blocks - 1) * width], masked], axis=1)
        weights = jnp.exp(scores)
        grad_scores = (weights * grads).astype(BF)
        low = lanes((tq, 128)) < HALF
        if dkv:
            values_grad = dot_nn(weights.astype(BF), b(cs))
            keys_grad = dot_nn(grad_scores, a(cs))
            if h % 2 == 0:
                state["k"], state["v"] = keys_grad, values_grad
            else:
                put(cs, SCORE_SCALE * jnp.where(low, state["k"], keys_grad), jnp.where(low, state["v"], values_grad))
        else:
            query_grad = dot_nn(grad_scores, k(cs))
            if h % 2 == 0:
                state["q"] = query_grad
            else:
                put(cs, SCORE_SCALE * jnp.where(low, state["q"], query_grad))

    schedule(heads, 1, first, rest)


TN = (((0,), (0,)), ((), ()))


def dot_tn(a, b):
    return lax.dot_general(a, b, TN, preferred_element_type=F32)


def head_inner(grad_mixed, mixed):
    product = grad_mixed.astype(F32) * mixed.astype(F32)
    lane = lax.broadcasted_iota(jnp.int32, (product.shape[1], 128), 1) % HALF
    head = lax.broadcasted_iota(jnp.int32, (product.shape[1], 128), 0) // HALF
    first = DELTA + 3 * head
    chosen = jnp.where((lane >= first) & (lane < first + 3), 1.0, 0.0).astype(BF)
    high = product.astype(BF)
    rest = product - high.astype(F32)
    middle = rest.astype(BF)
    inner = dot_nn(high, chosen) + dot_nn(middle, chosen) + dot_nn((rest - middle.astype(F32)).astype(BF), chosen)
    high = inner.astype(BF).astype(F32)
    rest = inner - high
    middle = rest.astype(BF).astype(F32)
    part = (lanes(inner.shape) % HALF - DELTA + 3) % 3
    return jnp.where(part == 0, high, jnp.where(part == 1, middle, rest - middle))


GROUP = 2


def back_kernel(dp_size, seq_size, pieces, orders, sequence,
                cross_out_grad, small, grad_crossed, cross_aux, self_aux, root, gain, away_refs,
                out, small_out, grad_tokens, grad_memory, *scratch):
    dims = dimensions(dp_size, seq_size)
    held = [[None] * len(order) for order in orders]
    taken = 0
    for c, order in enumerate(orders):
        for s in range(len(order)):
            held[c][s] = scratch[taken]
            taken += 1
    (own, gathered, small_slots, small_sum, gc_full, caux_full, ga_full, saux_full, dcq, pair, joined,
     send, recv, small_send, small_recv, save, row_send, row_recv, local_sem, load_sem, *here_refs) = scratch[taken:]
    half_rows = own.shape[0]
    chunks = len(pieces)
    place = lax.axis_index("seq")
    batch, length, width = grad_crossed.shape
    heads = width // HALF
    base = pl.multiple_of(place * length, length)
    mine = pl.ds(base, length)
    flat = batch * length

    peers = [(name, step) for name in ("core", "x", "y", "z") for step in range(1, dims[name][0])]
    barrier = pltpu.get_barrier_semaphore()
    for name, step in peers:
        size, me, device = dims[name]
        pl.semaphore_signal(barrier, inc=1, device_id=device((me + step) % size), device_id_type=MESH)

    locals_ = []
    for i, (block, full) in enumerate(((grad_crossed, gc_full), (cross_aux, caux_full))):
        locals_.append(pltpu.make_async_copy(block, full.at[:, mine], local_sem.at[i]))
    locals_.append(pltpu.make_async_copy(cross_out_grad, own.at[pl.ds(0, width)], local_sem.at[2]))
    for copy in locals_:
        copy.start()
    loads = {}
    here_refs = list(here_refs)
    here_refs[13:13] = here_refs[1:3]
    for i, (away, here) in enumerate(zip(away_refs, here_refs)):
        loads[i] = pltpu.make_async_copy(away, here, load_sem.at[i])
        if i not in (13, 14):
            loads[i].start()

    def load_later():
        loads[13].start()
        loads[14].start()

    def loaded(*which):
        def run():
            for i in which:
                loads.pop(i).wait()

        return run

    (ffn_grads, cross_key, cross_value, mask, self_low, unit, grad_mid, cross_q, self_out, attended, memory, cross_kv,
     cq_full, queries, keys, values, tokens, self_qkv) = here_refs
    small_value = [small[...]]
    pl.semaphore_wait(barrier, len(peers))
    for copy in locals_:
        copy.wait()

    def span(c):
        return pl.ds(pieces[c][2], pieces[c][3])

    def source(c):
        at, rows = pieces[c][:2]
        return ffn_grads.at[pl.ds(at, rows), span(c)] if at < half_rows else own.at[pl.ds(at - half_rows, rows), span(c)]

    def current(c, s):
        return source(c) if s == 0 else held[c][s - 1].at[0]

    firsts = {}
    count = 0
    for c, order in enumerate(orders):
        for s in range(2 * len(order)):
            firsts[c, s] = count
            count += dims[order[min(s, 2 * len(order) - 1 - s)]][0] - 1

    def reduce_copies(c, s):
        size, me, device = dims[orders[c][s]]
        now = current(c, s)
        piece = now.shape[0] // size
        copies = []
        for step in range(1, size):
            other = (me + step) % size
            copies.append(
                pltpu.make_async_remote_copy(
                    src_ref=now.at[pl.ds(pl.multiple_of(other * piece, piece), piece)],
                    dst_ref=held[c][s].at[size - step - 1],
                    send_sem=send.at[c, step - 1],
                    recv_sem=recv.at[firsts[c, s] + size - step - 1],
                    device_id=device(other),
                    device_id_type=MESH,
                )
            )
        return copies

    def offset(c, s):
        at, extent = pieces[c][:2]
        for name in orders[c][:s]:
            size, me, _ = dims[name]
            extent //= size
            at = at + me * extent
        return pl.multiple_of(at, extent), extent

    def spread_copies(c, s):
        size, me, device = dims[orders[c][s - 1]]
        at, extent = offset(c, s)
        copies = []
        for step in range(1, size):
            copies.append(
                pltpu.make_async_remote_copy(
                    src_ref=gathered.at[pl.ds(at, extent), span(c)],
                    dst_ref=gathered.at[pl.ds(at, extent), span(c)],
                    send_sem=send.at[c, step - 1],
                    recv_sem=recv.at[firsts[c, 2 * len(orders[c]) - s] + size - step - 1],
                    device_id=device((me + step) % size),
                    device_id_type=MESH,
                )
            )
        return copies

    def add_arrived(c, s):
        size, me, _ = dims[orders[c][s]]
        now = current(c, s)
        piece = now.shape[0] // size
        kept = now.at[pl.ds(pl.multiple_of(me * piece, piece), piece)]
        block = min(piece, 128)
        last = s == len(orders[c]) - 1
        at = offset(c, len(orders[c]))[0] if last else 0

        def add(i, carry):
            part = pl.ds(pl.multiple_of(i * block, block), block)
            value = kept[part].astype(F32)
            for slot in range(size - 1):
                value = value + held[c][s][slot, part].astype(F32)
            if last:
                gathered[pl.ds(pl.multiple_of(at + i * block, 16), block), span(c)] = value.astype(BF)
            else:
                held[c][s][0, part] = value.astype(BF)
            return carry

        lax.fori_loop(0, piece // block, add, 0)

    small_names = ("core", "x", "y", "z")

    def small_copies(s):
        size, me, device = dims[small_names[s]]
        return [
            pltpu.make_async_remote_copy(
                src_ref=small_sum.at[s],
                dst_ref=small_slots.at[s, me],
                send_sem=small_send.at[s, step - 1],
                recv_sem=small_recv.at[s, size - step - 1],
                device_id=device((me + step) % size),
                device_id_type=MESH,
            )
            for step in range(1, size)
        ]

    started = {}

    def begin(key, copies):
        for copy in copies:
            copy.start()
        started[key] = copies

    def finish(key):
        for copy in started.pop(key):
            copy.wait()

    saves = []
    reached = [0] * (chunks + 1)

    def advance(c):
        s = reached[c]
        reached[c] += 1
        if c == chunks:
            if s == 0:
                small_sum[0] = small_value[0]
            else:
                finish(("small", s - 1))
                size, me, _ = dims[small_names[s - 1]]
                small_slots[s - 1, me] = small_sum[s - 1]
                value = small_slots[s - 1, 0]
                for i in range(1, size):
                    value = value + small_slots[s - 1, i]
                small_sum[s] = value
            if s < len(small_names):
                begin(("small", s), small_copies(s))
            return
        stages = len(orders[c])
        if s > 0:
            finish((c, s - 1))
        if 1 <= s <= stages:
            add_arrived(c, s - 1)
        if s < stages:
            begin((c, s), reduce_copies(c, s))
        elif s < 2 * stages:
            begin((c, s), spread_copies(c, 2 * stages - s))
        else:
            part = pl.ds(*pieces[c][:2])
            copy = pltpu.make_async_copy(gathered.at[part, span(c)], out.at[part, span(c)], save.at[c])
            copy.start()
            saves.append(copy)

    def row_block(full, device):
        return full.at[:, pl.ds(pl.multiple_of(device * length, length), length)]

    def row_copies(which, fulls, far):
        copies = []
        y_size, y_me, y_device = dims["y"]
        _, core_me, core_device = dims["core"]
        for a, full in enumerate(fulls):
            if not far:
                for step in range(1, y_size):
                    copies.append((full, place, y_device((y_me + step) % y_size), which, a, step - 1, y_size - step - 1))
                copies.append((full, place, core_device(1 - core_me), which, a, y_size - 1, y_size - 1))
            else:
                for step in range(1, y_size):
                    copies.append((full, (y_me - step + y_size) % y_size * 2 + core_me, core_device(1 - core_me), which, a,
                                   y_size - 1 + step, y_size - 1 + step))
        return [
            pltpu.make_async_remote_copy(
                src_ref=row_block(full, block), dst_ref=row_block(full, block), send_sem=row_send.at[w, a, i],
                recv_sem=row_recv.at[w, a, j], device_id=device, device_id_type=MESH)
            for full, block, device, w, a, i, j in copies
        ]

    def put_row(row, value):
        small_value[0] = jnp.where(lax.broadcasted_iota(jnp.int32, small.shape, 0) == row, value, small_value[0])

    def total(value):
        return jnp.sum(value.astype(F32), axis=0, keepdims=True)

    def rowwise(ref):
        return ref[...].reshape(flat, ref.shape[2])

    def cross_query_grads(group):
        def step(r, carry):
            def put(cs, value):
                dcq[r, :, cs] = value.astype(BF)

            attn_step(False, r, group, mask.shape[1] // length, None, cq_full, gc_full, caux_full, mask, cross_key,
                      cross_value, mine, slice(None), put)
            return carry

        lax.fori_loop(0, batch, step, 0)

    def attn_step(dkv, r, group, blocks, seen, a, b, aq, ak, k, v, query_at, key_at, put):
        def loader(ref, at):
            return lambda cs: ref[r, at, cs]

        row_grads(dkv, range(group * GROUP, group * GROUP + GROUP), length, blocks, length, seen, loader(a, query_at),
                  loader(b, query_at), aq[r, query_at], ak[r, key_at], loader(k, key_at), loader(v, key_at), put)

    def cross_key_grads(group):
        def step(r, carry):
            def put(cs, keys_grad, values_grad):
                at = cs.start
                pair[r, :, at : at + 128] = keys_grad.astype(BF)
                pair[r, :, width + at : width + at + 128] = values_grad.astype(BF)

            attn_step(True, r, group, queries.shape[1] // length, None, cq_full, gc_full, caux_full, mask, cross_key,
                      cross_value, slice(None), mine, put)
            return carry

        lax.fori_loop(0, batch, step, 0)

    def causal(dkv):
        down = lax.broadcasted_iota(jnp.int32, (length, length), 0)
        along = lax.broadcasted_iota(jnp.int32, (length, length), 1)
        return down <= along if dkv else along <= down

    def self_query_grads(group):
        def step(r, carry):
            def put(cs, value):
                at = cs.start
                joined[r, :, at : at + 128] = value.astype(BF)

            for blocks in range(1, seq_size + 1):

                @pl.when(place == blocks - 1)
                def _(blocks=blocks):
                    attn_step(False, r, group, blocks, causal(False), queries, ga_full, saux_full, mask, keys, values,
                              pl.ds((blocks - 1) * length, length), pl.ds(0, blocks * length), put)

            return carry

        lax.fori_loop(0, batch, step, 0)

    def self_key_grads(group):
        def step(r, carry):
            def put(cs, keys_grad, values_grad):
                at = cs.start
                joined[r, :, width + at : width + at + 128] = keys_grad.astype(BF)
                joined[r, :, 2 * width + at : 2 * width + at + 128] = values_grad.astype(BF)

            for blocks in range(1, seq_size + 1):

                @pl.when(place == seq_size - blocks)
                def _(blocks=blocks):
                    first = (seq_size - blocks) * length
                    attn_step(True, r, group, blocks, causal(True), queries, ga_full, saux_full, mask, keys, values,
                              pl.ds(first, blocks * length), pl.ds(first, length), put)

            return carry

        lax.fori_loop(0, batch, step, 0)

    def put_block(block, value):
        own[pl.ds((block - half_rows // width) * width, width)] = value.astype(BF)

    def middle():
        query_grad = rowwise(dcq)
        put_block(9, dot_tn(rowwise(self_low), query_grad))
        put_row(9, total(query_grad))
        grad = rowwise(grad_mid) + dot_nt(query_grad, cross_q[...])
        u, v = rowwise(unit), rowwise(root)
        put_row(0, total(grad * u))
        put_row(3, total(grad))
        scaled = grad * gain[...]
        start = v * (scaled - jnp.mean(scaled, axis=-1, keepdims=True) - u * jnp.mean(scaled * u, axis=-1, keepdims=True))
        grad_mid[...] = start.reshape(batch, length, width)
        branch = start.astype(BF)
        put_row(8, total(branch))
        mixed = rowwise(attended)
        grad_mixed = dot_nt(branch, self_out[...]).astype(BF)
        ga_full[:, mine] = grad_mixed.reshape(batch, length, width)
        saux = rowwise(self_aux).astype(F32) + head_inner(grad_mixed, mixed)
        saux_full[:, mine] = saux.astype(BF).reshape(batch, length, 128)
        begin("self", row_copies(1, (ga_full, saux_full), False))
        put_block(10, dot_tn(mixed, branch))

    def cross_weights():
        both = rowwise(pair)
        grad = dot_tn(rowwise(memory), both)
        put_block(11, grad[:, :width])
        put_block(12, grad[:, width:])
        put_row(10, total(both[:, width:]))
        grad_memory[...] = dot_nt(both, cross_kv[...]).astype(BF).reshape(batch, length, width)

    def query_weights():
        grads = joined[:, :, :width].reshape(flat, width)
        put_block(13, dot_tn(rowwise(tokens), grads))
        put_row(6, total(grads))

    def self_weights():
        grads = joined[:, :, width:].reshape(flat, 2 * width)
        grad = dot_tn(rowwise(tokens), grads)
        put_block(14, grad[:, :width])
        put_block(15, grad[:, width:])
        put_row(7, total(grads[:, width:]))

    def last():
        grads = rowwise(joined)
        grad_tokens[...] = (rowwise(grad_mid) + dot_nt(grads, self_qkv[...])).astype(BF).reshape(batch, length, width)

    def relay(key, which, fulls):
        def run():
            finish(key)
            begin(key, row_copies(which, fulls, True))

        return run

    groups = range(heads // GROUP)
    begin("cross", row_copies(0, (gc_full, caux_full), False))
    loaded(0)()
    each = lambda tag, step: [(tag, functools.partial(step, g)) for g in groups]
    self_query = each("self query", self_query_grads)
    early = len(groups) // 2
    steps = each("cross query", cross_query_grads) + [("middle", middle)] + each("cross key", cross_key_grads)
    steps += [("cross weights", cross_weights)] + self_query[:early]
    steps += each("self key", self_key_grads) + [("self weights", self_weights)] + self_query[early:]
    steps += [("query weights", query_weights), ("last", last)]
    before = {
        "cross query": [loaded(1, 2, 3, 12)],
        "middle": [loaded(4, 5, 6, 7, 8, 9), relay("cross", 0, (gc_full, caux_full))],
        "cross key": [functools.partial(finish, "cross")],
        "cross weights": [load_later, loaded(10, 11), relay("self", 1, (ga_full, saux_full))],
        "self query": [loaded(13, 14, 15)],
        "self key": [functools.partial(finish, "self"), loaded(16, 17)],
    }
    todo = list(steps)
    for action in sequence:
        if action < 0:
            tag, step = todo.pop(0)
            for extra in before.pop(tag, ()):
                extra()
            step()
        else:
            advance(action)
    small_out[...] = small_sum[len(small_names)]
    for copy in saves:
        copy.wait()


def back_and_sum(mesh_shape, heads, operands):
    dp_size, seq_size = mesh_shape["dp"], mesh_shape["seq"]
    sizes = exchange_sizes(dp_size, seq_size)
    (cross_out_grad, small, nearby, away) = operands
    ffn_grads = away[0]
    columns = ffn_grads.shape[1]
    total_rows = 2 * ffn_grads.shape[0]
    batch, length, width = nearby[0].shape
    per_device = 1
    for name in ("core", "y", "x", "z"):
        per_device *= sizes[name]
    chunks = min(16, total_rows // (16 * per_device))
    pieces, orders, sequence = plan(chunks, total_rows, columns)
    most = max(sizes.values())
    scratch = []
    arrivals = 0
    for (_, extent, _, taken), order in zip(pieces, orders):
        for name in order:
            extent //= sizes[name]
            arrivals += 2 * (sizes[name] - 1)
            scratch.append(pltpu.VMEM((sizes[name] - 1, extent, taken), BF))
    full = seq_size * length
    scratch += [
        pltpu.VMEM((total_rows // 2, columns), BF),
        pltpu.VMEM((total_rows, columns), BF),
        pltpu.VMEM((4, most) + small.shape, F32),
        pltpu.VMEM((5,) + small.shape, F32),
        pltpu.VMEM((batch, full, width), BF),
        pltpu.VMEM((batch, full, 128), BF),
        pltpu.VMEM((batch, full, width), BF),
        pltpu.VMEM((batch, full, 128), BF),
        pltpu.VMEM((batch, length, width), BF),
        pltpu.VMEM((batch, length, 2 * width), BF),
        pltpu.VMEM((batch, length, 3 * width), BF),
        pltpu.SemaphoreType.DMA((len(pieces), most - 1)),
        pltpu.SemaphoreType.DMA((arrivals,)),
        pltpu.SemaphoreType.DMA((4, most - 1)),
        pltpu.SemaphoreType.DMA((4, most - 1)),
        pltpu.SemaphoreType.DMA((len(pieces),)),
        pltpu.SemaphoreType.DMA((2, 2, seq_size)),
        pltpu.SemaphoreType.DMA((2, 2, seq_size)),
        pltpu.SemaphoreType.DMA((3,)),
        pltpu.SemaphoreType.DMA((len(away),)),
    ] + [pltpu.VMEM(value.shape, value.dtype) for i, value in enumerate(away) if i not in (13, 14)]
    anywhere = pl.BlockSpec(memory_space=pl.ANY)

    def kernel(*refs):
        ends = 2 + len(nearby)
        back_kernel(dp_size, seq_size, pieces, orders, sequence, *refs[:ends],
                    refs[ends : ends + len(away)], *refs[ends + len(away) :])

    return pl.pallas_call(
        kernel,
        out_shape=(
            jax.ShapeDtypeStruct((total_rows, columns), BF),
            jax.ShapeDtypeStruct(small.shape, F32),
            jax.ShapeDtypeStruct((batch, length, width), BF),
            jax.ShapeDtypeStruct((batch, length, width), BF),
        ),
        in_specs=[anywhere, VM] + [anywhere] * 2 + [VM] * (len(nearby) - 2) + [anywhere] * len(away),
        out_specs=(anywhere, VM, VM, VM),
        scratch_shapes=scratch,
        name="backward_and_sums",
        compiler_params=pltpu.CompilerParams(collective_id=0, has_side_effects=True, vmem_limit_bytes=62 << 20),
    )(cross_out_grad, small, *nearby, *away)

SOURCE = 56


def row_mix(heads, tq, blocks, width, seen, q, aq, k, v, ak, put):
    state = {"aux": aq.astype(F32)}
    low = lanes((tq, 128)) < HALF

    def columns(h):
        return slice(h // 2 * 128, h // 2 * 128 + 128)

    def first(h):
        even = h % 2 == 0
        return dot_nt(pick(even, q(columns(h)) * jnp.asarray(SCORE_SCALE, BF), aq), pick(even, k(columns(h)), ak))

    def rest(h, scores):
        values = v(columns(h))
        if seen is not None:
            tail = jnp.where(seen, scores[:, (blocks - 1) * width :], -BIG)
            scores = tail if blocks == 1 else jnp.concatenate([scores[:, : (blocks - 1) * width], tail], axis=1)
        peak = jnp.max(scores, axis=1, keepdims=True)
        weights = jnp.exp(scores - peak).astype(BF)
        mixed = dot_nn(weights, pick(h % 2 == 0, values, jnp.ones_like(values)))
        at = HALF if h % 2 == 0 else 0
        state["aux"] = put_parts(state["aux"], peak + jnp.log(mixed[:, at : at + 1]), LSE + 3 * h)
        if h % 2 == 0:
            state["even"] = mixed
        else:
            total = pltpu.roll(jnp.where(low, mixed, state["even"]), HALF, 1)
            put(columns(h), jnp.where(low, state["even"], mixed) / total)

    schedule(heads, 1, first, rest)
    return state["aux"].astype(BF)


def norm_rows(residual, gain, shift):
    centred = residual - jnp.mean(residual, axis=-1, keepdims=True)
    inverse = lax.rsqrt(jnp.mean(centred * centred, axis=-1, keepdims=True) + EPSILON)
    unit = centred * inverse
    return unit * gain + shift, unit, inverse


def norm_rows_back(grad, unit, inverse, gain):
    scaled = grad * gain
    return inverse * (scaled - jnp.mean(scaled, axis=-1, keepdims=True) - unit * jnp.mean(scaled * unit, axis=-1, keepdims=True))


def front_kernel(dp_size, seq_size, self_mask, cross_mask, mask_local, gains, biases, hidden_bias, tokens, memory, cotangent, *refs):
    weights_away, refs = refs[:7], refs[7:]
    (output, small, *away_outs, root_out), refs = refs[:19], refs[19:]
    kept, refs = refs[:16], refs[16:]
    (ffn_grads, cross_out_grad, mask, queries, keys, values, cross_key, cross_value, cq_full, attended, self_aux, self_low, unit,
     grad_mid, grad_crossed, cross_aux) = kept
    (tokens_full, memory_full, self_qkv, self_out, cross_q, cross_kv, cross_out, ffn_in, ffn_out, cot, after_self, crossed, hidden,
     slope, row_send, row_recv, load_sem, save_sem) = refs
    here_weights = (self_qkv, self_out, cross_q, cross_kv, cross_out, ffn_in, ffn_out)
    dims = dimensions(dp_size, seq_size)
    place = lax.axis_index("seq")
    batch, length, width = attended.shape
    heads = width // HALF
    flat = batch * length
    base = pl.multiple_of(place * length, length)
    mine = pl.ds(base, length)

    y_size, y_me, y_device = dims["y"]
    _, core_me, core_device = dims["core"]
    barrier = pltpu.get_barrier_semaphore()
    targets = [y_device((y_me + step) % y_size) for step in range(1, y_size)] + [core_device(1 - core_me)]
    for device in targets:
        pl.semaphore_signal(barrier, inc=1, device_id=device, device_id_type=MESH)

    loads = []

    def load(away, here):
        copy = pltpu.make_async_copy(away, here, load_sem.at[len(loads)])
        copy.start()
        loads.append(copy)
        return len(loads) - 1

    load(tokens, tokens_full.at[:, mine])
    load(memory, memory_full.at[:, mine])
    for away, here in zip(weights_away, here_weights):
        load(away, here)
    load(cotangent, cot)
    mask[:, mine] = mask_local[...]
    pl.semaphore_wait(barrier, len(targets))

    def row_block(full, block):
        return full.at[:, pl.ds(pl.multiple_of(block * length, length), length)]

    started = {}

    def send(key, which, fulls, kind):
        copies = []
        for a, full in enumerate(fulls):
            if kind == "y":
                todo = [(place, y_device((y_me + step) % y_size), step - 1, y_size - step - 1) for step in range(1, y_size)]
            elif kind == "core":
                todo = [(place, core_device(1 - core_me), y_size - 1, y_size - 1)]
            else:
                todo = [((y_me - step + y_size) % y_size * 2 + core_me, core_device(1 - core_me), y_size - 1 + step, y_size - 1 + step)
                        for step in range(1, y_size)]
            for block, device, i, j in todo:
                copies.append(pltpu.make_async_remote_copy(
                    src_ref=row_block(full, block), dst_ref=row_block(full, block), send_sem=row_send.at[which, a, i],
                    recv_sem=row_recv.at[which, a, j], device_id=device, device_id_type=MESH))
        for copy in copies:
            copy.start()
        started[key] = copies

    def finish(key):
        for copy in started.pop(key):
            copy.wait()

    saves = []

    def save(*which):
        for i in which:
            copy = pltpu.make_async_copy(kept[i], away_outs[i], save_sem.at[i])
            copy.start()
            saves.append(copy)

    def total(value):
        return jnp.sum(value.astype(F32), axis=0, keepdims=True)

    def rowwise(ref):
        return ref[...].reshape(flat, ref.shape[2])

    small_rows = {}
    gain, shift = [gains[i : i + 1] for i in range(3)], [biases[i : i + 1] for i in range(3)]
    bias = lambda i: biases[i : i + 1]

    loads[0].wait()
    send("tokens y", 0, (tokens_full, mask), "y")
    send("tokens core", 0, (tokens_full, mask), "core")
    loads[1].wait()
    send("memory y", 1, (memory_full,), "y")
    send("memory core", 1, (memory_full,), "core")

    def project_block(block):
        at = pl.ds(pl.multiple_of(block * length, length), length)
        rows = tokens_full[:, at].reshape(flat, width)
        for i, (ref, extra) in enumerate(((queries, bias(3)), (keys, None), (values, bias(4)))):
            value = dot_nn(rows, self_qkv[:, i * width : (i + 1) * width])
            if extra is not None:
                value = value + extra
            ref[:, at] = value.astype(BF).reshape(batch, length, width)

    loads[2].wait()
    project_block(place)
    finish("tokens core")
    project_block(place + 1 - 2 * core_me)
    finish("tokens y")
    send("tokens relay", 0, (tokens_full, mask), "relay")
    for step in range(1, y_size):
        project_block((y_me - step + y_size) % y_size * 2 + core_me)
    finish("tokens relay")
    for step in range(1, y_size):
        project_block((y_me - step + y_size) % y_size * 2 + 1 - core_me)
    save(2, 3, 4, 5)

    down = lax.broadcasted_iota(jnp.int32, (length, length), 0)
    along = lax.broadcasted_iota(jnp.int32, (length, length), 1)
    for blocks in range(1, seq_size + 1):

        @pl.when(place == blocks - 1)
        def _(blocks=blocks):
            def row(r, carry):
                at, span = pl.ds((blocks - 1) * length, length), pl.ds(0, blocks * length)

                def put(cs, value):
                    attended[r, :, cs] = value.astype(BF)

                self_aux[r] = row_mix(heads, length, blocks, length, along <= down, lambda cs: queries[r, at, cs], self_mask[r],
                                      lambda cs: keys[r, span, cs], lambda cs: values[r, span, cs], mask[r, span], put)
                return carry

            lax.fori_loop(0, batch, row, 0)

    for i in (3, 4):
        loads[i].wait()
    state, unit_first, root_first = norm_rows(
        tokens_full[:, mine].reshape(flat, width).astype(F32) + dot_nn(rowwise(attended), self_out[...]) + bias(5), gain[0], shift[0]
    )
    after_self[...] = state
    unit[...] = unit_first.reshape(batch, length, width)
    root_out[...] = root_first.reshape(batch, length, 1)
    self_low[...] = state.astype(BF).reshape(batch, length, width)
    query = (dot_nn(state.astype(BF), cross_q[...]) + bias(6)).astype(BF)
    cq_full[:, mine] = query.reshape(batch, length, width)
    finish("memory core")
    finish("memory y")
    send("memory relay", 1, (memory_full,), "relay")
    send("query y", 2, (cq_full,), "y")
    send("query core", 2, (cq_full,), "core")
    save(9, 10, 11, 12)
    loads[5].wait()

    def project_memory(block):
        at = pl.ds(pl.multiple_of(block * length, length), length)
        rows = memory_full[:, at].reshape(flat, width)
        cross_key[:, at] = dot_nn(rows, cross_kv[:, :width]).astype(BF).reshape(batch, length, width)
        cross_value[:, at] = (dot_nn(rows, cross_kv[:, width:]) + bias(7)).astype(BF).reshape(batch, length, width)

    project_memory(place)
    project_memory(place + 1 - 2 * core_me)
    for step in range(1, y_size):
        project_memory((y_me - step + y_size) % y_size * 2 + core_me)
    finish("memory relay")
    for step in range(1, y_size):
        project_memory((y_me - step + y_size) % y_size * 2 + 1 - core_me)
    save(6, 7)

    def cross_row(r, carry):
        def put(cs, value):
            crossed[r, :, cs] = value.astype(BF)

        cross_aux[r] = row_mix(heads, length, seq_size, length, None, lambda cs: cq_full[r, mine, cs], cross_mask[r],
                               lambda cs: cross_key[r, :, cs], lambda cs: cross_value[r, :, cs], mask[r], put)
        return carry

    lax.fori_loop(0, batch, cross_row, 0)
    for i in range(6, 10):
        loads[i].wait()
    after_cross, unit_second, root_second = norm_rows(after_self[...] + dot_nn(rowwise(crossed), cross_out[...]) + bias(8), gain[1],
                                                      shift[1])
    finish("query core")
    finish("query y")
    send("query relay", 2, (cq_full,), "relay")
    cross_low = after_cross.astype(BF)
    parts = ffn_in.shape[1] // width
    summed = after_cross + bias(9)
    for j in range(parts):
        cs = slice(j * width, (j + 1) * width)
        before = dot_nn(cross_low, ffn_in[:, cs]) + hidden_bias[:, cs]
        share = 0.5 * (1.0 + lax.erf(before * ROOT_HALF))
        slope[:, cs] = share + before * NORMAL_DENSITY * jnp.exp(-0.5 * before * before)
        value = (before * share).astype(BF)
        hidden[:, cs] = value
        summed = summed + dot_nn(value, ffn_out[cs])
    result, unit_third, root_third = norm_rows(summed, gain[2], shift[2])
    output[...] = result.astype(BF).reshape(batch, length, width)
    grad = rowwise(cot).astype(F32)
    small_rows[2], small_rows[5] = total(grad * unit_third), total(grad)
    grad_third = norm_rows_back(grad, unit_third, root_third, gain[2])
    branch = grad_third.astype(BF)
    small_rows[12] = total(branch)
    grad_second = grad_third
    for j in range(parts):
        cs = slice(j * width, (j + 1) * width)
        ffn_grads[pl.ds((parts + j) * width, width)] = dot_tn(hidden[:, cs], branch).astype(BF)
        grad_hidden = (dot_nt(branch, ffn_out[cs]) * slope[:, cs]).astype(BF)
        small_rows[13 + j] = total(grad_hidden)
        ffn_grads[pl.ds(j * width, width)] = dot_tn(cross_low, grad_hidden).astype(BF)
        grad_second = grad_second + dot_nt(grad_hidden, ffn_in[:, cs])
    save(0)
    finish("query relay")
    save(8)
    small_rows[1], small_rows[4] = total(grad_second * unit_second), total(grad_second)
    middle = norm_rows_back(grad_second, unit_second, root_second, gain[1])
    grad_mid[...] = middle.reshape(batch, length, width)
    branch = middle.astype(BF)
    small_rows[11] = total(branch)
    mixed = rowwise(crossed)
    grad_mixed = dot_nt(branch, cross_out[...]).astype(BF)
    grad_crossed[...] = grad_mixed.reshape(batch, length, width)
    aux = rowwise(cross_aux).astype(F32) + head_inner(grad_mixed, mixed)
    cross_aux[...] = aux.astype(BF).reshape(batch, length, 128)
    cross_out_grad[...] = dot_tn(mixed, branch).astype(BF)
    save(1, 13, 14, 15)
    small[...] = jnp.zeros(small.shape, F32)
    for row, value in small_rows.items():
        small[row : row + 1] = value
    for copy in saves:
        copy.wait()


def front(mesh_shape, self_mask, cross_mask, mask_local, gains, biases, hidden_bias, tokens, memory, cotangent, weights):
    dp_size, seq_size = mesh_shape["dp"], mesh_shape["seq"]
    batch, length, width = tokens.shape
    hidden = weights[5].shape[1]
    flat, full = batch * length, seq_size * length
    anywhere = pl.BlockSpec(memory_space=pl.ANY)
    whole, part, narrow = (batch, full, width), (batch, length, width), (batch, length, 128)
    saved = [((2 * hidden, width), BF), ((width, width), BF), ((batch, full, 128), BF)] + [(whole, BF)] * 6
    saved += [(part, BF), (narrow, BF), (part, BF), (part, F32), (part, F32), (part, BF), (narrow, BF)]
    out_shape = [(part, BF), ((24, width), F32)] + saved + [((batch, length, 1), F32)]
    scratch = [pltpu.VMEM(shape, kind) for shape, kind in saved]
    scratch += [pltpu.VMEM(whole, BF)] * 2 + [pltpu.VMEM(value.shape, BF) for value in weights]
    scratch += [
        pltpu.VMEM(part, BF),
        pltpu.VMEM((flat, width), F32),
        pltpu.VMEM(part, BF),
        pltpu.VMEM((flat, hidden), BF),
        pltpu.VMEM((flat, hidden), F32),
        pltpu.SemaphoreType.DMA((3, 2, seq_size)),
        pltpu.SemaphoreType.DMA((3, 2, seq_size)),
        pltpu.SemaphoreType.DMA((10,)),
        pltpu.SemaphoreType.DMA((len(saved),)),
    ]
    return pl.pallas_call(
        functools.partial(front_kernel, dp_size, seq_size),
        out_shape=tuple(jax.ShapeDtypeStruct(shape, kind) for shape, kind in out_shape),
        in_specs=[VM] * 6 + [anywhere] * 10,
        out_specs=(VM, VM) + (anywhere,) * len(saved) + (VM,),
        scratch_shapes=scratch,
        name="forward_and_feed_forward",
        compiler_params=pltpu.CompilerParams(collective_id=1, has_side_effects=True, vmem_limit_bytes=62 << 20),
    )(self_mask, cross_mask, mask_local, gains, biases, hidden_bias, tokens, memory, cotangent, *weights)


def unpack_kernel(summed, small, *refs):
    passed, outs = refs[:3], refs[3:16]
    taken, given, held, load_sem, save_sem, pass_sem = refs[16:]
    width = summed.shape[1]
    arriving = [pltpu.make_async_copy(a, held.at[i], pass_sem.at[0, i]) for i, a in enumerate(passed)]
    through = [pltpu.make_async_copy(held.at[i], b, pass_sem.at[1, i]) for i, b in enumerate(outs[:3])]
    qkv, self_out, cross_q, cross_kv, cross_out, ffn_in, ffn_out, gains, biases, hidden = outs[3:]
    columns = lambda ref, i: ref.at[:, pl.ds(i * width, width)]
    places = [columns(ffn_in, i) for i in range(4)] + [ffn_out.at[pl.ds(i * width, width)] for i in range(4)]
    places += [cross_out, cross_q, self_out] + [columns(cross_kv, i) for i in range(2)] + [columns(qkv, i) for i in range(3)]
    loads = []
    for i in range(len(places)):
        loads.append(pltpu.make_async_copy(summed.at[pl.ds(i * width, width)], taken.at[i], load_sem.at[i]))
        loads[-1].start()
    saves = []
    for i, place in enumerate(places):
        loads[i].wait()
        given[i] = taken[i].astype(F32)
        saves.append(pltpu.make_async_copy(given.at[i], place, save_sem.at[i]))
        saves[-1].start()
        if i == 1:
            for copy in arriving:
                copy.start()
        if i == 6:
            for copy, onward in zip(arriving, through):
                copy.wait()
                onward.start()
    gains[...] = small[0:3]
    biases[...] = small[3:13]
    hidden[...] = small[13:17]
    for copy in saves + through:
        copy.wait()


def unpack(summed, small, passed):
    width = summed.shape[1]
    blocks = summed.shape[0] // width
    square = (width, width)
    shapes = [(width, 3 * width), square, square, (width, 2 * width), square, (width, 4 * width), (4 * width, width)]
    anywhere = pl.BlockSpec(memory_space=pl.ANY)
    return pl.pallas_call(
        unpack_kernel,
        out_shape=tuple(jax.ShapeDtypeStruct(value.shape, value.dtype) for value in passed)
        + tuple(jax.ShapeDtypeStruct(shape, F32) for shape in shapes + [(3, width), (10, width), (4, width)]),
        in_specs=[anywhere, VM] + [anywhere] * 3,
        out_specs=(anywhere,) * 10 + (VM,) * 3,
        scratch_shapes=[
            pltpu.VMEM((blocks,) + square, BF),
            pltpu.VMEM((blocks,) + square, F32),
            pltpu.VMEM((3,) + passed[0].shape, BF),
            pltpu.SemaphoreType.DMA((blocks,)),
            pltpu.SemaphoreType.DMA((blocks,)),
            pltpu.SemaphoreType.DMA((2, 3)),
        ],
        name="unpack_sums",
        compiler_params=pltpu.CompilerParams(vmem_limit_bytes=62 << 20),
    )(summed, small, *passed)


def shards(mesh_shape, tokens, memory, segment_ids, source_ids, source_lengths, cotangent, self_qkv, self_out, cross_q, cross_kv,
           cross_out, ffn_in, ffn_out, norm_gains, bias_rows, hidden_bias):
    length = tokens.shape[1]
    place = lax.axis_index("seq") * length + jnp.arange(length, dtype=jnp.int32)
    lane = jnp.arange(128) % HALF
    usable = (place[None] < source_lengths[:, None])[..., None]
    segments, sources = segment_ids[..., None], source_ids[..., None]
    self_mask = jnp.where(segments == lane, 1.0, 0.0).astype(BF)
    cross_mask = jnp.where(segments == lane - SOURCE, 1.0, 0.0).astype(BF)
    other = jnp.where(lane < 8, segments != lane, (lane >= SOURCE) & ~((sources == lane - SOURCE) & usable))
    mask = jnp.where(other, -BIG, 0.0).astype(BF)
    (output, small, ffn_grads, cross_out_grad, mask_full, queries, keys, values, cross_key, cross_value, cross_query, attended, self_aux,
     self_low, unit, grad_mid, grad_crossed, cross_aux, root) = front(
        mesh_shape, self_mask, cross_mask, mask, norm_gains, bias_rows, hidden_bias.reshape(1, -1), tokens, memory, cotangent,
        (self_qkv, self_out, cross_q, cross_kv, cross_out, ffn_in, ffn_out),
    )
    summed, small, grad_tokens, grad_memory = back_and_sum(
        mesh_shape, HEADS,
        (
            cross_out_grad, small,
            (grad_crossed, cross_aux, self_aux, root, norm_gains[:1]),
            (ffn_grads, cross_key, cross_value, mask_full, self_low, unit, grad_mid, cross_q, self_out, attended, memory,
             cross_kv, cross_query, queries, keys, values, tokens, self_qkv),
        ),
    )

    *arrays, hidden_row = unpack(summed, small, (output, grad_tokens, grad_memory))
    return (*arrays, hidden_row.reshape(hidden_bias.shape))


def solution(mesh):
    placed = (
        P("dp", "seq", None),
        P("dp", "seq", None),
        P("dp", "seq"),
        P("dp", "seq"),
        P("dp"),
        P("dp", "seq", None),
        P(),
        P(),
        P(),
        P(),
        P(),
        P(),
        P(),
        P(),
        P(),
        P(),
    )
    return jax.shard_map(
        functools.partial(shards, dict(mesh.shape)),
        mesh=mesh,
        in_specs=placed,
        out_specs=(
            P("dp", "seq", None),
            P("dp", "seq", None),
            P("dp", "seq", None),
            P(),
            P(),
            P(),
            P(),
            P(),
            P(),
            P(),
            P(),
            P(),
            P(),
        ),
        check_vma=False,
    )
```

```python
import functools

import jax
import jax.numpy as jnp
from jax import lax
from jax.experimental import pallas as pl
from jax.experimental.pallas import tpu as pltpu
from jax.sharding import PartitionSpec as P

HEADS = 8
SCORE_SCALE = 0.125
EPSILON = 1e-05
ROOT_HALF = 0.7071067811865476
NORMAL_DENSITY = 0.3989422804014327

BIG=float(2.0**30)
HALF=64
LSE=8; DELTA=32
NT=(((1,),(1,)),((),()))
F32=jnp.float32; BF=jnp.bfloat16
def lanes(shape): return lax.broadcasted_iota(jnp.int32,shape,len(shape)-1)
def pick(even, mine, aux):
    low=lanes(mine.shape)<HALF
    return jnp.where(low,mine,aux) if even else jnp.where(low,aux,mine)
def dot_nt(a,b): return lax.dot_general(a,b,NT,preferred_element_type=F32)
def dot_nn(a,b): return jnp.dot(a,b,preferred_element_type=F32)
def put_parts(aux,x,at):
    lane=lanes(aux.shape)%HALF
    hi=x.astype(BF).astype(F32); r=x-hi; mid=r.astype(BF).astype(F32)
    return jnp.where(lane==at,hi,jnp.where(lane==at+1,mid,jnp.where(lane==at+2,r-mid,aux)))
def row_const(shape,at,n):
    lane=lanes(shape)%HALF
    return (lane>=at)&(lane<at+n)
def schedule(heads,ahead,first,rest):
    heads=list(heads) if not isinstance(heads,int) else list(range(heads))
    kept={}
    for h in heads[:ahead]: kept[h]=first(h)
    for i,h in enumerate(heads):
        if i+ahead<len(heads): kept[heads[i+ahead]]=first(heads[i+ahead])
        rest(h,kept.pop(h))


VM = pl.BlockSpec(memory_space=pltpu.VMEM)

MESH = pl.DeviceIdType.MESH


def dimensions(dp_size, seq_size):
    dp, seq = lax.axis_index("dp"), lax.axis_index("seq")
    return {
        "core": (2, seq % 2, lambda i: (dp, seq - seq % 2 + i)),
        "y": (seq_size // 2, seq // 2, lambda i: (dp, i * 2 + seq % 2)),
        "x": (2, dp % 2, lambda i: (dp - dp % 2 + i, seq)),
        "z": (dp_size // 2, dp // 2, lambda i: (i * 2 + dp % 2, seq)),
        "near": (2, dp // 2 % 2, lambda i: (dp + (i - dp // 2 % 2) * 2, seq)),
        "far": (dp_size // 4, dp // 4, lambda i: (i * 4 + dp % 4, seq)),
    }


def plan(chunks, rows, columns):
    if chunks != 16:
        pieces = [(c * (rows // chunks), rows // chunks, 0, columns) for c in range(chunks)]
        orders = [("core", "x", "y", "z"), ("core", "y", "x", "z")] * (chunks // 2)
        waiting = [0] * (chunks // 2) + [20] * (chunks - chunks // 2)
        sequence = []
        for slot in range(21):
            sequence += [c for c in range(chunks) if waiting[c] <= slot < waiting[c] + 9]
            sequence.append(-1)
        sequence += [c for _ in range(8) for c in range(chunks) if waiting[c] == 20]
        return pieces, orders, sequence + [chunks] * 5
    half = columns // 2
    pieces = [(columns * block, columns, first * half, taken * half) for block, first, taken in [(0, 0, 2), (1, 0, 2), (2, 0, 2), (3, 0, 2), (4, 0, 2), (5, 0, 2), (6, 0, 2), (7, 0, 2), (8, 0, 2), (9, 0, 2), (10, 0, 2), (11, 0, 2), (12, 0, 2), (14, 0, 2), (15, 0, 2), (13, 0, 1), (13, 1, 1)]]
    kinds = (
        ('core', 'near', 'x', 'far', 'y'),
        ('core', 'x', 'near', 'y', 'far'),
        ('core', 'x', 'near', 'far', 'y'),
        ('core', 'y', 'x', 'z'),
        ('core', 'near', 'far', 'x', 'y'),
        ('core', 'near', 'x', 'y', 'far'),
        ('core', 'x', 'y', 'z'),
    )
    orders = [kinds[i] for i in (0, 0, 1, 2, 3, 2, 4, 5, 0, 2, 6, 0, 6, 6, 3, 3, 6)]
    sequence = [1, 0, 7, 4, 2, 3, 6, 8, 5, -1, -1, -1, 1, 0, 7, 4, 2, 3, 6, 8, 5, -1, -1, 4, 2, 10, 1, 3, 9, 5, -1, 0, 7, 10, 9, 4, 6, 8, 1, -1, 2, 3, 5, -1, 4, -1, 1, 0, 7, 2, 8, -1, 1, 0, 7, 4, 2, 12, 11, 10, 3, 9, 6, 8, 5, -1, 1, 0, 7, 2, 12, 11, 3, 9, 4, 6, 8, 5, -1, 0, 10, -1, 1, 7, 2, 12, 3, 9, 6, 8, 5, -1, 0, 4, 1, 10, -1, 7, 4, 12, 11, 9, 6, 0, -1, 2, 3, 9, 8, 5, 10, -1, 7, 14, 13, 6, -1, 12, 11, 10, -1, 2, 14, 13, 9, 8, -1, 16, 15, 17, -1, 2, 10, 1, 16, 15, 14, 3, 10, 13, 5, 11, 1, 17, 15, 12, 6, 11, 16, 0, 13, 9, 11, 0, 14, 16, 17, 15, 12, 7, 7, 13, 3, 11, 16, 15, 5, 8, 14, 17, 3, 5, 8, 9, 16, 15, 6, 13, 12, 11, 14, 9, 17, 15, 16, 6, 12, 13, 14, 11, 15, 16, 11, 15, 16, 13, 14, 13, 14]
    return pieces, orders, sequence


def exchange_sizes(dp_size, seq_size):
    return {"core": 2, "y": seq_size // 2, "x": 2, "z": dp_size // 2, "near": 2, "far": dp_size // 4}


def row_grads(dkv, heads, tq, blocks, width, seen, a, b, aq, ak, k, v, put):
    state = {}
    minus = jnp.asarray(-1.0, BF)
    edge = (slice(None), slice(0, width)) if dkv else (slice(None), slice((blocks - 1) * width, blocks * width))

    def columns(h):
        return slice(h // 2 * 128, h // 2 * 128 + 128)

    def first(h):
        e, cs = h % 2 == 0, columns(h)
        keys, values = k(cs), v(cs)
        ka = pick(e, keys, jnp.where(row_const(keys.shape, LSE + 3 * h, 3), minus, ak))
        va = pick(e, values, jnp.where(row_const(values.shape, DELTA + 3 * h, 3), minus, jnp.zeros_like(values)))
        qa, ga = pick(e, a(cs) * jnp.asarray(SCORE_SCALE, BF), aq), pick(e, b(cs), aq)
        return (dot_nt(ka, qa), dot_nt(va, ga)) if dkv else (dot_nt(qa, ka), dot_nt(ga, va))

    def rest(h, pair):
        scores, grads = pair
        cs = columns(h)
        if seen is not None:
            masked = jnp.where(seen, scores[edge], -BIG)
            if blocks == 1:
                scores = masked
            elif dkv:
                scores = jnp.concatenate([masked, scores[:, width:]], axis=1)
            else:
                scores = jnp.concatenate([scores[:, : (blocks - 1) * width], masked], axis=1)
        weights = jnp.exp(scores)
        grad_scores = (weights * grads).astype(BF)
        low = lanes((tq, 128)) < HALF
        if dkv:
            values_grad = dot_nn(weights.astype(BF), b(cs))
            keys_grad = dot_nn(grad_scores, a(cs))
            if h % 2 == 0:
                state["k"], state["v"] = keys_grad, values_grad
            else:
                put(cs, SCORE_SCALE * jnp.where(low, state["k"], keys_grad), jnp.where(low, state["v"], values_grad))
        else:
            query_grad = dot_nn(grad_scores, k(cs))
            if h % 2 == 0:
                state["q"] = query_grad
            else:
                put(cs, SCORE_SCALE * jnp.where(low, state["q"], query_grad))

    schedule(heads, 1, first, rest)


TN = (((0,), (0,)), ((), ()))


def dot_tn(a, b):
    return lax.dot_general(a, b, TN, preferred_element_type=F32)


def head_inner(grad_mixed, mixed):
    product = grad_mixed.astype(F32) * mixed.astype(F32)
    lane = lax.broadcasted_iota(jnp.int32, (product.shape[1], 128), 1) % HALF
    head = lax.broadcasted_iota(jnp.int32, (product.shape[1], 128), 0) // HALF
    first = DELTA + 3 * head
    chosen = jnp.where((lane >= first) & (lane < first + 3), 1.0, 0.0).astype(BF)
    high = product.astype(BF)
    rest = product - high.astype(F32)
    middle = rest.astype(BF)
    inner = dot_nn(high, chosen) + dot_nn(middle, chosen) + dot_nn((rest - middle.astype(F32)).astype(BF), chosen)
    high = inner.astype(BF).astype(F32)
    rest = inner - high
    middle = rest.astype(BF).astype(F32)
    part = (lanes(inner.shape) % HALF - DELTA + 3) % 3
    return jnp.where(part == 0, high, jnp.where(part == 1, middle, rest - middle))


GROUP = 2


def back_kernel(dp_size, seq_size, pieces, orders, sequence,
                cross_out_grad, small, grad_crossed, cross_aux, self_aux, root, gain, away_refs,
                out, small_out, grad_tokens, grad_memory, *scratch):
    dims = dimensions(dp_size, seq_size)
    held = [[None] * len(order) for order in orders]
    taken = 0
    for c, order in enumerate(orders):
        for s in range(len(order)):
            held[c][s] = scratch[taken]
            taken += 1
    (own, gathered, small_slots, small_sum, gc_full, caux_full, ga_full, saux_full, dcq, pair, joined,
     send, recv, small_send, small_recv, save, row_send, row_recv, local_sem, load_sem, *here_refs) = scratch[taken:]
    half_rows = own.shape[0]
    chunks = len(pieces)
    place = lax.axis_index("seq")
    batch, length, width = grad_crossed.shape
    heads = width // HALF
    base = pl.multiple_of(place * length, length)
    mine = pl.ds(base, length)
    flat = batch * length

    peers = [(name, step) for name in ("core", "x", "y", "z") for step in range(1, dims[name][0])]
    barrier = pltpu.get_barrier_semaphore()
    for name, step in peers:
        size, me, device = dims[name]
        pl.semaphore_signal(barrier, inc=1, device_id=device((me + step) % size), device_id_type=MESH)

    locals_ = []
    for i, (block, full) in enumerate(((grad_crossed, gc_full), (cross_aux, caux_full))):
        locals_.append(pltpu.make_async_copy(block, full.at[:, mine], local_sem.at[i]))
    locals_.append(pltpu.make_async_copy(cross_out_grad, own.at[pl.ds(0, width)], local_sem.at[2]))
    for copy in locals_:
        copy.start()
    loads = {}
    here_refs = list(here_refs)
    here_refs[13:13] = here_refs[1:3]
    for i, (away, here) in enumerate(zip(away_refs, here_refs)):
        loads[i] = pltpu.make_async_copy(away, here, load_sem.at[i])
        if i not in (13, 14):
            loads[i].start()

    def load_later():
        loads[13].start()
        loads[14].start()

    def loaded(*which):
        def run():
            for i in which:
                loads.pop(i).wait()

        return run

    (ffn_grads, cross_key, cross_value, mask, self_low, unit, grad_mid, cross_q, self_out, attended, memory, cross_kv,
     cq_full, queries, keys, values, tokens, self_qkv) = here_refs
    small_value = [small[...]]
    pl.semaphore_wait(barrier, len(peers))
    for copy in locals_:
        copy.wait()

    def span(c):
        return pl.ds(pieces[c][2], pieces[c][3])

    def source(c):
        at, rows = pieces[c][:2]
        return ffn_grads.at[pl.ds(at, rows), span(c)] if at < half_rows else own.at[pl.ds(at - half_rows, rows), span(c)]

    def current(c, s):
        return source(c) if s == 0 else held[c][s - 1].at[0]

    firsts = {}
    count = 0
    for c, order in enumerate(orders):
        for s in range(2 * len(order)):
            firsts[c, s] = count
            count += dims[order[min(s, 2 * len(order) - 1 - s)]][0] - 1

    def reduce_copies(c, s):
        size, me, device = dims[orders[c][s]]
        now = current(c, s)
        piece = now.shape[0] // size
        copies = []
        for step in range(1, size):
            other = (me + step) % size
            copies.append(
                pltpu.make_async_remote_copy(
                    src_ref=now.at[pl.ds(pl.multiple_of(other * piece, piece), piece)],
                    dst_ref=held[c][s].at[size - step - 1],
                    send_sem=send.at[c, step - 1],
                    recv_sem=recv.at[firsts[c, s] + size - step - 1],
                    device_id=device(other),
                    device_id_type=MESH,
                )
            )
        return copies

    def offset(c, s):
        at, extent = pieces[c][:2]
        for name in orders[c][:s]:
            size, me, _ = dims[name]
            extent //= size
            at = at + me * extent
        return pl.multiple_of(at, extent), extent

    def spread_copies(c, s):
        size, me, device = dims[orders[c][s - 1]]
        at, extent = offset(c, s)
        copies = []
        for step in range(1, size):
            copies.append(
                pltpu.make_async_remote_copy(
                    src_ref=gathered.at[pl.ds(at, extent), span(c)],
                    dst_ref=gathered.at[pl.ds(at, extent), span(c)],
                    send_sem=send.at[c, step - 1],
                    recv_sem=recv.at[firsts[c, 2 * len(orders[c]) - s] + size - step - 1],
                    device_id=device((me + step) % size),
                    device_id_type=MESH,
                )
            )
        return copies

    def add_arrived(c, s):
        size, me, _ = dims[orders[c][s]]
        now = current(c, s)
        piece = now.shape[0] // size
        kept = now.at[pl.ds(pl.multiple_of(me * piece, piece), piece)]
        block = min(piece, 128)
        last = s == len(orders[c]) - 1
        at = offset(c, len(orders[c]))[0] if last else 0

        def add(i, carry):
            part = pl.ds(pl.multiple_of(i * block, block), block)
            if size == 2:
                value = kept[part] + held[c][s][0, part]
            else:
                value = kept[part].astype(F32)
                for slot in range(size - 1):
                    value = value + held[c][s][slot, part].astype(F32)
            if last:
                gathered[pl.ds(pl.multiple_of(at + i * block, 16), block), span(c)] = value.astype(BF)
            else:
                held[c][s][0, part] = value.astype(BF)
            return carry

        lax.fori_loop(0, piece // block, add, 0)

    small_names = ("core", "x", "y", "z")

    def small_copies(s):
        size, me, device = dims[small_names[s]]
        return [
            pltpu.make_async_remote_copy(
                src_ref=small_sum.at[s],
                dst_ref=small_slots.at[s, me],
                send_sem=small_send.at[s, step - 1],
                recv_sem=small_recv.at[s, size - step - 1],
                device_id=device((me + step) % size),
                device_id_type=MESH,
            )
            for step in range(1, size)
        ]

    started = {}

    def begin(key, copies):
        for copy in copies:
            copy.start()
        started[key] = copies

    def finish(key):
        for copy in started.pop(key):
            copy.wait()

    saves = []
    reached = [0] * (chunks + 1)

    def advance(c):
        s = reached[c]
        reached[c] += 1
        if c == chunks:
            if s == 0:
                small_sum[0] = small_value[0]
            else:
                finish(("small", s - 1))
                size, me, _ = dims[small_names[s - 1]]
                small_slots[s - 1, me] = small_sum[s - 1]
                value = small_slots[s - 1, 0]
                for i in range(1, size):
                    value = value + small_slots[s - 1, i]
                small_sum[s] = value
            if s < len(small_names):
                begin(("small", s), small_copies(s))
            return
        stages = len(orders[c])
        if s > 0:
            finish((c, s - 1))
        if 1 <= s <= stages:
            add_arrived(c, s - 1)
        if s < stages:
            begin((c, s), reduce_copies(c, s))
        elif s < 2 * stages:
            begin((c, s), spread_copies(c, 2 * stages - s))
        else:
            part = pl.ds(*pieces[c][:2])
            copy = pltpu.make_async_copy(gathered.at[part, span(c)], out.at[part, span(c)], save.at[c])
            copy.start()
            saves.append(copy)

    def row_block(full, device):
        return full.at[:, pl.ds(pl.multiple_of(device * length, length), length)]

    def row_copies(which, fulls, far):
        copies = []
        y_size, y_me, y_device = dims["y"]
        _, core_me, core_device = dims["core"]
        for a, full in enumerate(fulls):
            if not far:
                for step in range(1, y_size):
                    copies.append((full, place, y_device((y_me + step) % y_size), which, a, step - 1, y_size - step - 1))
                copies.append((full, place, core_device(1 - core_me), which, a, y_size - 1, y_size - 1))
            else:
                for step in range(1, y_size):
                    copies.append((full, (y_me - step + y_size) % y_size * 2 + core_me, core_device(1 - core_me), which, a,
                                   y_size - 1 + step, y_size - 1 + step))
        return [
            pltpu.make_async_remote_copy(
                src_ref=row_block(full, block), dst_ref=row_block(full, block), send_sem=row_send.at[w, a, i],
                recv_sem=row_recv.at[w, a, j], device_id=device, device_id_type=MESH)
            for full, block, device, w, a, i, j in copies
        ]

    def put_row(row, value):
        small_value[0] = jnp.where(lax.broadcasted_iota(jnp.int32, small.shape, 0) == row, value, small_value[0])

    def total(value):
        return jnp.sum(value.astype(F32), axis=0, keepdims=True)

    def rowwise(ref):
        return ref[...].reshape(flat, ref.shape[2])

    def cross_query_grads(group):
        def step(r, carry):
            def put(cs, value):
                dcq[r, :, cs] = value.astype(BF)

            attn_step(False, r, group, mask.shape[1] // length, None, cq_full, gc_full, caux_full, mask, cross_key,
                      cross_value, mine, slice(None), put)
            return carry

        lax.fori_loop(0, batch, step, 0)

    def attn_step(dkv, r, group, blocks, seen, a, b, aq, ak, k, v, query_at, key_at, put):
        def loader(ref, at):
            return lambda cs: ref[r, at, cs]

        row_grads(dkv, range(group * GROUP, group * GROUP + GROUP), length, blocks, length, seen, loader(a, query_at),
                  loader(b, query_at), aq[r, query_at], ak[r, key_at], loader(k, key_at), loader(v, key_at), put)

    def cross_key_grads(group):
        def step(r, carry):
            def put(cs, keys_grad, values_grad):
                at = cs.start
                pair[r, :, at : at + 128] = keys_grad.astype(BF)
                pair[r, :, width + at : width + at + 128] = values_grad.astype(BF)

            attn_step(True, r, group, queries.shape[1] // length, None, cq_full, gc_full, caux_full, mask, cross_key,
                      cross_value, slice(None), mine, put)
            return carry

        lax.fori_loop(0, batch, step, 0)

    def causal(dkv):
        down = lax.broadcasted_iota(jnp.int32, (length, length), 0)
        along = lax.broadcasted_iota(jnp.int32, (length, length), 1)
        return down <= along if dkv else along <= down

    def self_query_grads(group):
        def step(r, carry):
            def put(cs, value):
                at = cs.start
                joined[r, :, at : at + 128] = value.astype(BF)

            for blocks in range(1, seq_size + 1):

                @pl.when(place == blocks - 1)
                def _(blocks=blocks):
                    attn_step(False, r, group, blocks, causal(False), queries, ga_full, saux_full, mask, keys, values,
                              pl.ds((blocks - 1) * length, length), pl.ds(0, blocks * length), put)

            return carry

        lax.fori_loop(0, batch, step, 0)

    def self_key_grads(group):
        def step(r, carry):
            def put(cs, keys_grad, values_grad):
                at = cs.start
                joined[r, :, width + at : width + at + 128] = keys_grad.astype(BF)
                joined[r, :, 2 * width + at : 2 * width + at + 128] = values_grad.astype(BF)

            for blocks in range(1, seq_size + 1):

                @pl.when(place == seq_size - blocks)
                def _(blocks=blocks):
                    first = (seq_size - blocks) * length
                    attn_step(True, r, group, blocks, causal(True), queries, ga_full, saux_full, mask, keys, values,
                              pl.ds(first, blocks * length), pl.ds(first, length), put)

            return carry

        lax.fori_loop(0, batch, step, 0)

    def put_block(block, value):
        own[pl.ds((block - half_rows // width) * width, width)] = value.astype(BF)

    def middle():
        query_grad = rowwise(dcq)
        put_block(9, dot_tn(rowwise(self_low), query_grad))
        put_row(9, total(query_grad))
        grad = rowwise(grad_mid) + dot_nt(query_grad, cross_q[...])
        u, v = rowwise(unit), rowwise(root)
        put_row(0, total(grad * u))
        put_row(3, total(grad))
        scaled = grad * gain[0:1]
        start = v * (scaled - jnp.mean(scaled, axis=-1, keepdims=True) - u * jnp.mean(scaled * u, axis=-1, keepdims=True))
        grad_mid[...] = start.reshape(batch, length, width)
        branch = start.astype(BF)
        put_row(8, total(branch))
        mixed = rowwise(attended)
        grad_mixed = dot_nt(branch, self_out[...]).astype(BF)
        ga_full[:, mine] = grad_mixed.reshape(batch, length, width)
        saux = rowwise(self_aux).astype(F32) + head_inner(grad_mixed, mixed)
        saux_full[:, mine] = saux.astype(BF).reshape(batch, length, 128)
        begin("self", row_copies(1, (ga_full, saux_full), False))
        put_block(10, dot_tn(mixed, branch))

    def cross_weights():
        both = rowwise(pair)
        grad = dot_tn(rowwise(memory), both)
        put_block(11, grad[:, :width])
        put_block(12, grad[:, width:])
        put_row(10, total(both[:, width:]))
        grad_memory[...] = dot_nt(both, cross_kv[...]).astype(BF).reshape(batch, length, width)

    def query_weights():
        grads = joined[:, :, :width].reshape(flat, width)
        put_block(13, dot_tn(rowwise(tokens), grads))
        put_row(6, total(grads))

    def self_weights():
        grads = joined[:, :, width:].reshape(flat, 2 * width)
        grad = dot_tn(rowwise(tokens), grads)
        put_block(14, grad[:, :width])
        put_block(15, grad[:, width:])
        put_row(7, total(grads[:, width:]))

    def last():
        grads = rowwise(joined)
        grad_tokens[...] = (rowwise(grad_mid) + dot_nt(grads, self_qkv[...])).astype(BF).reshape(batch, length, width)

    def relay(key, which, fulls):
        def run():
            finish(key)
            begin(key, row_copies(which, fulls, True))

        return run

    groups = range(heads // GROUP)
    begin("cross", row_copies(0, (gc_full, caux_full), False))
    loaded(0)()
    each = lambda tag, step: [(tag, functools.partial(step, g)) for g in groups]
    self_query = each("self query", self_query_grads)
    early = len(groups) // 2
    steps = each("cross query", cross_query_grads) + [("middle", middle)] + each("cross key", cross_key_grads)
    steps += [("cross weights", cross_weights)] + self_query[:early]
    steps += each("self key", self_key_grads) + [("self weights", self_weights)] + self_query[early:]
    steps += [("query weights", query_weights), ("last", last)]
    before = {
        "cross query": [loaded(1, 2, 3, 12)],
        "middle": [loaded(4, 5, 6, 7, 8, 9), relay("cross", 0, (gc_full, caux_full))],
        "cross key": [functools.partial(finish, "cross")],
        "cross weights": [load_later, loaded(10, 11), relay("self", 1, (ga_full, saux_full))],
        "self query": [loaded(13, 14, 15)],
        "self key": [functools.partial(finish, "self"), loaded(16, 17)],
    }
    todo = list(steps)
    for action in sequence:
        if action < 0:
            tag, step = todo.pop(0)
            for extra in before.pop(tag, ()):
                extra()
            step()
        else:
            advance(action)
    small_out[...] = small_sum[len(small_names)]
    for copy in saves:
        copy.wait()


def back_and_sum(mesh_shape, heads, operands):
    dp_size, seq_size = mesh_shape["dp"], mesh_shape["seq"]
    sizes = exchange_sizes(dp_size, seq_size)
    (cross_out_grad, small, nearby, away) = operands
    ffn_grads = away[0]
    columns = ffn_grads.shape[1]
    total_rows = 2 * ffn_grads.shape[0]
    batch, length, width = nearby[0].shape
    per_device = 1
    for name in ("core", "y", "x", "z"):
        per_device *= sizes[name]
    chunks = min(16, total_rows // (16 * per_device))
    pieces, orders, sequence = plan(chunks, total_rows, columns)
    most = max(sizes.values())
    scratch = []
    arrivals = 0
    for (_, extent, _, taken), order in zip(pieces, orders):
        for name in order:
            extent //= sizes[name]
            arrivals += 2 * (sizes[name] - 1)
            scratch.append(pltpu.VMEM((sizes[name] - 1, extent, taken), BF))
    full = seq_size * length
    scratch += [
        pltpu.VMEM((total_rows // 2, columns), BF),
        pltpu.VMEM((total_rows, columns), BF),
        pltpu.VMEM((4, most) + small.shape, F32),
        pltpu.VMEM((5,) + small.shape, F32),
        pltpu.VMEM((batch, full, width), BF),
        pltpu.VMEM((batch, full, 128), BF),
        pltpu.VMEM((batch, full, width), BF),
        pltpu.VMEM((batch, full, 128), BF),
        pltpu.VMEM((batch, length, width), BF),
        pltpu.VMEM((batch, length, 2 * width), BF),
        pltpu.VMEM((batch, length, 3 * width), BF),
        pltpu.SemaphoreType.DMA((len(pieces), most - 1)),
        pltpu.SemaphoreType.DMA((arrivals,)),
        pltpu.SemaphoreType.DMA((4, most - 1)),
        pltpu.SemaphoreType.DMA((4, most - 1)),
        pltpu.SemaphoreType.DMA((len(pieces),)),
        pltpu.SemaphoreType.DMA((2, 2, seq_size)),
        pltpu.SemaphoreType.DMA((2, 2, seq_size)),
        pltpu.SemaphoreType.DMA((3,)),
        pltpu.SemaphoreType.DMA((len(away),)),
    ] + [pltpu.VMEM(value.shape, value.dtype) for i, value in enumerate(away) if i not in (13, 14)]
    anywhere = pl.BlockSpec(memory_space=pl.ANY)

    def kernel(*refs):
        ends = 2 + len(nearby)
        back_kernel(dp_size, seq_size, pieces, orders, sequence, *refs[:ends],
                    refs[ends : ends + len(away)], *refs[ends + len(away) :])

    return pl.pallas_call(
        kernel,
        out_shape=(
            jax.ShapeDtypeStruct((total_rows, columns), BF),
            jax.ShapeDtypeStruct(small.shape, F32),
            jax.ShapeDtypeStruct((batch, length, width), BF),
            jax.ShapeDtypeStruct((batch, length, width), BF),
        ),
        in_specs=[anywhere, VM] + [anywhere] * 2 + [VM] * (len(nearby) - 2) + [anywhere] * len(away),
        out_specs=(anywhere, VM, VM, VM),
        scratch_shapes=scratch,
        name="backward_and_sums",
        compiler_params=pltpu.CompilerParams(collective_id=0, has_side_effects=True, vmem_limit_bytes=62 << 20),
    )(cross_out_grad, small, *nearby, *away)

SOURCE = 56


def row_mix(heads, tq, blocks, width, seen, q, aq, k, v, ak, put):
    state = {"aux": aq.astype(F32)}
    low = lanes((tq, 128)) < HALF

    def columns(h):
        return slice(h // 2 * 128, h // 2 * 128 + 128)

    def first(h):
        even = h % 2 == 0
        return dot_nt(pick(even, q(columns(h)) * jnp.asarray(SCORE_SCALE, BF), aq), pick(even, k(columns(h)), ak))

    def rest(h, scores):
        values = v(columns(h))
        if seen is not None:
            tail = jnp.where(seen, scores[:, (blocks - 1) * width :], -BIG)
            scores = tail if blocks == 1 else jnp.concatenate([scores[:, : (blocks - 1) * width], tail], axis=1)
        peak = jnp.max(scores, axis=1, keepdims=True)
        weights = jnp.exp(scores - peak).astype(BF)
        mixed = dot_nn(weights, pick(h % 2 == 0, values, jnp.ones_like(values)))
        at = HALF if h % 2 == 0 else 0
        state["aux"] = put_parts(state["aux"], peak + jnp.log(mixed[:, at : at + 1]), LSE + 3 * h)
        if h % 2 == 0:
            state["even"] = mixed
        else:
            total = pltpu.roll(jnp.where(low, mixed, state["even"]), HALF, 1)
            put(columns(h), jnp.where(low, state["even"], mixed) / total)

    schedule(heads, 1, first, rest)
    return state["aux"].astype(BF)


def norm_rows(residual, gain, shift):
    centred = residual - jnp.mean(residual, axis=-1, keepdims=True)
    inverse = lax.rsqrt(jnp.mean(centred * centred, axis=-1, keepdims=True) + EPSILON)
    unit = centred * inverse
    return unit * gain + shift, unit, inverse


def norm_rows_back(grad, unit, inverse, gain):
    scaled = grad * gain
    return inverse * (scaled - jnp.mean(scaled, axis=-1, keepdims=True) - unit * jnp.mean(scaled * unit, axis=-1, keepdims=True))


def front_kernel(dp_size, seq_size, self_mask, cross_mask, mask_local, gains, biases, hidden_bias, tokens, memory, cotangent, *refs):
    weights_away, refs = refs[:7], refs[7:]
    (output, small, *away_outs, root_out), refs = refs[:19], refs[19:]
    kept, refs = refs[:16], refs[16:]
    (ffn_grads, cross_out_grad, mask, queries, keys, values, cross_key, cross_value, cq_full, attended, self_aux, self_low, unit,
     grad_mid, grad_crossed, cross_aux) = kept
    (tokens_full, memory_full, self_qkv, self_out, cross_q, cross_kv, cross_out, ffn_in, ffn_out, cot, after_self, crossed, hidden,
     slope, row_send, row_recv, load_sem, save_sem) = refs
    here_weights = (self_qkv, self_out, cross_q, cross_kv, cross_out, ffn_in, ffn_out)
    dims = dimensions(dp_size, seq_size)
    place = lax.axis_index("seq")
    batch, length, width = attended.shape
    heads = width // HALF
    flat = batch * length
    base = pl.multiple_of(place * length, length)
    mine = pl.ds(base, length)

    y_size, y_me, y_device = dims["y"]
    _, core_me, core_device = dims["core"]
    barrier = pltpu.get_barrier_semaphore()
    targets = [y_device((y_me + step) % y_size) for step in range(1, y_size)] + [core_device(1 - core_me)]
    for device in targets:
        pl.semaphore_signal(barrier, inc=1, device_id=device, device_id_type=MESH)

    loads = []

    def load(away, here):
        copy = pltpu.make_async_copy(away, here, load_sem.at[len(loads)])
        copy.start()
        loads.append(copy)
        return len(loads) - 1

    load(tokens, tokens_full.at[:, mine])
    load(memory, memory_full.at[:, mine])
    for away, here in zip(weights_away, here_weights):
        load(away, here)
    load(cotangent, cot)
    mask[:, mine] = mask_local[...]
    pl.semaphore_wait(barrier, len(targets))

    def row_block(full, block):
        return full.at[:, pl.ds(pl.multiple_of(block * length, length), length)]

    started = {}

    def send(key, which, fulls, kind):
        copies = []
        for a, full in enumerate(fulls):
            if kind == "y":
                todo = [(place, y_device((y_me + step) % y_size), step - 1, y_size - step - 1) for step in range(1, y_size)]
            elif kind == "core":
                todo = [(place, core_device(1 - core_me), y_size - 1, y_size - 1)]
            else:
                todo = [((y_me - step + y_size) % y_size * 2 + core_me, core_device(1 - core_me), y_size - 1 + step, y_size - 1 + step)
                        for step in range(1, y_size)]
            for block, device, i, j in todo:
                copies.append(pltpu.make_async_remote_copy(
                    src_ref=row_block(full, block), dst_ref=row_block(full, block), send_sem=row_send.at[which, a, i],
                    recv_sem=row_recv.at[which, a, j], device_id=device, device_id_type=MESH))
        for copy in copies:
            copy.start()
        started[key] = copies

    def finish(key):
        for copy in started.pop(key):
            copy.wait()

    saves = []

    def save(*which):
        for i in which:
            copy = pltpu.make_async_copy(kept[i], away_outs[i], save_sem.at[i])
            copy.start()
            saves.append(copy)

    def total(value):
        return jnp.sum(value.astype(F32), axis=0, keepdims=True)

    def rowwise(ref):
        return ref[...].reshape(flat, ref.shape[2])

    small_rows = {}
    gain, shift = [gains[i : i + 1] for i in range(3)], [biases[i : i + 1] for i in range(3)]
    bias = lambda i: biases[i : i + 1]

    loads[0].wait()
    send("tokens y", 0, (tokens_full, mask), "y")
    send("tokens core", 0, (tokens_full, mask), "core")
    def project_block(block):
        at = pl.ds(pl.multiple_of(block * length, length), length)
        rows = tokens_full[:, at].reshape(flat, width)
        for i, (ref, extra) in enumerate(((queries, bias(3)), (keys, None), (values, bias(4)))):
            value = dot_nn(rows, self_qkv[:, i * width : (i + 1) * width])
            if extra is not None:
                value = value + extra
            ref[:, at] = value.astype(BF).reshape(batch, length, width)

    loads[2].wait()
    project_block(place)
    finish("tokens core")
    project_block(place + 1 - 2 * core_me)
    finish("tokens y")
    send("tokens relay", 0, (tokens_full, mask), "relay")
    loads[1].wait()
    send("memory y", 1, (memory_full,), "y")
    send("memory core", 1, (memory_full,), "core")
    for step in range(1, y_size):
        project_block((y_me - step + y_size) % y_size * 2 + core_me)
    finish("tokens relay")
    for step in range(1, y_size):
        project_block((y_me - step + y_size) % y_size * 2 + 1 - core_me)
    save(2, 3, 4, 5)

    down = lax.broadcasted_iota(jnp.int32, (length, length), 0)
    along = lax.broadcasted_iota(jnp.int32, (length, length), 1)
    for blocks in range(1, seq_size + 1):

        @pl.when(place == blocks - 1)
        def _(blocks=blocks):
            def row(r, carry):
                at, span = pl.ds((blocks - 1) * length, length), pl.ds(0, blocks * length)

                def put(cs, value):
                    attended[r, :, cs] = value.astype(BF)

                self_aux[r] = row_mix(heads, length, blocks, length, along <= down, lambda cs: queries[r, at, cs], self_mask[r],
                                      lambda cs: keys[r, span, cs], lambda cs: values[r, span, cs], mask[r, span], put)
                return carry

            lax.fori_loop(0, batch, row, 0)

    for i in (3, 4):
        loads[i].wait()
    state, unit_first, root_first = norm_rows(
        tokens_full[:, mine].reshape(flat, width).astype(F32) + dot_nn(rowwise(attended), self_out[...]) + bias(5), gain[0], shift[0]
    )
    after_self[...] = state
    unit[...] = unit_first.reshape(batch, length, width)
    root_out[...] = root_first.reshape(batch, length, 1)
    self_low[...] = state.astype(BF).reshape(batch, length, width)
    query = (dot_nn(state.astype(BF), cross_q[...]) + bias(6)).astype(BF)
    cq_full[:, mine] = query.reshape(batch, length, width)
    finish("memory core")
    finish("memory y")
    send("memory relay", 1, (memory_full,), "relay")
    send("query y", 2, (cq_full,), "y")
    send("query core", 2, (cq_full,), "core")
    save(9, 10, 11, 12)
    loads[5].wait()

    def project_memory(block):
        at = pl.ds(pl.multiple_of(block * length, length), length)
        rows = memory_full[:, at].reshape(flat, width)
        cross_key[:, at] = dot_nn(rows, cross_kv[:, :width]).astype(BF).reshape(batch, length, width)
        cross_value[:, at] = (dot_nn(rows, cross_kv[:, width:]) + bias(7)).astype(BF).reshape(batch, length, width)

    project_memory(place)
    project_memory(place + 1 - 2 * core_me)
    for step in range(1, y_size):
        project_memory((y_me - step + y_size) % y_size * 2 + core_me)
    finish("memory relay")
    for step in range(1, y_size):
        project_memory((y_me - step + y_size) % y_size * 2 + 1 - core_me)
    save(6, 7)

    def cross_row(r, carry):
        def put(cs, value):
            crossed[r, :, cs] = value.astype(BF)

        cross_aux[r] = row_mix(heads, length, seq_size, length, None, lambda cs: cq_full[r, mine, cs], cross_mask[r],
                               lambda cs: cross_key[r, :, cs], lambda cs: cross_value[r, :, cs], mask[r], put)
        return carry

    lax.fori_loop(0, batch, cross_row, 0)
    for i in range(6, 10):
        loads[i].wait()
    after_cross, unit_second, root_second = norm_rows(after_self[...] + dot_nn(rowwise(crossed), cross_out[...]) + bias(8), gain[1],
                                                      shift[1])
    finish("query core")
    finish("query y")
    send("query relay", 2, (cq_full,), "relay")
    cross_low = after_cross.astype(BF)
    parts = ffn_in.shape[1] // width
    summed = after_cross + bias(9)
    for j in range(parts):
        cs = slice(j * width, (j + 1) * width)
        before = dot_nn(cross_low, ffn_in[:, cs]) + hidden_bias[:, cs]
        share = 0.5 * (1.0 + lax.erf(before * ROOT_HALF))
        slope[:, cs] = share + before * NORMAL_DENSITY * jnp.exp(-0.5 * before * before)
        value = (before * share).astype(BF)
        hidden[:, cs] = value
        summed = summed + dot_nn(value, ffn_out[cs])
    result, unit_third, root_third = norm_rows(summed, gain[2], shift[2])
    output[...] = result.astype(BF).reshape(batch, length, width)
    grad = rowwise(cot).astype(F32)
    small_rows[2], small_rows[5] = total(grad * unit_third), total(grad)
    grad_third = norm_rows_back(grad, unit_third, root_third, gain[2])
    branch = grad_third.astype(BF)
    small_rows[12] = total(branch)
    grad_second = grad_third
    for j in range(parts):
        cs = slice(j * width, (j + 1) * width)
        ffn_grads[pl.ds((parts + j) * width, width)] = dot_tn(hidden[:, cs], branch).astype(BF)
        grad_hidden = (dot_nt(branch, ffn_out[cs]) * slope[:, cs]).astype(BF)
        small_rows[13 + j] = total(grad_hidden)
        ffn_grads[pl.ds(j * width, width)] = dot_tn(cross_low, grad_hidden).astype(BF)
        grad_second = grad_second + dot_nt(grad_hidden, ffn_in[:, cs])
    save(0)
    finish("query relay")
    save(8)
    small_rows[1], small_rows[4] = total(grad_second * unit_second), total(grad_second)
    middle = norm_rows_back(grad_second, unit_second, root_second, gain[1])
    grad_mid[...] = middle.reshape(batch, length, width)
    branch = middle.astype(BF)
    small_rows[11] = total(branch)
    mixed = rowwise(crossed)
    grad_mixed = dot_nt(branch, cross_out[...]).astype(BF)
    grad_crossed[...] = grad_mixed.reshape(batch, length, width)
    aux = rowwise(cross_aux).astype(F32) + head_inner(grad_mixed, mixed)
    cross_aux[...] = aux.astype(BF).reshape(batch, length, 128)
    cross_out_grad[...] = dot_tn(mixed, branch).astype(BF)
    save(1, 13, 14, 15)
    small[...] = jnp.zeros(small.shape, F32)
    for row, value in small_rows.items():
        small[row : row + 1] = value
    for copy in saves:
        copy.wait()


def front(mesh_shape, self_mask, cross_mask, mask_local, gains, biases, hidden_bias, tokens, memory, cotangent, weights):
    dp_size, seq_size = mesh_shape["dp"], mesh_shape["seq"]
    batch, length, width = tokens.shape
    hidden = weights[5].shape[1]
    flat, full = batch * length, seq_size * length
    anywhere = pl.BlockSpec(memory_space=pl.ANY)
    whole, part, narrow = (batch, full, width), (batch, length, width), (batch, length, 128)
    saved = [((2 * hidden, width), BF), ((width, width), BF), ((batch, full, 128), BF)] + [(whole, BF)] * 6
    saved += [(part, BF), (narrow, BF), (part, BF), (part, F32), (part, F32), (part, BF), (narrow, BF)]
    out_shape = [(part, BF), ((24, width), F32)] + saved + [((batch, length, 1), F32)]
    scratch = [pltpu.VMEM(shape, kind) for shape, kind in saved]
    scratch += [pltpu.VMEM(whole, BF)] * 2 + [pltpu.VMEM(value.shape, BF) for value in weights]
    scratch += [
        pltpu.VMEM(part, BF),
        pltpu.VMEM((flat, width), F32),
        pltpu.VMEM(part, BF),
        pltpu.VMEM((flat, hidden), BF),
        pltpu.VMEM((flat, hidden), F32),
        pltpu.SemaphoreType.DMA((3, 2, seq_size)),
        pltpu.SemaphoreType.DMA((3, 2, seq_size)),
        pltpu.SemaphoreType.DMA((10,)),
        pltpu.SemaphoreType.DMA((len(saved),)),
    ]
    return pl.pallas_call(
        functools.partial(front_kernel, dp_size, seq_size),
        out_shape=tuple(jax.ShapeDtypeStruct(shape, kind) for shape, kind in out_shape),
        in_specs=[VM] * 6 + [anywhere] * 10,
        out_specs=(VM, VM) + (anywhere,) * len(saved) + (VM,),
        scratch_shapes=scratch,
        name="forward_and_feed_forward",
        compiler_params=pltpu.CompilerParams(collective_id=1, has_side_effects=True, vmem_limit_bytes=62 << 20),
    )(self_mask, cross_mask, mask_local, gains, biases, hidden_bias, tokens, memory, cotangent, *weights)


def unpack_kernel(summed, small, *refs):
    passed, outs = refs[:3], refs[3:16]
    taken, given, held, load_sem, save_sem, pass_sem = refs[16:]
    width = summed.shape[1]
    arriving = [pltpu.make_async_copy(a, held.at[i], pass_sem.at[0, i]) for i, a in enumerate(passed)]
    through = [pltpu.make_async_copy(held.at[i], b, pass_sem.at[1, i]) for i, b in enumerate(outs[:3])]
    qkv, self_out, cross_q, cross_kv, cross_out, ffn_in, ffn_out, gains, biases, hidden = outs[3:]
    columns = lambda ref, i: ref.at[:, pl.ds(i * width, width)]
    places = [columns(ffn_in, i) for i in range(4)] + [ffn_out.at[pl.ds(i * width, width)] for i in range(4)]
    places += [cross_out, cross_q, self_out] + [columns(cross_kv, i) for i in range(2)] + [columns(qkv, i) for i in range(3)]
    loads = []
    for i in range(len(places)):
        loads.append(pltpu.make_async_copy(summed.at[pl.ds(i * width, width)], taken.at[i], load_sem.at[i]))
    for copy in loads:
        copy.start()
    saves = []
    for i, place in enumerate(places):
        loads[i].wait()
        given[i] = taken[i].astype(F32)
        saves.append(pltpu.make_async_copy(given.at[i], place, save_sem.at[i]))
        saves[-1].start()
        if i == 1:
            for copy in arriving:
                copy.start()
        if i == 6:
            for copy, onward in zip(arriving, through):
                copy.wait()
                onward.start()
    gains[...] = small[0:3]
    biases[...] = small[3:13]
    for i in range(4):
        hidden[pl.ds(i * width, width)] = small[13 + i]
    for copy in saves + through:
        copy.wait()


def unpack(summed, small, passed):
    width = summed.shape[1]
    blocks = summed.shape[0] // width
    square = (width, width)
    shapes = [(width, 3 * width), square, square, (width, 2 * width), square, (width, 4 * width), (4 * width, width)]
    anywhere = pl.BlockSpec(memory_space=pl.ANY)
    return pl.pallas_call(
        unpack_kernel,
        out_shape=tuple(jax.ShapeDtypeStruct(value.shape, value.dtype) for value in passed)
        + tuple(jax.ShapeDtypeStruct(shape, F32) for shape in shapes + [(3, width), (10, width), (4 * width,)]),
        in_specs=[anywhere, VM] + [anywhere] * 3,
        out_specs=(anywhere,) * 10 + (VM,) * 3,
        scratch_shapes=[
            pltpu.VMEM((blocks,) + square, BF),
            pltpu.VMEM((blocks,) + square, F32),
            pltpu.VMEM((3,) + passed[0].shape, BF),
            pltpu.SemaphoreType.DMA((blocks,)),
            pltpu.SemaphoreType.DMA((blocks,)),
            pltpu.SemaphoreType.DMA((2, 3)),
        ],
        name="unpack_sums",
        compiler_params=pltpu.CompilerParams(vmem_limit_bytes=62 << 20),
    )(summed, small, *passed)


def shards(mesh_shape, tokens, memory, segment_ids, source_ids, source_lengths, cotangent, self_qkv, self_out, cross_q, cross_kv,
           cross_out, ffn_in, ffn_out, norm_gains, bias_rows, hidden_bias):
    length = tokens.shape[1]
    place = lax.axis_index("seq") * length + jnp.arange(length, dtype=jnp.int32)
    lane = jnp.arange(128) % HALF
    usable = (place[None] < source_lengths[:, None])[..., None]
    segments, sources = segment_ids[..., None], source_ids[..., None]
    self_mask = jnp.where(segments == lane, 1.0, 0.0).astype(BF)
    cross_mask = jnp.where(segments == lane - SOURCE, 1.0, 0.0).astype(BF)
    other = jnp.where(lane < 8, segments != lane, (lane >= SOURCE) & ~((sources == lane - SOURCE) & usable))
    mask = jnp.where(other, -BIG, 0.0).astype(BF)
    (output, small, ffn_grads, cross_out_grad, mask_full, queries, keys, values, cross_key, cross_value, cross_query, attended, self_aux,
     self_low, unit, grad_mid, grad_crossed, cross_aux, root) = front(
        mesh_shape, self_mask, cross_mask, mask, norm_gains, bias_rows, hidden_bias.reshape(1, -1), tokens, memory, cotangent,
        (self_qkv, self_out, cross_q, cross_kv, cross_out, ffn_in, ffn_out),
    )
    summed, small, grad_tokens, grad_memory = back_and_sum(
        mesh_shape, HEADS,
        (
            cross_out_grad, small,
            (grad_crossed, cross_aux, self_aux, root, norm_gains),
            (ffn_grads, cross_key, cross_value, mask_full, self_low, unit, grad_mid, cross_q, self_out, attended, memory,
             cross_kv, cross_query, queries, keys, values, tokens, self_qkv),
        ),
    )

    return unpack(summed, small, (output, grad_tokens, grad_memory))


def solution(mesh):
    placed = (
        P("dp", "seq", None),
        P("dp", "seq", None),
        P("dp", "seq"),
        P("dp", "seq"),
        P("dp"),
        P("dp", "seq", None),
        P(),
        P(),
        P(),
        P(),
        P(),
        P(),
        P(),
        P(),
        P(),
        P(),
    )
    return jax.shard_map(
        functools.partial(shards, dict(mesh.shape)),
        mesh=mesh,
        in_specs=placed,
        out_specs=(
            P("dp", "seq", None),
            P("dp", "seq", None),
            P("dp", "seq", None),
            P(),
            P(),
            P(),
            P(),
            P(),
            P(),
            P(),
            P(),
            P(),
            P(),
        ),
        check_vma=False,
    )
```
